32 devices in a mesh: fsdp: 4 (over y, core), ctx: 4 (over z), tp: 2 (over x).
Axes of the slice: x: 2, y: 2, z: 4, core: 2. Of those that a mesh axis runs over, the one named last changes fastest.
Arguments:
- latents: bfloat16 [3, 4, 1024, 1152], P(None, 'fsdp', 'ctx'), may hold values from -6 to 6
- condition: bfloat16 [3, 4, 1152], P(None, 'fsdp'), may hold values from -6 to 6
- grad_out: bfloat16 [3, 4, 1024, 1152], P(None, 'fsdp', 'ctx'), may hold values from -6 to 6
- ada_weight: bfloat16 [1152, 6, 1152], P(('fsdp', 'ctx'), None, 'tp'), may hold values from -0.375 to 0.375
- ada_bias: bfloat16 [6, 1152], replicated, may hold values from -3 to 3
- qkv_weight: bfloat16 [1152, 3, 1152], P(('fsdp', 'ctx'), None, 'tp'), may hold values from -0.09375 to 0.09375
- qv_bias: bfloat16 [2, 1152], replicated, may hold values from -3 to 3
- proj_weight: bfloat16 [1152, 1152], P('tp', ('fsdp', 'ctx')), may hold values from -3 to 3
- proj_bias: bfloat16 [1152], replicated, may hold values from -3 to 3
- up_weight: bfloat16 [1152, 4608], P(('fsdp', 'ctx'), 'tp'), may hold values from -0.1875 to 0.1875
- up_bias: bfloat16 [4608], replicated, may hold values from -3 to 3
- down_weight: bfloat16 [4608, 1152], P('tp', ('fsdp', 'ctx')), may hold values from -0.09375 to 0.09375
- down_bias: bfloat16 [1152], replicated, may hold values from -3 to 3
Outputs:
- output: bfloat16 [3, 4, 1024, 1152], P(None, 'fsdp', 'ctx')
- grad_latents: float32 [3, 4, 1024, 1152], P(None, 'fsdp', 'ctx')
- grad_condition: float32 [3, 4, 1152], P(None, 'fsdp')
- grad_ada_weight: float32 [1152, 6, 1152], P(('fsdp', 'ctx'), None, 'tp')
- grad_ada_bias: float32 [6, 1152], replicated
- grad_qkv_weight: float32 [1152, 3, 1152], P(('fsdp', 'ctx'), None, 'tp')
- grad_qv_bias: float32 [2, 1152], replicated
- grad_proj_weight: float32 [1152, 1152], P('tp', ('fsdp', 'ctx'))
- grad_proj_bias: float32 [1152], replicated
- grad_up_weight: float32 [1152, 4608], P(('fsdp', 'ctx'), 'tp')
- grad_up_bias: float32 [4608], replicated
- grad_down_weight: float32 [4608, 1152], P('tp', ('fsdp', 'ctx'))
- grad_down_bias: float32 [1152], replicated
The draws below stay inside these ranges and needn't reach their ends.
All inputs are finite; a program needn't handle non-finite values.
Results may differ from the reference program's by a relative error of at most 0.01.
The reference program's roundings to bfloat16 on the way count: a program that leaves them out, or rounds other values in their place, can miss the bound.
Values may be sent and summed in bfloat16 or wider, within the bound.
No kernel may reach another device: no remote copies, remote signals or barrier semaphores. Data moves between devices by JAX's collectives and lax.ppermute only.
A program may use at most 256 MiB of HBM per device.

```python
import jax
import jax.numpy as jnp
from jax import lax

D = 1152
HEADS = 16
HEAD_DIM = 72
FF = 4608
SEQ = 1024
MICRO = 3
BATCH = 4


def level_of(key, extent, cuts, smallest, largest):
    factor_of, own = 1.0, jax.random.fold_in(key, 6)
    for axis_at, parts in cuts:
        heights = jnp.exp(jax.random.uniform(jax.random.fold_in(own, axis_at), (parts,), jnp.float32, smallest / len(cuts), largest / len(cuts)))
        factor_of = factor_of * jnp.repeat(heights, extent[axis_at] // parts).reshape([-1 if axis == axis_at else 1 for axis in range(len(extent))])
    return factor_of


def noise(key, shape, deviation, reach, cuts=(), dtype=jnp.bfloat16):
    loudness = level_of(key, shape, cuts, -0.22, 0.18) if cuts else 1.0
    values = jax.random.normal(key, shape, jnp.float32) * deviation * loudness
    return jnp.minimum(jnp.maximum(values, -reach), reach).astype(dtype)


def setup_inputs(seed: int = 0) -> dict:
    streams_of = jax.random.split(jax.random.key(seed), 14)
    latents = noise(streams_of[0], (MICRO, BATCH, SEQ, D), 1.0, 6.0, ((1, 4), (2, 4)))
    condition = noise(streams_of[1], (MICRO, BATCH, D), 1.0, 6.0, ((1, 4),))
    grad_out = noise(streams_of[2], (MICRO, BATCH, SEQ, D), 1.0, 6.0, ((1, 4), (2, 4)))
    ada_weight = noise(streams_of[3], (D, 6, D), (D // 4) ** -0.5, 0.375, ((0, 16), (2, 2)))
    ada_bias = noise(streams_of[4], (6, D), 0.5, 3.0)
    qkv_weight = noise(streams_of[5], (D, 3, D), (4 * D) ** -0.5, 0.09375, ((0, 16), (2, 2)))
    qv_bias = noise(streams_of[6], (2, D), 0.5, 3.0)
    proj_weight = noise(streams_of[7], (D, D), (max(4 * D // SEQ, 1)) ** -0.5, 3.0, ((0, 2), (1, 16)))
    proj_bias = noise(streams_of[8], (D,), 0.5, 3.0)
    up_weight = noise(streams_of[9], (D, FF), D ** -0.5, 0.1875, ((0, 16), (1, 2)))
    up_bias = noise(streams_of[10], (FF,), 0.5, 3.0)
    down_weight = noise(streams_of[11], (FF, D), FF ** -0.5, 0.09375, ((0, 2), (1, 16)))
    down_bias = noise(streams_of[12], (D,), 0.5, 3.0)
    return dict(latents=latents, condition=condition, grad_out=grad_out, ada_weight=ada_weight, ada_bias=ada_bias, qkv_weight=qkv_weight, qv_bias=qv_bias, proj_weight=proj_weight, proj_bias=proj_bias, up_weight=up_weight, up_bias=up_bias, down_weight=down_weight, down_bias=down_bias)


@jax.custom_vjp
def low(v):
    return lax.optimization_barrier(v.astype(jnp.bfloat16)).astype(jnp.float32)

@jax.custom_vjp
def low_back(v):
    return v

def low_keep(v):
    return (low(v), None)

def low_pass(kept, grad):
    return (grad,)

def back_keep(v):
    return (v, None)

def back_low(kept, grad):
    return (low(grad),)
low.defvjp(low_keep, low_pass)
low_back.defvjp(back_keep, back_low)

def normalize(values):
    centre = values - lax.optimization_barrier(jnp.mean(values, -1, keepdims=True))
    return centre * lax.rsqrt(lax.optimization_barrier(jnp.mean(centre * centre, -1, keepdims=True)) + 1e-06)

def block(params, latent, cond_value):
    ada_weight, ada_bias, qkv_weight, qv_bias, proj_weight, proj_bias, up_weight, up_bias, down_weight, down_bias = params
    highest = lax.Precision.HIGHEST
    silu_cond = low(jax.nn.silu(cond_value))
    modulation = low(low_back(jnp.einsum('d,dke->ke', silu_cond, ada_weight, precision=highest) + ada_bias))
    in_first = low(normalize(latent) * (1.0 + modulation[1]) + modulation[0])
    projected = jnp.einsum('td,dke->tke', in_first, qkv_weight, precision=highest)
    queries = low(low_back(projected[:, 0] + qv_bias[0]))
    key_rows = low(low_back(projected[:, 1]))
    value_rows = low(low_back(projected[:, 2] + qv_bias[1]))
    query_heads = queries.reshape(SEQ, HEADS, HEAD_DIM)
    key_heads = key_rows.reshape(SEQ, HEADS, HEAD_DIM)
    value_heads = value_rows.reshape(SEQ, HEADS, HEAD_DIM)
    scores = low_back(jnp.einsum('qhe,khe->hqk', query_heads, key_heads, precision=highest) * HEAD_DIM ** (-0.5))
    chances = jax.nn.softmax(scores, axis=-1)
    blended = jnp.einsum('hqk,khe->qhe', low(chances), value_heads, precision=highest).reshape(SEQ, D)
    blended = low(low_back(blended))
    attended = low_back(jnp.dot(blended, proj_weight, precision=highest) + proj_bias)
    residual = latent + modulation[2] * attended
    in_second = low(normalize(residual) * (1.0 + modulation[4]) + modulation[3])
    upward = low_back(jnp.dot(in_second, up_weight, precision=highest) + up_bias)
    activated = low(jax.nn.gelu(upward, approximate=True))
    feed_out = low_back(jnp.dot(activated, down_weight, precision=highest) + down_bias)
    return residual + modulation[5] * feed_out

def reference(latents, condition, grad_out, ada_weight, ada_bias, qkv_weight, qv_bias, proj_weight, proj_bias, up_weight, up_bias, down_weight, down_bias):
    params = tuple((weight_piece.astype(jnp.float32) for weight_piece in (ada_weight, ada_bias, qkv_weight, qv_bias, proj_weight, proj_bias, up_weight, up_bias, down_weight, down_bias)))
    flat_latents = latents.astype(jnp.float32).reshape(-1, SEQ, D)
    flat_cond = condition.astype(jnp.float32).reshape(-1, D)
    flat_grad = grad_out.astype(jnp.float32).reshape(-1, SEQ, D)

    def advance(running, sequence_item):
        latent, cond_value, cotangent = sequence_item
        result, pullback = jax.vjp(block, params, latent, cond_value)
        grad_params, grad_latent, grad_cond = pullback(cotangent)
        running = jax.tree.map(jnp.add, running, grad_params)
        return (running, (result.astype(jnp.bfloat16), grad_latent, grad_cond))
    start = jax.tree.map(jnp.zeros_like, params)
    summed, (results, latent_grads, cond_grads) = lax.scan(advance, start, (flat_latents, flat_cond, flat_grad))
    return (results.reshape(latents.shape), latent_grads.reshape(latents.shape), cond_grads.reshape(condition.shape), summed[0], summed[1], summed[2], summed[3], summed[4], summed[5], summed[6], summed[7], summed[8], summed[9])
```

```python
from functools import partial

import jax
import jax.numpy as jnp
from jax import lax
from jax.experimental import pallas as pl
from jax.experimental.pallas import tpu as pltpu
from jax.sharding import PartitionSpec as P

HEADS = 16
HEAD_DIM = 72
LOG2E = 1.4426950408889634
F32 = jnp.float32
BF16 = jnp.bfloat16


def dot(a, b, dims):
    return lax.dot_general(a, b, (dims, ((), ())), preferred_element_type=F32)


def normalize(values):
    centre = values - jnp.mean(values, -1, keepdims=True)
    inverse = lax.rsqrt(jnp.mean(centre * centre, -1, keepdims=True) + 1e-06)
    return (centre * inverse, inverse)


def norm_back(incoming, normed, inverse):
    return inverse * (
        incoming
        - jnp.mean(incoming, -1, keepdims=True)
        - normed * jnp.mean(incoming * normed, -1, keepdims=True)
    )


def shift(x, k):
    size = lax.axis_size("ctx")
    return lax.ppermute(x, "ctx", [(i, (i + k) % size) for i in range(size)])


def flip(x, axis, bit):
    size = lax.axis_size(axis)
    return lax.ppermute(x, axis, [(i, i ^ (1 << bit)) for i in range(size)])


def bits_of(axis):
    return lax.axis_size(axis).bit_length() - 1


def ring_gather(x):
    size = lax.axis_size("ctx")
    blocks = [x] * size
    moving = x
    for step in range(1, size // 2 + 1):
        moving = shift(moving, 1)
        blocks[step] = moving
    moving = x
    for step in range(1, (size - 1) // 2 + 1):
        moving = shift(moving, -1)
        blocks[size - step] = moving
    return blocks


def butterfly_sum(x, axis):
    for bit in range(bits_of(axis)):
        x = x + flip(x, axis, bit)
    return x


def cube_gather(x):
    x = x[None]
    for bit in range(bits_of("fsdp")):
        x = jnp.concatenate([x, flip(x, "fsdp", bit)], 0)
    return x


def cube_reduce(x):
    for bit in reversed(range(bits_of("fsdp"))):
        half = x.shape[0] // 2
        x = x[:half] + flip(x[half:], "fsdp", bit)
    return x[0]


def pick(entries, which):
    return lax.select_n(which, *entries) if len(entries) > 2 else jnp.where(which == 0, *entries)


def absolute(entries, rank, sign):
    size = len(entries)
    return jnp.stack([pick(entries, (sign * (place - rank)) % size) for place in range(size)])


def gather_pieces(shard):
    blocks = ring_gather(shard)
    size = len(blocks)
    if size * lax.axis_size("fsdp") > 16:
        pieces = [(0, tuple(range(size)), jnp.stack(blocks))]
    else:
        pieces = [(0, (k,), block[None]) for k, block in enumerate(blocks)]
    for bit in reversed(range(bits_of("fsdp"))):
        pieces = pieces + [
            (offset ^ (1 << bit), places, flip(block, "fsdp", bit))
            for offset, places, block in pieces
        ]
    return pieces


def place_kernel(targets, widths, *refs):
    count = len(targets)
    ins, outs = refs[:count], refs[count : count + len(widths)]
    held, in_sem, out_sem = refs[count + len(widths) :]
    own_f = lax.axis_index("fsdp")
    own_c = lax.axis_index("ctx")
    size_c = lax.axis_size("ctx")
    arriving, leaving = [], []
    for (offset, places), ref in zip(targets, ins):
        row = jnp.bitwise_xor(own_f, offset)
        for at, spot in enumerate(places):
            column = lax.rem(own_c + size_c - spot, size_c)
            slot = len(arriving)
            arriving.append(pltpu.make_async_copy(ref.at[at], held.at[slot], in_sem.at[slot]))
            first = 0
            for width, out in zip(widths, outs):
                leaving.append(
                    pltpu.make_async_copy(
                        held.at[slot, :, pl.ds(first, width)],
                        out.at[row, column],
                        out_sem.at[len(leaving)],
                    )
                )
                first += width
    for copy in arriving:
        copy.start()
    each = len(widths)
    for slot, copy in enumerate(arriving):
        copy.wait()
        for out_copy in leaving[slot * each : (slot + 1) * each]:
            out_copy.start()
    for copy in leaving:
        copy.wait()


def place(pieces, widths):
    size_f, size_c = lax.axis_size("fsdp"), lax.axis_size("ctx")
    rows, total = pieces[0][2].shape[1:]
    count = size_f * size_c
    outs = pl.pallas_call(
        partial(place_kernel, [piece[:2] for piece in pieces], widths),
        out_shape=[jax.ShapeDtypeStruct((size_f, size_c, rows, width), BF16) for width in widths],
        in_specs=[pl.BlockSpec(memory_space=pl.ANY)] * len(pieces),
        out_specs=[pl.BlockSpec(memory_space=pl.ANY)] * len(widths),
        scratch_shapes=[
            pltpu.VMEM((count, rows, total), BF16),
            pltpu.SemaphoreType.DMA((count,)),
            pltpu.SemaphoreType.DMA((count * len(widths),)),
        ],
        compiler_params=pltpu.CompilerParams(vmem_limit_bytes=40 << 20),
        cost_estimate=pl.CostEstimate(
            flops=0, bytes_accessed=4 * count * rows * total, transcendentals=0
        ),
    )(*[piece[2] for piece in pieces])
    return [out.reshape(-1, width) for out, width in zip(outs, widths)]


def reduce_rows(features, others, dims):
    size_f, size_c = lax.axis_size("fsdp"), lax.axis_size("ctx")
    own_f = lax.axis_index("fsdp")
    width = features.shape[-1] // size_f
    split = features.reshape(*features.shape[:-1], size_f // 2, 2, width)
    low = own_f % 2
    evens = split[..., 0, :].reshape(*features.shape[:-1], -1)
    odds = split[..., 1, :].reshape(*features.shape[:-1], -1)
    mine = jnp.where(low == 0, evens, odds)
    theirs = jnp.where(low == 0, odds, evens)
    there = flip(dot(theirs, others, dims), "fsdp", 0)
    total = dot(mine, others, dims) + there
    columns = total.shape[-1]
    for bit in range(1, bits_of("fsdp")):
        own_bit = (own_f >> bit) % 2
        pairs = total.reshape(-1, 2, width, columns)
        send = lax.dynamic_index_in_dim(pairs, 1 - own_bit, 1, False)
        keep = lax.dynamic_index_in_dim(pairs, own_bit, 1, False)
        total = keep + flip(send.astype(BF16), "fsdp", bit).astype(F32)
    return total.reshape(size_c, width // size_c, columns)


def ring_reduce(blocks):
    size = lax.axis_size("ctx")
    own = lax.axis_index("ctx")

    def block(offset):
        return lax.dynamic_index_in_dim(blocks, (own + offset) % size, 0, False)

    total = block(0)
    for sign, reach in ((1, size // 2), (-1, (size - 1) // 2)):
        moving = None
        for distance in range(reach, 0, -1):
            term = block(sign * distance)
            if moving is not None:
                term = term + moving
            moving = shift(term.astype(BF16), sign).astype(F32)
        if moving is not None:
            total = total + moving
    return total


def head_rows(ref, head):
    values = ref[...].astype(F32)
    row = lax.broadcasted_iota(jnp.int32, values.shape, 0)
    inside = (row >= head * HEAD_DIM) & (row < (head + 1) * HEAD_DIM)
    return jnp.where(inside, values, 0.0).astype(BF16), inside


def attend_kernel(heads, q_ref, k_ref, vt_ref, out_ref, log_ref):
    factor = HEAD_DIM ** (-0.5) * LOG2E
    total = None
    for head in range(heads):
        q_head, inside = head_rows(q_ref, head)
        scores = dot(k_ref[...], q_head, ((1,), (0,)))
        highest = jnp.max(scores, 0, keepdims=True)
        exponent = jnp.exp2((scores - highest) * factor)
        summed = jnp.sum(exponent, 0, keepdims=True)
        chances = (exponent * (1.0 / summed)).astype(BF16)
        mixed = dot(vt_ref[...], chances, ((1,), (0,)))
        total = mixed if total is None else jnp.where(inside, mixed, total)
        log_ref[pl.ds(head, 1), :] = highest * factor + jnp.log2(summed)
    out_ref[...] = total.astype(BF16)


def attend(qkv_t, keys, block):
    width = keys.shape[1]
    tokens = keys.shape[0]
    heads = width // HEAD_DIM
    return pl.pallas_call(
        partial(attend_kernel, heads),
        grid=(tokens // block,),
        in_specs=[
            pl.BlockSpec((None, width, block), lambda i: (0, 0, i)),
            pl.BlockSpec((tokens, width), lambda i: (0, 0)),
            pl.BlockSpec((None, width, tokens), lambda i: (2, 0, 0)),
        ],
        out_specs=[
            pl.BlockSpec((width, block), lambda i: (0, i)),
            pl.BlockSpec((heads, block), lambda i: (0, i)),
        ],
        out_shape=[
            jax.ShapeDtypeStruct((width, tokens), BF16),
            jax.ShapeDtypeStruct((heads, tokens), F32),
        ],
        compiler_params=pltpu.CompilerParams(vmem_limit_bytes=40 << 20),
        cost_estimate=pl.CostEstimate(
            flops=heads * tokens * tokens * 1600,
            bytes_accessed=8 * width * tokens,
            transcendentals=heads * tokens * tokens,
        ),
    )(qkv_t, keys, qkv_t)


def attend_back_kernel(
    heads, q_ref, k_ref, kt_ref, v_ref, do_ref, log_ref, out_ref, dk_ref, dv_ref
):
    step = pl.program_id(0)
    scaling = HEAD_DIM ** (-0.5)
    block = q_ref.shape[1]

    @pl.when(step == 0)
    def _():
        dk_ref[...] = jnp.zeros_like(dk_ref)
        dv_ref[...] = jnp.zeros_like(dv_ref)

    grad_query = None
    for head in range(heads):
        q_head, inside = head_rows(q_ref, head)
        do_head, _ = head_rows(do_ref, head)
        scores = dot(k_ref[...], q_head, ((1,), (0,)))
        chances = jnp.exp2(scores * (scaling * LOG2E) - log_ref[pl.ds(head, 1), :])
        grad_chances = dot(v_ref[...], do_head, ((1,), (0,)))
        weighted = jnp.sum(chances * grad_chances, 0, keepdims=True)
        grad_scores = (chances * (grad_chances - weighted)).astype(BF16)
        term = dot(kt_ref[...], grad_scores, ((1,), (0,)))
        grad_query = term if grad_query is None else jnp.where(inside, term, grad_query)
        dk_ref[...] += dot(q_head, grad_scores, ((1,), (1,)))
        dv_ref[...] += dot(do_head, chances.astype(BF16), ((1,), (1,)))
    columns = pl.ds(pl.multiple_of(step * block, block), block)
    out_ref[0, :, columns] = (grad_query * scaling).astype(BF16)

    @pl.when(step == pl.num_programs(0) - 1)
    def _():
        out_ref[1] = (dk_ref[...] * scaling).astype(BF16)
        out_ref[2] = dv_ref[...].astype(BF16)


def attend_back(qkv_t, keys, values, grad_t, logs, block):
    width = keys.shape[1]
    tokens = keys.shape[0]
    heads = width // HEAD_DIM
    return pl.pallas_call(
        partial(attend_back_kernel, heads),
        grid=(tokens // block,),
        in_specs=[
            pl.BlockSpec((None, width, block), lambda i: (0, 0, i)),
            pl.BlockSpec((tokens, width), lambda i: (0, 0)),
            pl.BlockSpec((None, width, tokens), lambda i: (1, 0, 0)),
            pl.BlockSpec((tokens, width), lambda i: (0, 0)),
            pl.BlockSpec((width, block), lambda i: (0, i)),
            pl.BlockSpec((heads, block), lambda i: (0, i)),
        ],
        out_specs=pl.BlockSpec((3, width, tokens), lambda i: (0, 0, 0)),
        out_shape=jax.ShapeDtypeStruct((3, width, tokens), BF16),
        scratch_shapes=[pltpu.VMEM((width, tokens), F32), pltpu.VMEM((width, tokens), F32)],
        compiler_params=pltpu.CompilerParams(vmem_limit_bytes=40 << 20),
        cost_estimate=pl.CostEstimate(
            flops=heads * tokens * tokens * 4000,
            bytes_accessed=16 * width * tokens,
            transcendentals=heads * tokens * tokens,
        ),
    )(qkv_t, keys, qkv_t, values, grad_t, logs)


def body(
    latents,
    condition,
    grad_out,
    ada_weight,
    ada_bias,
    qkv_weight,
    qv_bias,
    proj_weight,
    proj_bias,
    up_weight,
    up_bias,
    down_weight,
    down_bias,
):
    t = lax.axis_index("tp")
    c = lax.axis_index("ctx")
    f = lax.axis_index("fsdp")
    size_c = lax.axis_size("ctx")
    size_f = lax.axis_size("fsdp")
    micro, batch, here, model = latents.shape
    items = micro * batch
    half = here // 2
    half_width = qkv_weight.shape[2]
    group = half_width // size_c
    hidden = up_weight.shape[1]
    rows = qkv_weight.shape[0]
    first_column = t * half_width

    def swap(x):
        return flip(x, "tp", 0)

    def both(own, peer, axis):
        return jnp.where(
            t == 0,
            jnp.concatenate([own, peer], axis),
            jnp.concatenate([peer, own], axis),
        )

    def own_first(x):
        ahead, behind = x[:, :half], x[:, half:]
        return jnp.concatenate(
            [jnp.where(t == 0, ahead, behind), jnp.where(t == 0, behind, ahead)], 1
        )

    latent = own_first(latents.reshape(items, here, model))
    cotangent = own_first(grad_out.reshape(items, here, model))
    cond = condition.reshape(items, model).astype(F32)

    silu_all = cube_gather(jax.nn.silu(cond).astype(BF16))
    first_row = (f * size_c + c) * rows
    silu_here = lax.dynamic_slice_in_dim(silu_all, first_row, rows, 2).reshape(-1, rows)
    mod_part = dot(silu_here, ada_weight.reshape(rows, -1), ((1,), (0,)))
    mod_part = butterfly_sum(cube_reduce(mod_part.reshape(size_f, items, -1)), "ctx")
    bias_mod = lax.dynamic_slice_in_dim(ada_bias.astype(F32), first_column, half_width, 1)
    mod_half = (mod_part.reshape(items, 6, half_width) + bias_mod).astype(BF16)
    modulation = both(mod_half, swap(mod_half), 2).astype(F32)
    shift_one, scale_one, gate_one, shift_two, scale_two, gate_two = (
        modulation[:, k : k + 1] for k in range(6)
    )

    qkv_groups = (
        qkv_weight.reshape(rows, 3, size_c, group)
        .transpose(2, 0, 1, 3)
        .reshape(size_c, rows, 3 * group)
    )
    blocks = [
        shift(lax.dynamic_index_in_dim(qkv_groups, (c + k) % size_c, 0, False), k) if k
        else lax.dynamic_index_in_dim(qkv_groups, c, 0, False)
        for k in range(size_c)
    ]
    pieces = [(0, tuple(range(size_c)), jnp.stack(blocks))]
    for bit in reversed(range(bits_of("fsdp"))):
        pieces = pieces + [
            (offset ^ (1 << bit), places, flip(block, "fsdp", bit))
            for offset, places, block in pieces
        ]
    (qkv_mine,) = place(pieces, [3 * group])
    bias_pair = lax.dynamic_slice_in_dim(
        qv_bias.astype(F32), first_column + c * group, group, 1
    )
    bias_mine = jnp.concatenate([bias_pair[0], jnp.zeros((group,), F32), bias_pair[1]])

    tokens_all = []
    for item in range(items):
        pairs = [latent[item]]
        for block in ring_gather(latent[item, :half])[1:]:
            pairs += [block, swap(block)]
        tokens_all.append(jnp.concatenate(pairs, 0))

    proj_t = proj_weight.T
    down_t = down_weight.T
    (proj_full,) = place(gather_pieces(proj_t), [half_width])
    up_full, down_full = place(
        gather_pieces(jnp.concatenate([up_weight, down_t], 1)), [hidden, hidden]
    )
    (qkv_full,) = place(
        gather_pieces(qkv_groups.transpose(1, 0, 2).reshape(rows, -1)), [3 * half_width]
    )

    bias_proj = proj_bias.astype(F32)
    bias_down = down_bias.astype(F32)
    bias_up = lax.dynamic_slice_in_dim(up_bias.astype(F32), t * hidden, hidden, 0)
    block = min(256, here * size_c)

    saved = []
    outputs = []
    for item in range(items):
        in_first = (
            normalize(tokens_all[item].astype(F32))[0] * (1.0 + scale_one[item])
            + shift_one[item]
        ).astype(BF16)
        qkv = (dot(in_first, qkv_mine, ((1,), (0,))) + bias_mine).astype(BF16)
        keys = qkv[:, group : 2 * group]
        values = qkv[:, 2 * group :]
        qkv_t = qkv.T.reshape(3, group, -1)
        mixed_t, logs = attend(qkv_t, keys, block)
        sent = [
            shift(mixed_t[:, k * here : (k + 1) * here], -k) if k else mixed_t[:, :here]
            for k in range(size_c)
        ]
        mixed = absolute(sent, c, 1).reshape(half_width, here)
        part = dot(mixed, proj_full, ((0,), (1,)))
        attended = part[:half] + swap(part[half:].astype(BF16)).astype(F32) + bias_proj
        residual = latent[item, :half].astype(F32) + gate_one[item] * attended
        normed, inverse = normalize(residual)
        in_second_half = (normed * (1.0 + scale_two[item]) + shift_two[item]).astype(BF16)
        in_second = jnp.concatenate([in_second_half, swap(in_second_half)], 0)
        saved.append(
            dict(
                in_first=in_first,
                keys=keys,
                values=values,
                qkv_t=qkv_t,
                logs=logs,
                mixed=mixed,
                attended=attended,
                residual=residual,
                normed=normed,
                inverse=inverse,
                in_second=in_second,
            )
        )

    for item, kept in enumerate(saved):
        upward = dot(kept["in_second"], up_full, ((1,), (0,))) + bias_up
        grad_feed = (cotangent[item].astype(F32) * gate_two[item]).astype(BF16)
        grad_act = dot(grad_feed, down_full, ((1,), (0,)))
        activated, pull = jax.vjp(partial(jax.nn.gelu, approximate=True), upward)
        activated = activated.astype(BF16)
        grad_upward = pull(grad_act)[0].astype(BF16)
        part = dot(grad_upward, up_full, ((1,), (1,)))
        kept["grad_in_second"] = part[:half] + swap(part[half:].astype(BF16)).astype(F32)
        part = dot(activated, down_full, ((1,), (1,)))
        kept["feed_out"] = (
            part[:half] + swap(part[half:].astype(BF16)).astype(F32) + bias_down
        )
        out_half = (kept["residual"] + gate_two[item] * kept["feed_out"]).astype(BF16)
        outputs.append(both(out_half, swap(out_half), 0))
        kept.update(activated=activated, grad_upward=grad_upward, grad_feed=grad_feed)

    input_grads = []
    mod_terms = []
    for item, kept in enumerate(saved):
        cot = cotangent[item, :half].astype(F32)
        grad_in_second = kept["grad_in_second"]
        grad_residual = cot + norm_back(
            grad_in_second * (1.0 + scale_two[item]), kept["normed"], kept["inverse"]
        )
        grad_attended_half = (grad_residual * gate_one[item]).astype(BF16)
        grad_attended = jnp.concatenate([grad_attended_half, swap(grad_attended_half)], 0)
        grad_mixed = (
            dot(proj_full, grad_attended, ((0,), (1,)))
            .astype(BF16)
            .reshape(size_c, group, here)
        )
        grad_mixed = [
            shift(lax.dynamic_index_in_dim(grad_mixed, (c + k) % size_c, 0, False), k) if k
            else lax.dynamic_index_in_dim(grad_mixed, c, 0, False)
            for k in range(size_c)
        ]
        grad_qkv = attend_back(
            kept["qkv_t"],
            kept["keys"],
            kept["values"],
            jnp.concatenate(grad_mixed, 1),
            kept["logs"],
            block,
        ).reshape(3 * group, -1)
        sent = [
            shift(grad_qkv[:, k * here : (k + 1) * here], -k) if k else grad_qkv[:, :here]
            for k in range(size_c)
        ]
        grad_here = absolute(sent, c, 1).reshape(3 * half_width, here)
        part = dot(grad_here, qkv_full, ((0,), (1,)))
        grad_in_first = part[:half] + swap(part[half:].astype(BF16)).astype(F32)
        normed_one, inverse_one = normalize(latent[item, :half].astype(F32))
        grad_latent = grad_residual + norm_back(
            grad_in_first * (1.0 + scale_one[item]), normed_one, inverse_one
        )
        input_grads.append(both(grad_latent, swap(grad_latent), 0))
        mod_terms.append(
            jnp.stack(
                [
                    jnp.sum(grad_in_first, 0),
                    jnp.sum(grad_in_first * normed_one, 0),
                    jnp.sum(grad_residual * kept["attended"], 0),
                    jnp.sum(grad_in_second, 0),
                    jnp.sum(grad_in_second * kept["normed"], 0),
                    jnp.sum(cot * kept["feed_out"], 0),
                ]
            )
        )
        kept.update(grad_attended=grad_attended, grad_qkv=grad_qkv)

    def rows_of(name):
        return jnp.concatenate([kept[name] for kept in saved], 0)

    def columns_of(name):
        return jnp.concatenate([kept[name] for kept in saved], 1)

    grad_feed = rows_of("grad_feed")
    grad_upward = rows_of("grad_upward")
    grad_attended = rows_of("grad_attended")
    grad_qkv = columns_of("grad_qkv")
    by_rows = ((0,), (0,))
    grad_down = ring_reduce(reduce_rows(grad_feed, rows_of("activated"), by_rows)).T
    grad_up = ring_reduce(reduce_rows(rows_of("in_second"), grad_upward, by_rows))
    grad_proj = ring_reduce(reduce_rows(grad_attended, columns_of("mixed"), ((0,), (1,)))).T
    qkv_rows = reduce_rows(rows_of("in_first"), grad_qkv, ((0,), (1,)))
    sent = [
        shift(lax.dynamic_index_in_dim(qkv_rows, (c + k) % size_c, 0, False), k) if k
        else lax.dynamic_index_in_dim(qkv_rows, c, 0, False)
        for k in range(size_c)
    ]
    grad_qkv_weight = (
        absolute(sent, c, -1)
        .reshape(size_c, rows, 3, group)
        .transpose(1, 2, 0, 3)
        .reshape(rows, 3, half_width)
    )

    own_rows = [kept["grad_attended"][:half] for kept in saved]
    proj_sum = sum(jnp.sum(piece.astype(F32), 0) for piece in own_rows)
    down_sum = sum(jnp.sum(kept["grad_feed"][:half].astype(F32), 0) for kept in saved)
    up_sum = jnp.sum(grad_upward.astype(F32), 0)
    qkv_sum = jnp.sum(grad_qkv.astype(F32), 1).reshape(3, group)
    pair_sum = jnp.stack([qkv_sum[0], qkv_sum[2]])
    up_total = lax.dynamic_update_slice_in_dim(
        jnp.zeros(up_bias.shape, F32), up_sum, t * hidden, 0
    )
    pair_total = lax.dynamic_update_slice_in_dim(
        jnp.zeros(qv_bias.shape, F32), pair_sum, first_column + c * group, 1
    )
    sums = jnp.concatenate([up_total, pair_total.reshape(-1), proj_sum, down_sum])
    sums = sums.reshape(-1, 128)
    for axis in ("fsdp", "ctx", "tp"):
        sums = butterfly_sum(sums, axis)
    sums = sums.reshape(-1)
    ends = [up_bias.shape[0], up_bias.shape[0] + qv_bias.size]
    grad_up_bias = sums[: ends[0]]
    grad_qv_bias = sums[ends[0] : ends[1]].reshape(qv_bias.shape)
    grad_proj_bias = sums[ends[1] : ends[1] + model]
    grad_down_bias = sums[ends[1] + model :]

    grad_mod = jnp.stack(mod_terms)
    grad_mod = butterfly_sum(butterfly_sum(grad_mod, "tp"), "ctx").astype(BF16)
    grad_mod_all = cube_gather(grad_mod)
    grad_ada_bias = jnp.sum(
        absolute_xor(grad_mod_all, f).astype(F32), (0, 1)
    )
    mod_here = lax.dynamic_slice_in_dim(grad_mod_all, first_column, half_width, 3).reshape(
        size_f * items, -1
    )
    grad_ada = dot(silu_here, mod_here, ((0,), (0,))).reshape(rows, 6, half_width)
    cond_part = dot(mod_here, ada_weight.reshape(rows, -1), ((1,), (1,)))
    cond_part = lax.dynamic_update_slice_in_dim(
        jnp.zeros((size_f * items, model), F32), cond_part, first_row, 1
    ).reshape(size_f, items, model)
    cond_total = butterfly_sum(butterfly_sum(cube_reduce(cond_part), "ctx"), "tp")
    grad_cond = jax.vjp(jax.nn.silu, cond)[1](cond_total)[0]

    return (
        jnp.stack(outputs).reshape(latents.shape),
        jnp.stack(input_grads).reshape(latents.shape),
        grad_cond.reshape(condition.shape),
        grad_ada,
        grad_ada_bias,
        grad_qkv_weight,
        grad_qv_bias,
        grad_proj,
        grad_proj_bias,
        grad_up,
        grad_up_bias,
        grad_down,
        grad_down_bias,
    )


def absolute_xor(entries, rank):
    size = entries.shape[0]
    for bit in range(size.bit_length() - 1):
        pairs = entries.reshape(-1, 2, 1 << bit, *entries.shape[1:])
        turned = jnp.flip(pairs, 1)
        entries = jnp.where((rank >> bit) % 2 == 0, pairs, turned).reshape(entries.shape)
    return entries


def solution(mesh):
    in_specs = (
        P(None, "fsdp", "ctx", None),
        P(None, "fsdp", None),
        P(None, "fsdp", "ctx", None),
        P(("fsdp", "ctx"), None, "tp"),
        P(),
        P(("fsdp", "ctx"), None, "tp"),
        P(),
        P("tp", ("fsdp", "ctx")),
        P(),
        P(("fsdp", "ctx"), "tp"),
        P(),
        P("tp", ("fsdp", "ctx")),
        P(),
    )
    out_specs = (
        P(None, "fsdp", "ctx", None),
        P(None, "fsdp", "ctx", None),
        P(None, "fsdp", None),
        P(("fsdp", "ctx"), None, "tp"),
        P(),
        P(("fsdp", "ctx"), None, "tp"),
        P(),
        P("tp", ("fsdp", "ctx")),
        P(),
        P(("fsdp", "ctx"), "tp"),
        P(),
        P("tp", ("fsdp", "ctx")),
        P(),
    )
    return jax.shard_map(body, mesh=mesh, in_specs=in_specs, out_specs=out_specs, check_vma=False)
```

```python
from functools import partial

import jax
import jax.numpy as jnp
from jax import lax
from jax.experimental import pallas as pl
from jax.experimental.pallas import tpu as pltpu
from jax.sharding import PartitionSpec as P

HEADS = 16
HEAD_DIM = 72
LOG2E = 1.4426950408889634
F32 = jnp.float32
BF16 = jnp.bfloat16


def dot(a, b, dims):
    return lax.dot_general(a, b, (dims, ((), ())), preferred_element_type=F32)


def normalize(values):
    centre = values - jnp.mean(values, -1, keepdims=True)
    inverse = lax.rsqrt(jnp.mean(centre * centre, -1, keepdims=True) + 1e-06)
    return (centre * inverse, inverse)


def norm_back(incoming, normed, inverse):
    return inverse * (
        incoming
        - jnp.mean(incoming, -1, keepdims=True)
        - normed * jnp.mean(incoming * normed, -1, keepdims=True)
    )


def shift(x, k, name="shift"):
    size = lax.axis_size("ctx")
    with jax.named_scope(name):
        return lax.ppermute(x, "ctx", [(i, (i + k) % size) for i in range(size)])


def flip(x, axis, bit, name="flip"):
    size = lax.axis_size(axis)
    with jax.named_scope(name):
        return lax.ppermute(x, axis, [(i, i ^ (1 << bit)) for i in range(size)])


def exchange(x, name):
    with jax.named_scope(name):
        return lax.all_to_all(x, "ctx", 0, 0)


def gather_rows(x, name):
    with jax.named_scope(name):
        return lax.all_gather(x, ("fsdp", "ctx"), tiled=True)


def bits_of(axis):
    return lax.axis_size(axis).bit_length() - 1


def ring_gather(x, name):
    size = lax.axis_size("ctx")
    blocks = [x] * size
    moving = x
    for step in range(1, size // 2 + 1):
        moving = shift(moving, 1, name + "_right")
        blocks[step] = moving
    moving = x
    for step in range(1, (size - 1) // 2 + 1):
        moving = shift(moving, -1, name + "_left")
        blocks[size - step] = moving
    return blocks


def butterfly_sum(x, axis, name):
    for bit in range(bits_of(axis)):
        x = x + flip(x, axis, bit, name)
    return x


def butterfly_max(x, axis, name):
    for bit in range(bits_of(axis)):
        x = jnp.maximum(x, flip(x, axis, bit, name))
    return x


def cube_gather(x, name):
    x = x[None]
    for bit in range(bits_of("fsdp")):
        x = jnp.concatenate([x, flip(x, "fsdp", bit, name)], 0)
    return x


def cube_reduce(x, name):
    for bit in reversed(range(bits_of("fsdp"))):
        half = x.shape[0] // 2
        x = x[:half] + flip(x[half:], "fsdp", bit, name)
    return x[0]


def spread(pieces, name):
    for bit in reversed(range(bits_of("fsdp"))):
        pieces = pieces + [
            (offset ^ (1 << bit), places, flip(block, "fsdp", bit, name + "_%d" % bit))
            for offset, places, block in pieces
        ]
    return pieces


def gather_stacked(shard, name):
    blocks = ring_gather(shard, name)
    return spread([(0, "before", jnp.stack(blocks))], name)


def place_kernel(targets, widths, *refs):
    count = len(targets)
    ins, outs = refs[:count], refs[-3 - len(widths) : -3]
    held, in_sem, out_sem = refs[-3:]
    own_f = lax.axis_index("fsdp")
    own_c = lax.axis_index("ctx")
    size_c = lax.axis_size("ctx")
    arriving, leaving = [], []
    for (offset, places), ref in zip(targets, ins):
        row = jnp.bitwise_xor(own_f, offset)
        for at in range(size_c):
            column = at if places == "own" else lax.rem(own_c + size_c - at, size_c)
            slot = len(arriving)
            arriving.append(pltpu.make_async_copy(ref.at[at], held.at[slot], in_sem.at[slot]))
            first = 0
            for width, out in zip(widths, outs):
                leaving.append(
                    pltpu.make_async_copy(
                        held.at[slot, :, pl.ds(first, width)],
                        out.at[row, column],
                        out_sem.at[len(leaving)],
                    )
                )
                first += width
    for copy in arriving:
        copy.start()
    each = len(widths)
    for slot, copy in enumerate(arriving):
        copy.wait()
        for out_copy in leaving[slot * each : (slot + 1) * each]:
            out_copy.start()
    for copy in leaving:
        copy.wait()


def place(pieces, widths, after=()):
    size_f, size_c = lax.axis_size("fsdp"), lax.axis_size("ctx")
    rows, total = pieces[0][2].shape[1:]
    count = size_f * size_c
    outs = pl.pallas_call(
        partial(place_kernel, [piece[:2] for piece in pieces], widths),
        out_shape=[jax.ShapeDtypeStruct((size_f, size_c, rows, width), BF16) for width in widths],
        in_specs=[ANYWHERE] * (len(pieces) + len(after)),
        out_specs=[ANYWHERE] * len(widths),
        scratch_shapes=[
            pltpu.VMEM((count, rows, total), BF16),
            pltpu.SemaphoreType.DMA((count,)),
            pltpu.SemaphoreType.DMA((count * len(widths),)),
        ],
        compiler_params=pltpu.CompilerParams(vmem_limit_bytes=40 << 20),
        cost_estimate=pl.CostEstimate(
            flops=0, bytes_accessed=4 * count * rows * total, transcendentals=0
        ),
    )(*[piece[2] for piece in pieces], *after)
    return [out.reshape(-1, width) for out, width in zip(outs, widths)]


def lower(x, scale):
    return x if scale is None else (x * scale).astype(jnp.float16)


def higher(x, scale):
    return x if scale is None else x.astype(F32) * (1.0 / scale)


def reduce_rows(send, keep, name, scale=None):
    size_c = lax.axis_size("ctx")
    own_f = lax.axis_index("fsdp")
    _, width, columns = keep.shape
    parts = [keep, flip(send, "fsdp", 0, name + "_0")]
    for bit in range(1, bits_of("fsdp")):
        own_bit = (own_f >> bit) % 2
        pairs = [part.reshape(-1, 2, width, columns) for part in parts]
        got = sum(lax.dynamic_index_in_dim(pair, 1 - own_bit, 1, False) for pair in pairs)
        got = flip(lower(got, scale), "fsdp", bit, name + "_%d" % bit)
        parts = [lax.dynamic_index_in_dim(pair, own_bit, 1, False) for pair in pairs]
        parts.append(higher(got, scale))
    return sum(parts).reshape(size_c, width // size_c, columns)


def ring_reduce(blocks, name, scale=None):
    size = lax.axis_size("ctx")
    own = lax.axis_index("ctx")

    def block(offset):
        return lax.dynamic_index_in_dim(blocks, (own + offset) % size, 0, False)

    total = block(0)
    for sign, reach in ((1, size // 2), (-1, (size - 1) // 2)):
        moving = None
        for distance in range(reach, 0, -1):
            term = block(sign * distance)
            if moving is not None:
                term = term + moving
            moving = higher(shift(lower(term, scale), sign, name + "_ring"), scale)
        if moving is not None:
            total = total + moving
    return total


def whole(shape):
    return pl.BlockSpec(tuple(shape), lambda *_: (0,) * len(shape))


def struct(shape, dtype):
    return jax.ShapeDtypeStruct(tuple(shape), dtype)


ANYWHERE = pl.BlockSpec(memory_space=pltpu.HBM)
PARAMS = pltpu.CompilerParams(vmem_limit_bytes=48 << 20)


def cost(flops, nbytes, exps=0):
    return pl.CostEstimate(flops=int(flops), bytes_accessed=int(nbytes), transcendentals=int(exps))


def mods_spec(mods, item):
    return pl.BlockSpec((None,) + mods.shape[1:], lambda *_: (item, 0, 0))


def largest(x):
    return jnp.full((8, 128), jnp.max(jnp.abs(x)), F32)


def slab_call(kernel, args, in_specs, helds, after=(), **options):
    taken = [held for held in helds if held is not None]
    count = len(args)
    more = len(taken) + len(after)

    def run(*refs):
        kernel(*refs[:count], *refs[count + more :])

    return pl.pallas_call(
        run,
        in_specs=in_specs + [ANYWHERE] * more,
        input_output_aliases={count + at: at for at in range(len(taken))},
        compiler_params=PARAMS,
        **options,
    )(*args, *taken, *after)


def halves_kernel(first, both_ref, own_ref, peer_ref):
    count, half, _ = own_ref.shape
    t = lax.axis_index("tp")
    for rank, out in ((t, own_ref), (1 - t, peer_ref)):
        rows = pl.ds(pl.multiple_of(rank * half, half), half)
        for at in range(count):
            out[at] = both_ref[first + at, rows, :]


def halves(x, first, count, after=()):
    items, here, model = x.shape
    shape = (count, here // 2, model)
    return slab_call(
        partial(halves_kernel, first),
        [x],
        [whole(x.shape)],
        [],
        after,
        grid=(1,),
        out_specs=[whole(shape)] * 2,
        out_shape=[struct(shape, x.dtype)] * 2,
        cost_estimate=cost(0, 4 * count * here * model),
    )


def wait_kernel(in_ref, out_ref):
    out_ref[...] = in_ref[...]


def once_after(x, after):
    return slab_call(
        wait_kernel,
        [x],
        [whole(x.shape)],
        [],
        after,
        grid=(1,),
        out_specs=whole(x.shape),
        out_shape=struct(x.shape, x.dtype),
        cost_estimate=cost(0, 4 * x.size),
    )


def project_kernel(count, *refs):
    pieces = refs[:count]
    mods_ref, weight_ref, bias_ref, in_ref, out_ref = refs[count:]
    for pair in range(count // 2):
        rows = jnp.concatenate([pieces[2 * pair][...], pieces[2 * pair + 1][...]], 0)
        here = rows.shape[0]
        normed, _ = normalize(rows.astype(F32))
        in_first = (normed * (1.0 + mods_ref[1:2, :]) + mods_ref[0:1, :]).astype(BF16)
        in_ref[pl.ds(pair * here, here), :] = in_first
        product = dot(weight_ref[...], in_first, ((1,), (1,))) + bias_ref[...]
        out_ref[:, pl.ds(pair * here, here)] = product.astype(BF16)


def project(pieces, place_in, mods, item, items, weight_t, bias, held, after=()):
    _, half, model = pieces[0].shape
    total = half * len(pieces)
    piece_spec = pl.BlockSpec((None, half, model), lambda i: (place_in, 0, 0))
    width = weight_t.shape[0]
    return slab_call(
        partial(project_kernel, len(pieces)),
        [*pieces, mods, weight_t, bias],
        [piece_spec] * len(pieces)
        + [mods_spec(mods, item), whole(weight_t.shape), whole(bias.shape)],
        [held],
        after,
        grid=(1,),
        out_specs=[
            pl.BlockSpec((total, model), lambda i: (item, 0)),
            whole((width, total)),
        ],
        out_shape=[struct((items * total, model), BF16), struct((width, total), BF16)],
        cost_estimate=cost(2 * total * model * width, 6 * total * model),
    )


def head_rows(values, head):
    values = values.astype(F32)
    row = lax.broadcasted_iota(jnp.int32, values.shape, 0)
    inside = (row >= head * HEAD_DIM) & (row < (head + 1) * HEAD_DIM)
    return jnp.where(inside, values, 0.0).astype(BF16), inside


def attend_kernel(heads, steps, q_ref, kt_ref, vt_ref, out_ref, log_ref, k_ref):
    step = pl.program_id(0)
    factor = HEAD_DIM ** (-0.5) * LOG2E

    @pl.when(step == 0)
    def _():
        k_ref[...] = kt_ref[...].T

    total = None
    for head in range(heads):
        q_head, inside = head_rows(q_ref[...], head)
        scores = dot(k_ref[...], q_head, ((1,), (0,)))
        highest = jnp.max(scores, 0, keepdims=True)
        exponent = jnp.exp2((scores - highest) * factor)
        summed = jnp.sum(exponent, 0, keepdims=True)
        chances = (exponent * (1.0 / summed)).astype(BF16)
        mixed = dot(vt_ref[...], chances, ((1,), (0,)))
        total = mixed if total is None else jnp.where(inside, mixed, total)
        log_ref[pl.ds(head, 1), :] = highest * factor + jnp.log2(summed)
    out_ref[lax.rem(lax.axis_index("ctx") + steps - step, steps)] = total.astype(BF16)


def attend(qkv_t, here, after=()):
    group, total = qkv_t.shape[0] // 3, qkv_t.shape[1]
    heads, steps = group // HEAD_DIM, total // here
    thirds = qkv_t.reshape(3, group, total)
    return slab_call(
        partial(attend_kernel, heads, steps),
        [thirds, thirds, thirds],
        [
            pl.BlockSpec((None, group, here), lambda i: (0, 0, i)),
            pl.BlockSpec((None, group, total), lambda i: (1, 0, 0)),
            pl.BlockSpec((None, group, total), lambda i: (2, 0, 0)),
        ],
        [],
        after,
        grid=(steps,),
        out_specs=[
            whole((steps, group, here)),
            pl.BlockSpec((heads, here), lambda i: (0, i)),
        ],
        out_shape=[struct((steps, group, here), BF16), struct((heads, total), F32)],
        scratch_shapes=[pltpu.VMEM((total, group), BF16)],
        cost_estimate=cost(heads * total * total * 1600, 8 * group * total, heads * total * total),
    )


def attend_back_kernel(
    heads,
    steps,
    q_ref,
    kt_ref,
    vt_ref,
    log_ref,
    grad_ref,
    all_ref,
    out_ref,
    k_ref,
    v_ref,
    dk_ref,
    dv_ref,
):
    step = pl.program_id(0)
    own_c = lax.axis_index("ctx")
    scaling = HEAD_DIM ** (-0.5)
    group, block = q_ref.shape

    @pl.when(step == 0)
    def _():
        dk_ref[...] = jnp.zeros_like(dk_ref)
        dv_ref[...] = jnp.zeros_like(dv_ref)
        k_ref[...] = kt_ref[...].T
        v_ref[...] = vt_ref[...].T

    grad = grad_ref[lax.rem(own_c + steps - step, steps)]
    grad_query = None
    for head in range(heads):
        q_head, inside = head_rows(q_ref[...], head)
        do_head, _ = head_rows(grad, head)
        scores = dot(k_ref[...], q_head, ((1,), (0,)))
        chances = jnp.exp2(scores * (scaling * LOG2E) - log_ref[pl.ds(head, 1), :])
        grad_chances = dot(v_ref[...], do_head, ((1,), (0,)))
        weighted = jnp.sum(chances * grad_chances, 0, keepdims=True)
        grad_scores = (chances * (grad_chances - weighted)).astype(BF16)
        term = dot(kt_ref[...], grad_scores, ((1,), (0,)))
        grad_query = term if grad_query is None else jnp.where(inside, term, grad_query)
        dk_ref[...] += dot(q_head, grad_scores, ((1,), (1,)))
        dv_ref[...] += dot(do_head, chances.astype(BF16), ((1,), (1,)))
    columns = pl.ds(pl.multiple_of(step * block, block), block)
    all_ref[0, :, columns] = (grad_query * scaling).astype(BF16)

    @pl.when(step == steps - 1)
    def _():
        all_ref[1] = (dk_ref[...] * scaling).astype(BF16)
        all_ref[2] = dv_ref[...].astype(BF16)
        for at in range(steps):
            out_ref[lax.rem(own_c + steps - at, steps)] = all_ref[
                :, :, at * block : (at + 1) * block
            ]


def attend_back(qkv_t, grads, logs, held, item, items, after=()):
    group, total = qkv_t.shape[0] // 3, qkv_t.shape[1]
    heads, steps = group // HEAD_DIM, grads.shape[0]
    here = total // steps
    thirds = qkv_t.reshape(3, group, total)
    return slab_call(
        partial(attend_back_kernel, heads, steps),
        [thirds, thirds, thirds, logs, grads],
        [
            pl.BlockSpec((None, group, here), lambda i: (0, 0, i)),
            pl.BlockSpec((None, group, total), lambda i: (1, 0, 0)),
            pl.BlockSpec((None, group, total), lambda i: (2, 0, 0)),
            pl.BlockSpec((heads, here), lambda i: (0, i)),
            whole(grads.shape),
        ],
        [held],
        after,
        grid=(steps,),
        out_specs=[
            pl.BlockSpec((3, group, total), lambda i: (0, 0, item)),
            whole((steps, 3, group, here)),
        ],
        out_shape=[
            struct((3, group, items * total), BF16),
            struct((steps, 3, group, here), BF16),
        ],
        scratch_shapes=[
            pltpu.VMEM((total, group), BF16),
            pltpu.VMEM((total, group), BF16),
            pltpu.VMEM((group, total), F32),
            pltpu.VMEM((group, total), F32),
        ],
        cost_estimate=cost(heads * total * total * 4000, 16 * group * total, heads * total * total),
    )


def back_to_rows_kernel(contract, keep, blocks_ref, weight_ref, *outs):
    own_ref, peer_ref = outs[-2:]
    rows = blocks_ref[...].reshape(-1, blocks_ref.shape[-1])
    if keep:
        outs[0][...] = rows
    total = dot(rows, weight_ref[...], ((0,), (contract,)))
    half = own_ref.shape[0]
    own_ref[...] = total[:half]
    peer_ref[...] = total[half:]


def back_to_rows(blocks, weight, contract, keep=False, held=None, item=0, items=1, after=()):
    here = blocks.shape[-1]
    features, model = weight.shape[contract], weight.shape[1 - contract]
    half = here // 2
    out_specs = [whole((half, model))] * 2
    out_shape = [struct((half, model), F32)] * 2
    if keep:
        out_specs = [pl.BlockSpec((features, here), lambda i: (0, item))] + out_specs
        out_shape = [struct((features, items * here), BF16)] + out_shape
    return slab_call(
        partial(back_to_rows_kernel, contract, keep),
        [blocks, weight],
        [whole(blocks.shape), whole(weight.shape)],
        [held],
        after,
        grid=(1,),
        out_specs=out_specs,
        out_shape=out_shape,
        cost_estimate=cost(
            2 * here * features * model, 2 * features * model + 8 * here * model
        ),
    )


def second_kernel(own_ref, peer_ref, bias_ref, latent_ref, mods_ref, att_ref, res_ref, in_ref):
    attended = own_ref[...] + peer_ref[...] + bias_ref[...]
    residual = latent_ref[...].astype(F32) + mods_ref[2:3, :] * attended
    normed, _ = normalize(residual)
    att_ref[...] = attended
    res_ref[...] = residual
    in_ref[...] = (normed * (1.0 + mods_ref[4:5, :]) + mods_ref[3:4, :]).astype(BF16)


def second(own, peer, bias, latent, place_in, mods, item, after=()):
    shape = own.shape
    return slab_call(
        second_kernel,
        [own, peer, bias, latent, mods],
        [
            whole(shape),
            whole(shape),
            whole(bias.shape),
            pl.BlockSpec((None,) + shape, lambda i: (place_in, 0, 0)),
            mods_spec(mods, item),
        ],
        [],
        after,
        grid=(1,),
        out_specs=[whole(shape)] * 3,
        out_shape=[struct(shape, F32), struct(shape, F32), struct(shape, BF16)],
        cost_estimate=cost(20 * own.size, 20 * own.size),
    )


def feed_kernel(
    steps,
    own_ref,
    peer_ref,
    cot_own,
    cot_peer,
    mods_ref,
    up_ref,
    down_ref,
    bias_ref,
    in_all,
    grad_all,
    act_ref,
    gup_ref,
    out_own,
    out_peer,
    gin_own,
    gin_peer,
    sum_ref,
    highs,
    in_ref,
    grad_ref,
    out_acc,
    gin_acc,
):
    step = pl.program_id(0)
    half = own_ref.shape[0]

    @pl.when(step == 0)
    def _():
        in_ref[:half, :] = own_ref[...]
        in_ref[half:, :] = peer_ref[...]
        in_all[...] = in_ref[...]
        gate = mods_ref[5:6, :]
        grad_ref[:half, :] = (cot_own[...].astype(F32) * gate).astype(BF16)
        grad_ref[half:, :] = (cot_peer[...].astype(F32) * gate).astype(BF16)
        grad_all[...] = grad_ref[...]
        highs[0] = largest(in_ref[...].astype(F32))
        highs[1] = largest(grad_ref[...].astype(F32))
        highs[2] = jnp.zeros((8, 128), F32)
        highs[3] = jnp.zeros((8, 128), F32)

    upward = dot(in_ref[...], up_ref[...], ((1,), (0,))) + bias_ref[...]
    grad_act = dot(grad_ref[...], down_ref[...], ((1,), (0,)))
    inner = 0.7978845608028654
    squared = upward * upward
    curve = jnp.tanh(inner * upward * (1.0 + 0.044715 * squared))
    activated = (0.5 * upward * (1.0 + curve)).astype(BF16)
    slope = 0.5 * (1.0 + curve) + (0.5 * inner) * upward * (1.0 - curve * curve) * (
        1.0 + (3.0 * 0.044715) * squared
    )
    grad_up = (slope * grad_act).astype(BF16)
    act_ref[...] = activated
    gup_ref[...] = grad_up
    wide = grad_up.astype(F32)
    sum_ref[...] = jnp.sum(wide, 0, keepdims=True)
    highs[2] = jnp.maximum(highs[2], largest(activated.astype(F32)))
    highs[3] = jnp.maximum(highs[3], largest(wide))
    out_term = dot(activated, down_ref[...], ((1,), (1,)))
    gin_term = dot(grad_up, up_ref[...], ((1,), (1,)))

    @pl.when(step == 0)
    def _():
        out_acc[...] = out_term
        gin_acc[...] = gin_term

    @pl.when(step > 0)
    def _():
        out_acc[...] += out_term
        gin_acc[...] += gin_term

    @pl.when(step == steps - 1)
    def _():
        out_own[...] = out_acc[:half, :]
        out_peer[...] = out_acc[half:, :].astype(BF16)
        gin_own[...] = gin_acc[:half, :]
        gin_peer[...] = gin_acc[half:, :]


def feed(own, peer, cots, mods, weights, bias, helds, item, items, after=()):
    half, model = own.shape
    here, hidden = 2 * half, weights.shape[1] // 2
    cot = pl.BlockSpec((None, half, model), lambda j: (item, 0, 0))
    tile = 768
    steps = hidden // tile
    rows = pl.BlockSpec((here, model), lambda j: (item, 0))
    slab = pl.BlockSpec((here, tile), lambda j: (item, j))
    return slab_call(
        partial(feed_kernel, steps),
        [own, peer, *cots, mods, weights, weights, bias],
        [whole(own.shape)] * 2
        + [cot] * 2
        + [
            mods_spec(mods, item),
            pl.BlockSpec((model, tile), lambda j: (0, j)),
            pl.BlockSpec((model, tile), lambda j: (0, j + steps)),
            pl.BlockSpec((1, tile), lambda j: (0, j)),
        ],
        helds,
        after,
        grid=(steps,),
        out_specs=[rows, rows, slab, slab]
        + [pl.BlockSpec((half, model), lambda j: (item, 0))] * 2
        + [whole(own.shape)] * 2
        + [pl.BlockSpec((1, tile), lambda j: (0, j)), whole((4, 8, 128))],
        out_shape=[
            struct((items * here, model), BF16),
            struct((items * here, model), BF16),
            struct((items * here, hidden), BF16),
            struct((items * here, hidden), BF16),
            struct((items * half, model), F32),
            struct((items * half, model), BF16),
            struct(own.shape, F32),
            struct(own.shape, F32),
            struct((1, hidden), F32),
            struct((4, 8, 128), F32),
        ],
        scratch_shapes=[
            pltpu.VMEM((here, model), BF16),
            pltpu.VMEM((here, model), BF16),
            pltpu.VMEM((here, model), F32),
            pltpu.VMEM((here, model), F32),
        ],
        cost_estimate=cost(8 * here * model * hidden, 4 * model * hidden + 4 * here * hidden),
    )


def finish_kernel(own_ref, peer_ref, bias_ref, res_ref, cot_ref, mods_ref, out_ref, sum_ref):
    feed_out = own_ref[...] + peer_ref[...].astype(F32) + bias_ref[...]
    out_ref[...] = (res_ref[...] + mods_ref[5:6, :] * feed_out).astype(BF16)
    sum_ref[...] = jnp.sum(cot_ref[...].astype(F32) * feed_out, 0, keepdims=True)


def finish(own, peer, bias, residual, cots, mods, held, item, after=()):
    items, half, model = cots.shape
    part = pl.BlockSpec((half, model), lambda i: (item, 0))
    return slab_call(
        finish_kernel,
        [own, peer, bias, residual, cots, mods],
        [
            part,
            part,
            whole(bias.shape),
            whole((half, model)),
            pl.BlockSpec((None, half, model), lambda i: (item, 0, 0)),
            mods_spec(mods, item),
        ],
        [held],
        after,
        grid=(1,),
        out_specs=[part, whole(bias.shape)],
        out_shape=[struct((items * half, model), BF16), struct(bias.shape, F32)],
        cost_estimate=cost(8 * half * model, 16 * half * model),
    )


def second_back_kernel(
    own_ref, peer_ref, res_ref, att_ref, cot_ref, mods_ref, grad_ref, low_ref, sum_ref
):
    incoming = own_ref[...] + peer_ref[...]
    normed, inverse = normalize(res_ref[...])
    grad = cot_ref[...].astype(F32) + norm_back(
        incoming * (1.0 + mods_ref[4:5, :]), normed, inverse
    )
    low = (grad * mods_ref[2:3, :]).astype(BF16)
    grad_ref[...] = grad
    low_ref[...] = low
    sum_ref[0:1, :] = jnp.sum(grad * att_ref[...], 0, keepdims=True)
    sum_ref[1:2, :] = jnp.sum(incoming, 0, keepdims=True)
    sum_ref[2:3, :] = jnp.sum(incoming * normed, 0, keepdims=True)
    sum_ref[3:4, :] = jnp.sum(low.astype(F32), 0, keepdims=True)


def second_back(own, peer, residual, attended, cots, mods, item, after=()):
    shape = own.shape
    return slab_call(
        second_back_kernel,
        [own, peer, residual, attended, cots, mods],
        [whole(shape)] * 4
        + [pl.BlockSpec((None,) + shape, lambda i: (item, 0, 0)), mods_spec(mods, item)],
        [],
        after,
        grid=(1,),
        out_specs=[whole(shape), whole(shape), whole((4, shape[1]))],
        out_shape=[struct(shape, F32), struct(shape, BF16), struct((4, shape[1]), F32)],
        cost_estimate=cost(30 * own.size, 24 * own.size),
    )


def grad_mixed_kernel(own_ref, peer_ref, weight_ref, all_ref, out_ref):
    rows = jnp.concatenate([own_ref[...], peer_ref[...]], 0)
    all_ref[...] = rows
    out_ref[...] = dot(weight_ref[...], rows, ((1,), (1,))).astype(BF16)


def grad_mixed_of(own, peer, weight, held, item, items, after=()):
    features, model = weight.shape
    here = 2 * own.shape[0]
    return slab_call(
        grad_mixed_kernel,
        [own, peer, weight],
        [whole(own.shape), whole(own.shape), whole(weight.shape)],
        [held],
        after,
        grid=(1,),
        out_specs=[
            pl.BlockSpec((here, model), lambda i: (item, 0)),
            whole((features, here)),
        ],
        out_shape=[struct((items * here, model), BF16), struct((features, here), BF16)],
        cost_estimate=cost(2 * here * features * model, 2 * features * model),
    )


def first_back_kernel(own_ref, peer_ref, latent_ref, res_ref, mods_ref, grad_ref, sum_ref):
    incoming = own_ref[...] + peer_ref[...]
    normed, inverse = normalize(latent_ref[...].astype(F32))
    grad_ref[...] = res_ref[...] + norm_back(
        incoming * (1.0 + mods_ref[1:2, :]), normed, inverse
    )
    sum_ref[0:1, :] = jnp.sum(incoming, 0, keepdims=True)
    sum_ref[1:2, :] = jnp.sum(incoming * normed, 0, keepdims=True)


def first_back(own, peer, latent, place_in, grad_residual, mods, item, after=()):
    shape = own.shape
    return slab_call(
        first_back_kernel,
        [own, peer, latent, grad_residual, mods],
        [
            whole(shape),
            whole(shape),
            pl.BlockSpec((None,) + shape, lambda i: (place_in, 0, 0)),
            whole(shape),
            mods_spec(mods, item),
        ],
        [],
        after,
        grid=(1,),
        out_specs=[whole(shape), whole((2, shape[1]))],
        out_shape=[struct(shape, F32), struct((2, shape[1]), F32)],
        cost_estimate=cost(30 * own.size, 20 * own.size),
    )


def split_rows(product_ref, send_ref, keep_ref):
    width = keep_ref.shape[1]
    core = lax.rem(lax.axis_index("fsdp"), 2)
    for high in range(keep_ref.shape[0]):
        theirs = pl.multiple_of((2 * high + 1 - core) * width, 8)
        mine = pl.multiple_of((2 * high + core) * width, 8)
        send_ref[high] = product_ref[pl.ds(theirs, width), :]
        keep_ref[high] = product_ref[pl.ds(mine, width), :]


def outer_kernel(right, left_ref, right_ref, send_ref, keep_ref, left_t, *product):
    @pl.when(pl.program_id(0) == 0)
    def _():
        left_t[...] = left_ref[...].T

    if product:
        product[0][...] = dot(left_t[...], right_ref[...], ((1,), (right,)))
        split_rows(product[0], send_ref, keep_ref)
        return
    width = keep_ref.shape[1]
    core = lax.rem(lax.axis_index("fsdp"), 2)
    for high in range(keep_ref.shape[0]):
        for out, which in ((send_ref, 1 - core), (keep_ref, core)):
            rows = pl.ds(pl.multiple_of((2 * high + which) * width, 8), width)
            out[high] = dot(left_t[rows, :], right_ref[...], ((1,), (right,)))


def outer(left, right, contract, tile, first, columns, helds, after=()):
    rows, model = left.shape
    size_f = lax.axis_size("fsdp")
    wide = right.shape[1 - contract]
    shape = (size_f // 2, model // size_f, columns)
    block = pl.BlockSpec(shape[:2] + (tile,), lambda j: (0, 0, j + first))
    right_spec = (
        pl.BlockSpec((rows, tile), lambda j: (0, j))
        if contract == 0
        else pl.BlockSpec((tile, rows), lambda j: (j, 0))
    )
    return slab_call(
        partial(outer_kernel, contract),
        [left, right],
        [whole(left.shape), right_spec],
        helds,
        after,
        grid=(wide // tile,),
        out_specs=[block] * 2,
        out_shape=[struct(shape, F32)] * 2,
        scratch_shapes=[pltpu.VMEM((model, rows), BF16)]
        + ([pltpu.VMEM((model, tile), F32)] if shape[1] % 16 else []),
        cost_estimate=cost(2 * rows * model * wide, 2 * rows * wide + 4 * model * wide),
    )


def long_outer_kernel(steps, left_ref, right_ref, send_ref, keep_ref, product):
    step = pl.program_id(0)
    term = dot(left_ref[...], right_ref[...], ((0,), (1,)))

    @pl.when(step == 0)
    def _():
        product[...] = term

    @pl.when(step > 0)
    def _():
        product[...] += term

    @pl.when(step == steps - 1)
    def _():
        split_rows(product, send_ref, keep_ref)


def long_outer(left, right, steps, after=()):
    rows, model = left.shape
    wide = right.shape[0]
    size_f = lax.axis_size("fsdp")
    shape = (size_f // 2, model // size_f, wide)
    return slab_call(
        partial(long_outer_kernel, steps),
        [left, right],
        [
            pl.BlockSpec((rows // steps, model), lambda j: (j, 0)),
            pl.BlockSpec((wide, rows // steps), lambda j: (0, j)),
        ],
        [],
        after,
        grid=(steps,),
        out_specs=[whole(shape)] * 2,
        out_shape=[struct(shape, F32)] * 2,
        scratch_shapes=[pltpu.VMEM((model, wide), F32)],
        cost_estimate=cost(2 * rows * model * wide, 2 * rows * (model + wide)),
    )


def order_kernel(count, *refs):
    out_ref = refs[-1]
    half = out_ref.shape[1] // 2
    items = out_ref.shape[0]
    t = lax.axis_index("tp")
    for rank, parts in ((t, refs[:count]), (1 - t, refs[count : 2 * count])):
        rows = pl.ds(pl.multiple_of(rank * half, half), half)
        for item in range(items):
            part = parts[0][item * half : (item + 1) * half, :] if count == 1 else parts[item][...]
            out_ref[item, rows, :] = part


def order(owns, peers, items, after=()):
    model = owns[0].shape[1]
    half = sum(own.shape[0] for own in owns) // items
    return slab_call(
        partial(order_kernel, len(owns)),
        [*owns, *peers],
        [whole(part.shape) for part in (*owns, *peers)],
        [],
        after,
        grid=(1,),
        out_specs=whole((items, 2 * half, model)),
        out_shape=struct((items, 2 * half, model), owns[0].dtype),
        cost_estimate=cost(0, 16 * items * half * model),
    )


def body(
    latents,
    condition,
    grad_out,
    ada_weight,
    ada_bias,
    qkv_weight,
    qv_bias,
    proj_weight,
    proj_bias,
    up_weight,
    up_bias,
    down_weight,
    down_bias,
):
    t = lax.axis_index("tp")
    c = lax.axis_index("ctx")
    f = lax.axis_index("fsdp")
    size_c = lax.axis_size("ctx")
    size_f = lax.axis_size("fsdp")
    micro, batch, here, model = latents.shape
    items = micro * batch
    half = here // 2
    half_width = qkv_weight.shape[2]
    group = half_width // size_c
    hidden = up_weight.shape[1]
    rows = qkv_weight.shape[0]
    first_column = t * half_width

    def swap(x, name):
        return flip(x, "tp", 0, name)

    def both(own, peer, axis):
        return jnp.where(
            t == 0,
            jnp.concatenate([own, peer], axis),
            jnp.concatenate([peer, own], axis),
        )

    qkv_groups = (
        qkv_weight.reshape(rows, 3, size_c, group)
        .transpose(2, 0, 1, 3)
        .reshape(size_c, rows, 3 * group)
    )
    qkv_came = exchange(qkv_groups, "qkv_c")

    flat_latents = latents.reshape(items, here, model)

    def swapped_ring(first, count, after=()):
        own, peer = halves(flat_latents, first, count, after)
        pairs = [own, peer]
        for piece in ring_gather(own, "latent%d" % first)[1:]:
            pairs += [piece, swap(piece, "latent%d_t" % first)]
        return pairs

    rings = [swapped_ring(0, 1)]

    cond = condition.reshape(items, model).astype(F32)
    silu_all = cube_gather(jax.nn.silu(cond).astype(BF16), "cond")
    first_row = (f * size_c + c) * rows
    silu_here = lax.dynamic_slice_in_dim(silu_all, first_row, rows, 2).reshape(-1, rows)
    silu_here = once_after(silu_here, [rings[0][2], rings[0][-2]])
    mod_part = dot(silu_here, ada_weight.reshape(rows, -1), ((1,), (0,)))
    mod_part = cube_reduce(mod_part.reshape(size_f, items, -1), "mod_f")
    mod_part = butterfly_sum(mod_part, "ctx", "mod_c")
    bias_mod = lax.dynamic_slice_in_dim(ada_bias.astype(F32), first_column, half_width, 1)
    mod_half = (mod_part.reshape(items, 6, half_width) + bias_mod).astype(BF16)
    mods = both(mod_half, swap(mod_half, "mod_t"), 2).astype(F32)
    mods = once_after(mods, [qkv_came])

    pieces = spread([(0, "own", qkv_came)], "qkv")
    (qkv_mine,) = place(pieces, [3 * group])
    bias_pair = lax.dynamic_slice_in_dim(
        qv_bias.astype(F32), first_column + c * group, group, 1
    )
    bias_mine = jnp.concatenate([bias_pair[0], jnp.zeros((group,), F32), bias_pair[1]])
    bias_mine = bias_mine.reshape(-1, 1)
    qkv_mine = qkv_mine.T

    in_first, qkv_t = project(rings[0], 0, mods, 0, items, qkv_mine, bias_mine, None)
    qkv_ts = [qkv_t]
    rings.append(swapped_ring(1, items - 1, [qkv_t]))
    latent = [(pairs[0], at) for pairs in rings for at in range(pairs[0].shape[0])]

    hop = [rings[1][2], rings[1][-2]]
    (proj_full,) = place(gather_stacked(once_after(proj_weight.T, hop), "proj"), [half_width])
    proj_full = proj_full.T
    feed_shard = jnp.concatenate([up_weight, down_weight.T], 1)
    feed_full = gather_rows(once_after(feed_shard, [mods]), "feed_weights")
    cots = halves(grad_out.reshape(items, here, model), 0, items)

    bias_proj = proj_bias.astype(F32).reshape(1, -1)
    bias_down = down_bias.astype(F32).reshape(1, -1)
    bias_up = lax.dynamic_slice_in_dim(up_bias.astype(F32), t * hidden, hidden, 0)
    bias_up = bias_up.reshape(1, -1)
    mixed = in_second = grad_feed = activated = grad_upward = None
    grad_attended = grad_qkv = out_own = out_peer = out_half = None

    kept = []
    for item in range(items):
        if item:
            in_first, qkv_t = project(
                rings[1], item - 1, mods, item, items, qkv_mine, bias_mine, in_first
            )
            qkv_ts.append(qkv_t)
        qkv_t = qkv_ts[item]
        outs, logs = attend(qkv_t, here)
        mixed, own, peer = back_to_rows(
            exchange(outs, "mixed%d" % item), proj_full, 0, True, mixed, item, items
        )
        attended, residual, in_half = second(
            own, swap(peer, "attended%d" % item), bias_proj, *latent[item], mods, item
        )
        in_peer = swap(in_half, "in_second%d" % item)
        kept.append((qkv_t, logs, attended, residual, in_half, in_peer))

    qkv_rows = once_after(qkv_groups.transpose(1, 0, 2).reshape(rows, -1), [kept[0][5]])
    qkv_full = gather_rows(qkv_rows, "qkv_weights")

    up_sums, grads_in, highs = [], [], []
    for item in range(items):
        _, _, _, _, in_half, in_peer = kept[item]
        (
            in_second,
            grad_feed,
            activated,
            grad_upward,
            out_own,
            out_peer,
            gin_own,
            gin_peer,
            up_sum,
            high,
        ) = feed(
            in_half,
            in_peer,
            cots,
            mods,
            feed_full,
            bias_up,
            (in_second, grad_feed, activated, grad_upward, out_own, out_peer),
            item,
            items,
            [grads_in[0][1]] if item == items - 1 else [],
        )
        grads_in.append((gin_own, swap(gin_peer, "grad_in_second%d" % item)))
        up_sums.append(up_sum)
        highs.append(high)

    def before_attention(item):
        _, _, attended, residual, _, _ = kept[item]
        grad_residual, low, sums_two = second_back(
            *grads_in[item], residual, attended, cots[0], mods, item
        )
        return grad_residual, low, sums_two, swap(low, "grad_attended%d" % item)

    bounds = highs[0]
    for high in highs[1:]:
        bounds = jnp.maximum(bounds, high)
    for axis in ("fsdp", "ctx"):
        bounds = butterfly_max(bounds, axis, "bounds")
    bounds = jnp.maximum(bounds[:, 0, 0], 1e-15)
    tokens = items * here * size_c * size_f
    up_scale = 32768.0 / (bounds[0] * bounds[3] * tokens)
    down_scale = 32768.0 / (bounds[1] * bounds[2] * tokens)
    scales = jnp.where(jnp.arange(2 * hidden) < hidden, up_scale, down_scale)
    middles = [before_attention(item) for item in range(items)]
    parts = outer(
        in_second, grad_upward, 0, 768, 0, 2 * hidden, [None, None], [grads_in[1][1]]
    )
    parts = outer(
        grad_feed, activated, 0, 768, hidden // 768, 2 * hidden, parts, [middles[0][3]]
    )
    feed_rows = reduce_rows(*parts, "grad_feed", scales)
    grad_feed_weights = ring_reduce(feed_rows, "grad_feed", scales)

    peers = swap(out_peer, "feed_out")
    gate_sums = []
    for item in range(items):
        out_half, gate_sum = finish(
            out_own, peers, bias_down, kept[item][3], cots[0], mods, out_half, item
        )
        gate_sums.append(gate_sum)
    output = order([out_half], [swap(out_half, "output")], items)

    grad_blocks = []
    for item in range(items):
        _, low, _, low_peer = middles[item]
        grad_attended, grad_mixed = grad_mixed_of(
            low, low_peer, proj_full, grad_attended, item, items
        )
        grad_blocks.append(
            exchange(grad_mixed.reshape(size_c, group, here), "grad_mixed%d" % item)
        )

    input_grads, input_peers, mod_terms = [], [], []
    for item in range(items):
        qkv_t, logs, _, _, _, _ = kept[item]
        grad_qkv, blocks = attend_back(
            qkv_t,
            grad_blocks[item],
            logs,
            grad_qkv,
            item,
            items,
            [parts[0]] if item == 0 else [],
        )
        own, peer = back_to_rows(
            exchange(blocks, "grad_qkv%d" % item),
            qkv_full,
            1,
            after=[feed_rows] if item == 1 else [],
        )
        grad_latent, sums_one = first_back(
            own,
            swap(peer, "grad_in_first%d" % item),
            *latent[item],
            middles[item][0],
            mods,
            item,
            input_peers[-1:],
        )
        input_grads.append(grad_latent)
        input_peers.append(swap(grad_latent, "grad_latent%d" % item))
        mod_terms.append(jnp.concatenate([sums_one, middles[item][2][:3], gate_sums[item]], 0))

    proj_parts = outer(grad_attended, mixed, 1, half_width, 0, half_width, [None, None])
    grad_proj = ring_reduce(reduce_rows(*proj_parts, "grad_proj"), "grad_proj").T
    grad_qkv = grad_qkv.reshape(3 * group, -1)
    qkv_rows = reduce_rows(*long_outer(in_first, grad_qkv, items), "grad_qkvw")
    grad_qkv_weight = (
        exchange(qkv_rows, "grad_qkvw_c")
        .reshape(size_c, rows, 3, group)
        .transpose(1, 2, 0, 3)
        .reshape(rows, 3, half_width)
    )

    down_sum = sum(
        jnp.sum(grad_feed[item * here : item * here + half].astype(F32), 0)
        for item in range(items)
    )
    qkv_sum = jnp.sum(grad_qkv.astype(F32), 1).reshape(3, group)
    pair_sum = jnp.stack([qkv_sum[0], qkv_sum[2]])
    up_total = lax.dynamic_update_slice_in_dim(
        jnp.zeros(up_bias.shape, F32), sum(up_sums)[0], t * hidden, 0
    )
    pair_total = lax.dynamic_update_slice_in_dim(
        jnp.zeros(qv_bias.shape, F32), pair_sum, first_column + c * group, 1
    )
    proj_sum = sum(middle[2][3] for middle in middles)
    sums = jnp.concatenate(
        [jnp.stack(mod_terms).reshape(-1), up_total, pair_total.reshape(-1), proj_sum, down_sum]
    ).reshape(-1, 128)
    sums = butterfly_sum(butterfly_sum(sums, "tp", "sums"), "ctx", "sums")
    sums = cube_gather(sums, "sums").reshape(size_f, -1)
    edge = items * 6 * model
    grad_mod_all = sums[:, :edge].astype(BF16).reshape(size_f, items, 6, model)
    ada_sum = tree_sum(jnp.sum(grad_mod_all.astype(F32), 1))
    bias_sum = tree_sum(sums[:, edge:])
    ends = [up_bias.shape[0], up_bias.shape[0] + qv_bias.size]

    mod_here = lax.dynamic_slice_in_dim(grad_mod_all, first_column, half_width, 3).reshape(
        size_f * items, -1
    )
    grad_ada = dot(silu_here, mod_here, ((0,), (0,))).reshape(rows, 6, half_width)
    cond_part = dot(mod_here, ada_weight.reshape(rows, -1), ((1,), (1,)))
    cond_part = lax.dynamic_update_slice_in_dim(
        jnp.zeros((size_f * items, model), F32), cond_part, first_row, 1
    ).reshape(size_f, items, model)
    cond_total = cube_reduce(cond_part, "grad_cond")
    for axis in ("ctx", "tp"):
        cond_total = butterfly_sum(cond_total, axis, "grad_cond")
    grad_cond = jax.vjp(jax.nn.silu, cond)[1](cond_total)[0]

    return (
        output.reshape(latents.shape),
        order(input_grads, input_peers, items).reshape(latents.shape),
        grad_cond.reshape(condition.shape),
        grad_ada,
        ada_sum,
        grad_qkv_weight,
        bias_sum[ends[0] : ends[1]].reshape(qv_bias.shape),
        grad_proj,
        bias_sum[ends[1] : ends[1] + model],
        grad_feed_weights[:, :hidden],
        bias_sum[: ends[0]],
        grad_feed_weights[:, hidden:].T,
        bias_sum[ends[1] + model :],
    )


def tree_sum(entries):
    while entries.shape[0] > 1:
        entries = entries[0::2] + entries[1::2]
    return entries[0]


def solution(mesh):
    in_specs = (
        P(None, "fsdp", "ctx", None),
        P(None, "fsdp", None),
        P(None, "fsdp", "ctx", None),
        P(("fsdp", "ctx"), None, "tp"),
        P(),
        P(("fsdp", "ctx"), None, "tp"),
        P(),
        P("tp", ("fsdp", "ctx")),
        P(),
        P(("fsdp", "ctx"), "tp"),
        P(),
        P("tp", ("fsdp", "ctx")),
        P(),
    )
    out_specs = (
        P(None, "fsdp", "ctx", None),
        P(None, "fsdp", "ctx", None),
        P(None, "fsdp", None),
        P(("fsdp", "ctx"), None, "tp"),
        P(),
        P(("fsdp", "ctx"), None, "tp"),
        P(),
        P("tp", ("fsdp", "ctx")),
        P(),
        P(("fsdp", "ctx"), "tp"),
        P(),
        P("tp", ("fsdp", "ctx")),
        P(),
    )
    return jax.shard_map(body, mesh=mesh, in_specs=in_specs, out_specs=out_specs, check_vma=False)
```

```python
from functools import partial

import jax
import jax.numpy as jnp
from jax import lax
from jax.experimental import pallas as pl
from jax.experimental.pallas import tpu as pltpu
from jax.sharding import PartitionSpec as P

HEADS = 16
HEAD_DIM = 72
LOG2E = 1.4426950408889634
F32 = jnp.float32
BF16 = jnp.bfloat16


def dot(a, b, dims):
    return lax.dot_general(a, b, (dims, ((), ())), preferred_element_type=F32)


def normalize(values):
    centre = values - jnp.mean(values, -1, keepdims=True)
    inverse = lax.rsqrt(jnp.mean(centre * centre, -1, keepdims=True) + 1e-06)
    return (centre * inverse, inverse)


def norm_back(incoming, normed, inverse):
    return inverse * (
        incoming
        - jnp.mean(incoming, -1, keepdims=True)
        - normed * jnp.mean(incoming * normed, -1, keepdims=True)
    )


def shift(x, k, name="shift"):
    size = lax.axis_size("ctx")
    with jax.named_scope(name):
        return lax.ppermute(x, "ctx", [(i, (i + k) % size) for i in range(size)])


def flip(x, axis, bit, name="flip"):
    size = lax.axis_size(axis)
    with jax.named_scope(name):
        return lax.ppermute(x, axis, [(i, i ^ (1 << bit)) for i in range(size)])


def exchange(x, name):
    with jax.named_scope(name):
        return lax.all_to_all(x, "ctx", 0, 0)


def gather_rows(x, name):
    with jax.named_scope(name):
        return lax.all_gather(x, ("fsdp", "ctx"), tiled=True)


def bits_of(axis):
    return lax.axis_size(axis).bit_length() - 1


def ring_gather(x, name, second=lambda x: x):
    size = lax.axis_size("ctx")
    blocks = [x] * size
    moving = x
    for step in range(1, size // 2 + 1):
        moving = shift(second(moving) if step == 2 else moving, 1, name + "_right")
        blocks[step] = moving
    moving = x
    for step in range(1, (size - 1) // 2 + 1):
        moving = shift(moving, -1, name + "_left")
        blocks[size - step] = moving
    return blocks


def butterfly_sum(x, axis, name):
    for bit in range(bits_of(axis)):
        x = x + flip(x, axis, bit, name)
    return x


def butterfly_max(x, axis, name):
    for bit in range(bits_of(axis)):
        x = jnp.maximum(x, flip(x, axis, bit, name))
    return x


def cube_gather(x, name):
    x = x[None]
    for bit in range(bits_of("fsdp")):
        x = jnp.concatenate([x, flip(x, "fsdp", bit, name)], 0)
    return x


def cube_reduce(x, name):
    for bit in reversed(range(bits_of("fsdp"))):
        half = x.shape[0] // 2
        x = x[:half] + flip(x[half:], "fsdp", bit, name)
    return x[0]


def spread(pieces, name):
    for bit in reversed(range(bits_of("fsdp"))):
        pieces = pieces + [
            (offset ^ (1 << bit), places, flip(block, "fsdp", bit, name + "_%d" % bit))
            for offset, places, block in pieces
        ]
    return pieces


def gather_stacked(shard, name):
    blocks = ring_gather(shard, name)
    return spread([(0, "before", jnp.stack(blocks))], name)


def place_kernel(targets, widths, *refs):
    count = len(targets)
    ins, outs = refs[:count], refs[-3 - len(widths) : -3]
    held, in_sem, out_sem = refs[-3:]
    own_f = lax.axis_index("fsdp")
    own_c = lax.axis_index("ctx")
    size_c = lax.axis_size("ctx")
    arriving, leaving = [], []
    for (offset, places), ref in zip(targets, ins):
        row = jnp.bitwise_xor(own_f, offset)
        for at in range(size_c):
            column = at if places == "own" else lax.rem(own_c + size_c - at, size_c)
            slot = len(arriving)
            arriving.append(pltpu.make_async_copy(ref.at[at], held.at[slot], in_sem.at[slot]))
            first = 0
            for width, out in zip(widths, outs):
                leaving.append(
                    pltpu.make_async_copy(
                        held.at[slot, :, pl.ds(first, width)],
                        out.at[row, column],
                        out_sem.at[len(leaving)],
                    )
                )
                first += width
    for copy in arriving:
        copy.start()
    each = len(widths)
    for slot, copy in enumerate(arriving):
        copy.wait()
        for out_copy in leaving[slot * each : (slot + 1) * each]:
            out_copy.start()
    for copy in leaving:
        copy.wait()


def place(pieces, widths, after=()):
    size_f, size_c = lax.axis_size("fsdp"), lax.axis_size("ctx")
    rows, total = pieces[0][2].shape[1:]
    count = size_f * size_c
    outs = pl.pallas_call(
        partial(place_kernel, [piece[:2] for piece in pieces], widths),
        out_shape=[jax.ShapeDtypeStruct((size_f, size_c, rows, width), BF16) for width in widths],
        in_specs=[ANYWHERE] * (len(pieces) + len(after)),
        out_specs=[ANYWHERE] * len(widths),
        scratch_shapes=[
            pltpu.VMEM((count, rows, total), BF16),
            pltpu.SemaphoreType.DMA((count,)),
            pltpu.SemaphoreType.DMA((count * len(widths),)),
        ],
        compiler_params=pltpu.CompilerParams(vmem_limit_bytes=40 << 20),
        cost_estimate=pl.CostEstimate(
            flops=0, bytes_accessed=4 * count * rows * total, transcendentals=0
        ),
    )(*[piece[2] for piece in pieces], *after)
    return [out.reshape(-1, width) for out, width in zip(outs, widths)]


def lower(x, scale):
    return x if scale is None else (x * scale).astype(jnp.float16)


def higher(x, scale):
    return x if scale is None else x.astype(F32) * (1.0 / scale)


def reduce_rows(send, keep, name, scale=None):
    size_c = lax.axis_size("ctx")
    own_f = lax.axis_index("fsdp")
    _, width, columns = keep.shape
    parts = [keep, flip(send, "fsdp", 0, name + "_0")]
    for bit in range(1, bits_of("fsdp")):
        own_bit = (own_f >> bit) % 2
        pairs = [part.reshape(-1, 2, width, columns) for part in parts]
        got = sum(lax.dynamic_index_in_dim(pair, 1 - own_bit, 1, False) for pair in pairs)
        got = flip(lower(got, scale), "fsdp", bit, name + "_%d" % bit)
        parts = [lax.dynamic_index_in_dim(pair, own_bit, 1, False) for pair in pairs]
        parts.append(higher(got, scale))
    return sum(parts).reshape(size_c, width // size_c, columns)


def ring_reduce(blocks, name, scale=None):
    size = lax.axis_size("ctx")
    own = lax.axis_index("ctx")

    def block(offset):
        return lax.dynamic_index_in_dim(blocks, (own + offset) % size, 0, False)

    total = block(0)
    hops = []
    for sign, reach in ((1, size // 2), (-1, (size - 1) // 2)):
        moving = None
        for distance in range(reach, 0, -1):
            term = block(sign * distance)
            if moving is not None:
                term = term + moving
            hops.append(shift(lower(term, scale), sign, name + "_ring"))
            moving = higher(hops[-1], scale)
        if moving is not None:
            total = total + moving
    return total, hops


def whole(shape):
    return pl.BlockSpec(tuple(shape), lambda *_: (0,) * len(shape))


def struct(shape, dtype):
    return jax.ShapeDtypeStruct(tuple(shape), dtype)


ANYWHERE = pl.BlockSpec(memory_space=pltpu.HBM)
PARAMS = pltpu.CompilerParams(vmem_limit_bytes=48 << 20)


def cost(flops, nbytes, exps=0):
    return pl.CostEstimate(flops=int(flops), bytes_accessed=int(nbytes), transcendentals=int(exps))


def mods_spec(mods, item):
    return pl.BlockSpec((None,) + mods.shape[1:], lambda *_: (item, 0, 0))


def largest(x):
    return jnp.full((8, 128), jnp.max(jnp.abs(x)), F32)


def slab_call(kernel, args, in_specs, helds, after=(), **options):
    taken = [held for held in helds if held is not None]
    count = len(args)
    more = len(taken) + len(after)

    def run(*refs):
        kernel(*refs[:count], *refs[count + more :])

    return pl.pallas_call(
        run,
        in_specs=in_specs + [ANYWHERE] * more,
        input_output_aliases={count + at: at for at in range(len(taken))},
        compiler_params=PARAMS,
        **options,
    )(*args, *taken, *after)


def halves_kernel(first, both_ref, own_ref, peer_ref):
    count, half, _ = own_ref.shape
    t = lax.axis_index("tp")
    for rank, out in ((t, own_ref), (1 - t, peer_ref)):
        rows = pl.ds(pl.multiple_of(rank * half, half), half)
        for at in range(count):
            out[at] = both_ref[first + at, rows, :]


def halves(x, first, count, after=()):
    items, here, model = x.shape
    shape = (count, here // 2, model)
    return slab_call(
        partial(halves_kernel, first),
        [x],
        [whole(x.shape)],
        [],
        after,
        grid=(1,),
        out_specs=[whole(shape)] * 2,
        out_shape=[struct(shape, x.dtype)] * 2,
        cost_estimate=cost(0, 4 * count * here * model),
    )


def wait_kernel(in_ref, out_ref):
    out_ref[...] = in_ref[...]


def once_after(x, after):
    return slab_call(
        wait_kernel,
        [x],
        [whole(x.shape)],
        [],
        after,
        grid=(1,),
        out_specs=whole(x.shape),
        out_shape=struct(x.shape, x.dtype),
        cost_estimate=cost(0, 4 * x.size),
    )


def project_kernel(count, *refs):
    pieces = refs[:count]
    mods_ref, weight_ref, bias_ref, in_ref, out_ref = refs[count:]
    for pair in range(count // 2):
        rows = jnp.concatenate([pieces[2 * pair][...], pieces[2 * pair + 1][...]], 0)
        here = rows.shape[0]
        normed, _ = normalize(rows.astype(F32))
        in_first = (normed * (1.0 + mods_ref[1:2, :]) + mods_ref[0:1, :]).astype(BF16)
        in_ref[pl.ds(pair * here, here), :] = in_first
        product = dot(weight_ref[...], in_first, ((1,), (1,))) + bias_ref[...]
        out_ref[:, pl.ds(pair * here, here)] = product.astype(BF16)


def project(pieces, place_in, mods, item, items, weight_t, bias, held, after=()):
    _, half, model = pieces[0].shape
    total = half * len(pieces)
    piece_spec = pl.BlockSpec((None, half, model), lambda i: (place_in, 0, 0))
    width = weight_t.shape[0]
    return slab_call(
        partial(project_kernel, len(pieces)),
        [*pieces, mods, weight_t, bias],
        [piece_spec] * len(pieces)
        + [mods_spec(mods, item), whole(weight_t.shape), whole(bias.shape)],
        [held],
        after,
        grid=(1,),
        out_specs=[
            pl.BlockSpec((total, model), lambda i: (item, 0)),
            whole((width, total)),
        ],
        out_shape=[struct((items * total, model), BF16), struct((width, total), BF16)],
        cost_estimate=cost(2 * total * model * width, 6 * total * model),
    )


def head_rows(values, head):
    values = values.astype(F32)
    row = lax.broadcasted_iota(jnp.int32, values.shape, 0)
    inside = (row >= head * HEAD_DIM) & (row < (head + 1) * HEAD_DIM)
    return jnp.where(inside, values, 0.0).astype(BF16), inside


def attend_kernel(heads, steps, q_ref, kt_ref, vt_ref, out_ref, log_ref, k_ref):
    step = pl.program_id(0)
    factor = HEAD_DIM ** (-0.5) * LOG2E

    @pl.when(step == 0)
    def _():
        k_ref[...] = kt_ref[...].T

    total = None
    for head in range(heads):
        q_head, inside = head_rows(q_ref[...], head)
        scores = dot(k_ref[...], q_head, ((1,), (0,)))
        highest = jnp.max(scores, 0, keepdims=True)
        exponent = jnp.exp2((scores - highest) * factor)
        summed = jnp.sum(exponent, 0, keepdims=True)
        chances = (exponent * (1.0 / summed)).astype(BF16)
        mixed = dot(vt_ref[...], chances, ((1,), (0,)))
        total = mixed if total is None else jnp.where(inside, mixed, total)
        log_ref[pl.ds(head, 1), :] = highest * factor + jnp.log2(summed)
    out_ref[lax.rem(lax.axis_index("ctx") + steps - step, steps)] = total.astype(BF16)


def attend(qkv_t, here, after=()):
    group, total = qkv_t.shape[0] // 3, qkv_t.shape[1]
    heads, steps = group // HEAD_DIM, total // here
    thirds = qkv_t.reshape(3, group, total)
    return slab_call(
        partial(attend_kernel, heads, steps),
        [thirds, thirds, thirds],
        [
            pl.BlockSpec((None, group, here), lambda i: (0, 0, i)),
            pl.BlockSpec((None, group, total), lambda i: (1, 0, 0)),
            pl.BlockSpec((None, group, total), lambda i: (2, 0, 0)),
        ],
        [],
        after,
        grid=(steps,),
        out_specs=[
            whole((steps, group, here)),
            pl.BlockSpec((heads, here), lambda i: (0, i)),
        ],
        out_shape=[struct((steps, group, here), BF16), struct((heads, total), F32)],
        scratch_shapes=[pltpu.VMEM((total, group), BF16)],
        cost_estimate=cost(heads * total * total * 1600, 8 * group * total, heads * total * total),
    )


def attend_back_kernel(
    heads,
    steps,
    q_ref,
    kt_ref,
    vt_ref,
    log_ref,
    grad_ref,
    all_ref,
    out_ref,
    k_ref,
    v_ref,
    dk_ref,
    dv_ref,
):
    step = pl.program_id(0)
    own_c = lax.axis_index("ctx")
    scaling = HEAD_DIM ** (-0.5)
    group, block = q_ref.shape

    @pl.when(step == 0)
    def _():
        dk_ref[...] = jnp.zeros_like(dk_ref)
        dv_ref[...] = jnp.zeros_like(dv_ref)
        k_ref[...] = kt_ref[...].T
        v_ref[...] = vt_ref[...].T

    grad = grad_ref[lax.rem(own_c + steps - step, steps)]
    grad_query = None
    for head in range(heads):
        q_head, inside = head_rows(q_ref[...], head)
        do_head, _ = head_rows(grad, head)
        scores = dot(k_ref[...], q_head, ((1,), (0,)))
        chances = jnp.exp2(scores * (scaling * LOG2E) - log_ref[pl.ds(head, 1), :])
        grad_chances = dot(v_ref[...], do_head, ((1,), (0,)))
        weighted = jnp.sum(chances * grad_chances, 0, keepdims=True)
        grad_scores = (chances * (grad_chances - weighted)).astype(BF16)
        term = dot(kt_ref[...], grad_scores, ((1,), (0,)))
        grad_query = term if grad_query is None else jnp.where(inside, term, grad_query)
        dk_ref[...] += dot(q_head, grad_scores, ((1,), (1,)))
        dv_ref[...] += dot(do_head, chances.astype(BF16), ((1,), (1,)))
    columns = pl.ds(pl.multiple_of(step * block, block), block)
    all_ref[0, :, columns] = (grad_query * scaling).astype(BF16)

    @pl.when(step == steps - 1)
    def _():
        all_ref[1] = (dk_ref[...] * scaling).astype(BF16)
        all_ref[2] = dv_ref[...].astype(BF16)
        for at in range(steps):
            out_ref[lax.rem(own_c + steps - at, steps)] = all_ref[
                :, :, at * block : (at + 1) * block
            ]


def attend_back(qkv_t, grads, logs, held, item, items, after=()):
    group, total = qkv_t.shape[0] // 3, qkv_t.shape[1]
    heads, steps = group // HEAD_DIM, grads.shape[0]
    here = total // steps
    thirds = qkv_t.reshape(3, group, total)
    return slab_call(
        partial(attend_back_kernel, heads, steps),
        [thirds, thirds, thirds, logs, grads],
        [
            pl.BlockSpec((None, group, here), lambda i: (0, 0, i)),
            pl.BlockSpec((None, group, total), lambda i: (1, 0, 0)),
            pl.BlockSpec((None, group, total), lambda i: (2, 0, 0)),
            pl.BlockSpec((heads, here), lambda i: (0, i)),
            whole(grads.shape),
        ],
        [held],
        after,
        grid=(steps,),
        out_specs=[
            pl.BlockSpec((3, group, total), lambda i: (0, 0, item)),
            whole((steps, 3, group, here)),
        ],
        out_shape=[
            struct((3, group, items * total), BF16),
            struct((steps, 3, group, here), BF16),
        ],
        scratch_shapes=[
            pltpu.VMEM((total, group), BF16),
            pltpu.VMEM((total, group), BF16),
            pltpu.VMEM((group, total), F32),
            pltpu.VMEM((group, total), F32),
        ],
        cost_estimate=cost(heads * total * total * 4000, 16 * group * total, heads * total * total),
    )


def back_to_rows_kernel(contract, keep, blocks_ref, weight_ref, *outs):
    own_ref, peer_ref = outs[-2:]
    rows = blocks_ref[...].reshape(-1, blocks_ref.shape[-1])
    if keep:
        outs[0][...] = rows
    total = dot(rows, weight_ref[...], ((0,), (contract,)))
    half = own_ref.shape[0]
    own_ref[...] = total[:half]
    peer_ref[...] = total[half:]


def back_to_rows(blocks, weight, contract, keep=False, held=None, item=0, items=1, after=()):
    here = blocks.shape[-1]
    features, model = weight.shape[contract], weight.shape[1 - contract]
    half = here // 2
    out_specs = [whole((half, model))] * 2
    out_shape = [struct((half, model), F32)] * 2
    if keep:
        out_specs = [pl.BlockSpec((features, here), lambda i: (0, item))] + out_specs
        out_shape = [struct((features, items * here), BF16)] + out_shape
    return slab_call(
        partial(back_to_rows_kernel, contract, keep),
        [blocks, weight],
        [whole(blocks.shape), whole(weight.shape)],
        [held],
        after,
        grid=(1,),
        out_specs=out_specs,
        out_shape=out_shape,
        cost_estimate=cost(
            2 * here * features * model, 2 * features * model + 8 * here * model
        ),
    )


def second_kernel(own_ref, peer_ref, bias_ref, latent_ref, mods_ref, att_ref, res_ref, in_ref):
    attended = own_ref[...] + peer_ref[...] + bias_ref[...]
    residual = latent_ref[...].astype(F32) + mods_ref[2:3, :] * attended
    normed, _ = normalize(residual)
    att_ref[...] = attended
    res_ref[...] = residual
    in_ref[...] = (normed * (1.0 + mods_ref[4:5, :]) + mods_ref[3:4, :]).astype(BF16)


def second(own, peer, bias, latent, place_in, mods, item, after=()):
    shape = own.shape
    return slab_call(
        second_kernel,
        [own, peer, bias, latent, mods],
        [
            whole(shape),
            whole(shape),
            whole(bias.shape),
            pl.BlockSpec((None,) + shape, lambda i: (place_in, 0, 0)),
            mods_spec(mods, item),
        ],
        [],
        after,
        grid=(1,),
        out_specs=[whole(shape)] * 3,
        out_shape=[struct(shape, F32), struct(shape, F32), struct(shape, BF16)],
        cost_estimate=cost(20 * own.size, 20 * own.size),
    )


def feed_kernel(
    steps,
    own_ref,
    peer_ref,
    cot_own,
    cot_peer,
    mods_ref,
    up_ref,
    down_ref,
    bias_ref,
    in_all,
    grad_all,
    act_ref,
    gup_ref,
    out_own,
    out_peer,
    gin_own,
    gin_peer,
    sum_ref,
    highs,
    in_ref,
    grad_ref,
    out_acc,
    gin_acc,
):
    step = pl.program_id(0)
    half = own_ref.shape[0]

    @pl.when(step == 0)
    def _():
        in_ref[:half, :] = own_ref[...]
        in_ref[half:, :] = peer_ref[...]
        in_all[...] = in_ref[...]
        gate = mods_ref[5:6, :]
        grad_ref[:half, :] = (cot_own[...].astype(F32) * gate).astype(BF16)
        grad_ref[half:, :] = (cot_peer[...].astype(F32) * gate).astype(BF16)
        grad_all[...] = grad_ref[...]
        highs[0] = largest(in_ref[...].astype(F32))
        highs[1] = largest(grad_ref[...].astype(F32))
        highs[2] = jnp.zeros((8, 128), F32)
        highs[3] = jnp.zeros((8, 128), F32)

    upward = dot(in_ref[...], up_ref[...], ((1,), (0,))) + bias_ref[...]
    grad_act = dot(grad_ref[...], down_ref[...], ((1,), (0,)))
    inner = 0.7978845608028654
    squared = upward * upward
    curve = jnp.tanh(inner * upward * (1.0 + 0.044715 * squared))
    activated = (0.5 * upward * (1.0 + curve)).astype(BF16)
    slope = 0.5 * (1.0 + curve) + (0.5 * inner) * upward * (1.0 - curve * curve) * (
        1.0 + (3.0 * 0.044715) * squared
    )
    grad_up = (slope * grad_act).astype(BF16)
    act_ref[...] = activated
    gup_ref[...] = grad_up
    wide = grad_up.astype(F32)
    sum_ref[...] = jnp.sum(wide, 0, keepdims=True)
    highs[2] = jnp.maximum(highs[2], largest(activated.astype(F32)))
    highs[3] = jnp.maximum(highs[3], largest(wide))
    out_term = dot(activated, down_ref[...], ((1,), (1,)))
    gin_term = dot(grad_up, up_ref[...], ((1,), (1,)))

    @pl.when(step == 0)
    def _():
        out_acc[...] = out_term
        gin_acc[...] = gin_term

    @pl.when(step > 0)
    def _():
        out_acc[...] += out_term
        gin_acc[...] += gin_term

    @pl.when(step == steps - 1)
    def _():
        out_own[...] = out_acc[:half, :]
        out_peer[...] = out_acc[half:, :].astype(BF16)
        gin_own[...] = gin_acc[:half, :]
        gin_peer[...] = gin_acc[half:, :]


def feed(own, peer, cots, mods, weights, bias, helds, item, items, after=()):
    half, model = own.shape
    here, hidden = 2 * half, weights.shape[1] // 2
    cot = pl.BlockSpec((None, half, model), lambda j: (item, 0, 0))
    tile = 768
    steps = hidden // tile
    rows = pl.BlockSpec((here, model), lambda j: (item, 0))
    slab = pl.BlockSpec((here, tile), lambda j: (item, j))
    return slab_call(
        partial(feed_kernel, steps),
        [own, peer, *cots, mods, weights, weights, bias],
        [whole(own.shape)] * 2
        + [cot] * 2
        + [
            mods_spec(mods, item),
            pl.BlockSpec((model, tile), lambda j: (0, j)),
            pl.BlockSpec((model, tile), lambda j: (0, j + steps)),
            pl.BlockSpec((1, tile), lambda j: (0, j)),
        ],
        helds,
        after,
        grid=(steps,),
        out_specs=[rows, rows, slab, slab]
        + [pl.BlockSpec((half, model), lambda j: (item, 0))] * 2
        + [whole(own.shape)] * 2
        + [pl.BlockSpec((1, tile), lambda j: (0, j)), whole((4, 8, 128))],
        out_shape=[
            struct((items * here, model), BF16),
            struct((items * here, model), BF16),
            struct((items * here, hidden), BF16),
            struct((items * here, hidden), BF16),
            struct((items * half, model), F32),
            struct((items * half, model), BF16),
            struct(own.shape, F32),
            struct(own.shape, F32),
            struct((1, hidden), F32),
            struct((4, 8, 128), F32),
        ],
        scratch_shapes=[
            pltpu.VMEM((here, model), BF16),
            pltpu.VMEM((here, model), BF16),
            pltpu.VMEM((here, model), F32),
            pltpu.VMEM((here, model), F32),
        ],
        cost_estimate=cost(8 * here * model * hidden, 4 * model * hidden + 4 * here * hidden),
    )


def finish_kernel(own_ref, peer_ref, bias_ref, res_ref, cot_ref, mods_ref, out_ref, sum_ref):
    feed_out = own_ref[...] + peer_ref[...].astype(F32) + bias_ref[...]
    out_ref[...] = (res_ref[...] + mods_ref[5:6, :] * feed_out).astype(BF16)
    sum_ref[...] = jnp.sum(cot_ref[...].astype(F32) * feed_out, 0, keepdims=True)


def finish(own, peer, bias, residual, cots, mods, held, item, after=()):
    items, half, model = cots.shape
    part = pl.BlockSpec((half, model), lambda i: (item, 0))
    return slab_call(
        finish_kernel,
        [own, peer, bias, residual, cots, mods],
        [
            part,
            part,
            whole(bias.shape),
            whole((half, model)),
            pl.BlockSpec((None, half, model), lambda i: (item, 0, 0)),
            mods_spec(mods, item),
        ],
        [held],
        after,
        grid=(1,),
        out_specs=[part, whole(bias.shape)],
        out_shape=[struct((items * half, model), BF16), struct(bias.shape, F32)],
        cost_estimate=cost(8 * half * model, 16 * half * model),
    )


def second_back_kernel(
    own_ref, peer_ref, res_ref, att_ref, cot_ref, mods_ref, grad_ref, low_ref, sum_ref
):
    incoming = own_ref[...] + peer_ref[...]
    normed, inverse = normalize(res_ref[...])
    grad = cot_ref[...].astype(F32) + norm_back(
        incoming * (1.0 + mods_ref[4:5, :]), normed, inverse
    )
    low = (grad * mods_ref[2:3, :]).astype(BF16)
    grad_ref[...] = grad
    low_ref[...] = low
    sum_ref[0:1, :] = jnp.sum(grad * att_ref[...], 0, keepdims=True)
    sum_ref[1:2, :] = jnp.sum(incoming, 0, keepdims=True)
    sum_ref[2:3, :] = jnp.sum(incoming * normed, 0, keepdims=True)
    sum_ref[3:4, :] = jnp.sum(low.astype(F32), 0, keepdims=True)


def second_back(own, peer, residual, attended, cots, mods, item, after=()):
    shape = own.shape
    return slab_call(
        second_back_kernel,
        [own, peer, residual, attended, cots, mods],
        [whole(shape)] * 4
        + [pl.BlockSpec((None,) + shape, lambda i: (item, 0, 0)), mods_spec(mods, item)],
        [],
        after,
        grid=(1,),
        out_specs=[whole(shape), whole(shape), whole((4, shape[1]))],
        out_shape=[struct(shape, F32), struct(shape, BF16), struct((4, shape[1]), F32)],
        cost_estimate=cost(30 * own.size, 24 * own.size),
    )


def grad_mixed_kernel(own_ref, peer_ref, weight_ref, all_ref, out_ref):
    rows = jnp.concatenate([own_ref[...], peer_ref[...]], 0)
    all_ref[...] = rows
    out_ref[...] = dot(weight_ref[...], rows, ((1,), (1,))).astype(BF16)


def grad_mixed_of(own, peer, weight, held, item, items, after=()):
    features, model = weight.shape
    here = 2 * own.shape[0]
    return slab_call(
        grad_mixed_kernel,
        [own, peer, weight],
        [whole(own.shape), whole(own.shape), whole(weight.shape)],
        [held],
        after,
        grid=(1,),
        out_specs=[
            pl.BlockSpec((here, model), lambda i: (item, 0)),
            whole((features, here)),
        ],
        out_shape=[struct((items * here, model), BF16), struct((features, here), BF16)],
        cost_estimate=cost(2 * here * features * model, 2 * features * model),
    )


def first_back_kernel(own_ref, peer_ref, latent_ref, res_ref, mods_ref, grad_ref, sum_ref):
    incoming = own_ref[...] + peer_ref[...]
    normed, inverse = normalize(latent_ref[...].astype(F32))
    grad_ref[...] = res_ref[...] + norm_back(
        incoming * (1.0 + mods_ref[1:2, :]), normed, inverse
    )
    sum_ref[0:1, :] = jnp.sum(incoming, 0, keepdims=True)
    sum_ref[1:2, :] = jnp.sum(incoming * normed, 0, keepdims=True)


def first_back(own, peer, latent, place_in, grad_residual, mods, item, after=()):
    shape = own.shape
    return slab_call(
        first_back_kernel,
        [own, peer, latent, grad_residual, mods],
        [
            whole(shape),
            whole(shape),
            pl.BlockSpec((None,) + shape, lambda i: (place_in, 0, 0)),
            whole(shape),
            mods_spec(mods, item),
        ],
        [],
        after,
        grid=(1,),
        out_specs=[whole(shape), whole((2, shape[1]))],
        out_shape=[struct(shape, F32), struct((2, shape[1]), F32)],
        cost_estimate=cost(30 * own.size, 20 * own.size),
    )


def split_rows(product_ref, send_ref, keep_ref):
    width = keep_ref.shape[1]
    core = lax.rem(lax.axis_index("fsdp"), 2)
    for high in range(keep_ref.shape[0]):
        theirs = pl.multiple_of((2 * high + 1 - core) * width, 8)
        mine = pl.multiple_of((2 * high + core) * width, 8)
        send_ref[high] = product_ref[pl.ds(theirs, width), :]
        keep_ref[high] = product_ref[pl.ds(mine, width), :]


def outer_kernel(right, left_ref, right_ref, send_ref, keep_ref, left_t, *product):
    @pl.when(pl.program_id(0) == 0)
    def _():
        left_t[...] = left_ref[...].T

    if product:
        product[0][...] = dot(left_t[...], right_ref[...], ((1,), (right,)))
        split_rows(product[0], send_ref, keep_ref)
        return
    width = keep_ref.shape[1]
    core = lax.rem(lax.axis_index("fsdp"), 2)
    for high in range(keep_ref.shape[0]):
        for out, which in ((send_ref, 1 - core), (keep_ref, core)):
            rows = pl.ds(pl.multiple_of((2 * high + which) * width, 8), width)
            out[high] = dot(left_t[rows, :], right_ref[...], ((1,), (right,)))


def outer(left, right, contract, tile, first, columns, helds, after=()):
    rows, model = left.shape
    size_f = lax.axis_size("fsdp")
    wide = right.shape[1 - contract]
    shape = (size_f // 2, model // size_f, columns)
    block = pl.BlockSpec(shape[:2] + (tile,), lambda j: (0, 0, j + first))
    right_spec = (
        pl.BlockSpec((rows, tile), lambda j: (0, j))
        if contract == 0
        else pl.BlockSpec((tile, rows), lambda j: (j, 0))
    )
    return slab_call(
        partial(outer_kernel, contract),
        [left, right],
        [whole(left.shape), right_spec],
        helds,
        after,
        grid=(wide // tile,),
        out_specs=[block] * 2,
        out_shape=[struct(shape, F32)] * 2,
        scratch_shapes=[pltpu.VMEM((model, rows), BF16)]
        + ([pltpu.VMEM((model, tile), F32)] if shape[1] % 16 else []),
        cost_estimate=cost(2 * rows * model * wide, 2 * rows * wide + 4 * model * wide),
    )


def long_outer_kernel(steps, left_ref, right_ref, send_ref, keep_ref, product):
    step = pl.program_id(0)
    term = dot(left_ref[...], right_ref[...], ((0,), (1,)))

    @pl.when(step == 0)
    def _():
        product[...] = term

    @pl.when(step > 0)
    def _():
        product[...] += term

    @pl.when(step == steps - 1)
    def _():
        split_rows(product, send_ref, keep_ref)


def long_outer(left, right, steps, after=()):
    rows, model = left.shape
    wide = right.shape[0]
    size_f = lax.axis_size("fsdp")
    shape = (size_f // 2, model // size_f, wide)
    return slab_call(
        partial(long_outer_kernel, steps),
        [left, right],
        [
            pl.BlockSpec((rows // steps, model), lambda j: (j, 0)),
            pl.BlockSpec((wide, rows // steps), lambda j: (0, j)),
        ],
        [],
        after,
        grid=(steps,),
        out_specs=[whole(shape)] * 2,
        out_shape=[struct(shape, F32)] * 2,
        scratch_shapes=[pltpu.VMEM((model, wide), F32)],
        cost_estimate=cost(2 * rows * model * wide, 2 * rows * (model + wide)),
    )


def order_kernel(count, *refs):
    out_ref = refs[-1]
    half = out_ref.shape[1] // 2
    items = out_ref.shape[0]
    t = lax.axis_index("tp")
    for rank, parts in ((t, refs[:count]), (1 - t, refs[count : 2 * count])):
        rows = pl.ds(pl.multiple_of(rank * half, half), half)
        for item in range(items):
            part = parts[0][item * half : (item + 1) * half, :] if count == 1 else parts[item][...]
            out_ref[item, rows, :] = part


def order(owns, peers, items, after=()):
    model = owns[0].shape[1]
    half = sum(own.shape[0] for own in owns) // items
    return slab_call(
        partial(order_kernel, len(owns)),
        [*owns, *peers],
        [whole(part.shape) for part in (*owns, *peers)],
        [],
        after,
        grid=(1,),
        out_specs=whole((items, 2 * half, model)),
        out_shape=struct((items, 2 * half, model), owns[0].dtype),
        cost_estimate=cost(0, 16 * items * half * model),
    )


def body(
    latents,
    condition,
    grad_out,
    ada_weight,
    ada_bias,
    qkv_weight,
    qv_bias,
    proj_weight,
    proj_bias,
    up_weight,
    up_bias,
    down_weight,
    down_bias,
):
    t = lax.axis_index("tp")
    c = lax.axis_index("ctx")
    f = lax.axis_index("fsdp")
    size_c = lax.axis_size("ctx")
    size_f = lax.axis_size("fsdp")
    micro, batch, here, model = latents.shape
    items = micro * batch
    half = here // 2
    half_width = qkv_weight.shape[2]
    group = half_width // size_c
    hidden = up_weight.shape[1]
    rows = qkv_weight.shape[0]
    first_column = t * half_width

    def swap(x, name):
        return flip(x, "tp", 0, name)

    def both(own, peer, axis):
        return jnp.where(
            t == 0,
            jnp.concatenate([own, peer], axis),
            jnp.concatenate([peer, own], axis),
        )

    qkv_groups = (
        qkv_weight.reshape(rows, 3, size_c, group)
        .transpose(2, 0, 1, 3)
        .reshape(size_c, rows, 3 * group)
    )
    qkv_came = exchange(qkv_groups, "qkv_c")

    flat_latents = latents.reshape(items, here, model)

    def swapped_ring(first, count, after=(), second=lambda x: x):
        own, peer = halves(flat_latents, first, count, after)
        pairs = [own, peer]
        for piece in ring_gather(own, "latent%d" % first, second)[1:]:
            pairs += [piece, swap(piece, "latent%d_t" % first)]
        return pairs

    rings = [swapped_ring(0, 1)]

    cond = condition.reshape(items, model).astype(F32)
    silu_all = cube_gather(jax.nn.silu(cond).astype(BF16), "cond")
    first_row = (f * size_c + c) * rows
    silu_here = lax.dynamic_slice_in_dim(silu_all, first_row, rows, 2).reshape(-1, rows)
    silu_here = once_after(silu_here, [rings[0][2], rings[0][-2]])
    mod_part = dot(silu_here, ada_weight.reshape(rows, -1), ((1,), (0,)))
    mod_part = cube_reduce(mod_part.reshape(size_f, items, -1), "mod_f")
    mod_part = butterfly_sum(mod_part, "ctx", "mod_c")
    bias_mod = lax.dynamic_slice_in_dim(ada_bias.astype(F32), first_column, half_width, 1)
    mod_half = (mod_part.reshape(items, 6, half_width) + bias_mod).astype(BF16)
    mods = both(mod_half, swap(mod_half, "mod_t"), 2).astype(F32)
    mods = once_after(mods, [qkv_came])

    pieces = spread([(0, "own", qkv_came)], "qkv")
    (qkv_mine,) = place(pieces, [3 * group])
    bias_pair = lax.dynamic_slice_in_dim(
        qv_bias.astype(F32), first_column + c * group, group, 1
    )
    bias_mine = jnp.concatenate([bias_pair[0], jnp.zeros((group,), F32), bias_pair[1]])
    bias_mine = bias_mine.reshape(-1, 1)
    qkv_mine = qkv_mine.T

    in_first, qkv_t = project(rings[0], 0, mods, 0, items, qkv_mine, bias_mine, None)
    qkv_ts = [qkv_t]
    outs, logs = attend(qkv_t, here)
    first_attended = exchange(outs, "mixed0"), logs
    rings.append(swapped_ring(1, items - 1, [mods], lambda x: once_after(x, [logs])))
    latent = [(pairs[0], at) for pairs in rings for at in range(pairs[0].shape[0])]

    proj_full = gather_rows(proj_weight.T, "proj_weights").T
    feed_shard = jnp.concatenate([up_weight, down_weight.T], 1)
    feed_full = gather_rows(once_after(feed_shard, [logs, rings[1][2], rings[1][-2]]), "feed_weights")
    cots = halves(grad_out.reshape(items, here, model), 0, items)

    bias_proj = proj_bias.astype(F32).reshape(1, -1)
    bias_down = down_bias.astype(F32).reshape(1, -1)
    bias_up = lax.dynamic_slice_in_dim(up_bias.astype(F32), t * hidden, hidden, 0)
    bias_up = bias_up.reshape(1, -1)
    mixed = in_second = grad_feed = activated = grad_upward = None
    grad_attended = grad_qkv = out_own = out_peer = out_half = None

    kept = []
    for item in range(items):
        if item:
            in_first, qkv_t = project(
                rings[1], item - 1, mods, item, items, qkv_mine, bias_mine, in_first
            )
            qkv_ts.append(qkv_t)
        qkv_t = qkv_ts[item]
        if item:
            outs, logs = attend(qkv_t, here)
            came = exchange(outs, "mixed%d" % item)
        else:
            came, logs = first_attended
        mixed, own, peer = back_to_rows(came, proj_full, 0, True, mixed, item, items)
        attended, residual, in_half = second(
            own, swap(peer, "attended%d" % item), bias_proj, *latent[item], mods, item
        )
        in_peer = swap(in_half, "in_second%d" % item)
        kept.append((qkv_t, logs, attended, residual, in_half, in_peer))

    qkv_rows = once_after(qkv_groups.transpose(1, 0, 2).reshape(rows, -1), [kept[0][5]])
    qkv_full = gather_rows(qkv_rows, "qkv_weights")

    up_sums, grads_in, highs = [], [], []
    for item in range(items):
        _, _, _, _, in_half, in_peer = kept[item]
        (
            in_second,
            grad_feed,
            activated,
            grad_upward,
            out_own,
            out_peer,
            gin_own,
            gin_peer,
            up_sum,
            high,
        ) = feed(
            in_half,
            in_peer,
            cots,
            mods,
            feed_full,
            bias_up,
            (in_second, grad_feed, activated, grad_upward, out_own, out_peer),
            item,
            items,
            [grads_in[0][1]] if item == items - 1 else [],
        )
        grads_in.append((gin_own, swap(gin_peer, "grad_in_second%d" % item)))
        up_sums.append(up_sum)
        highs.append(high)

    def before_attention(item):
        _, _, attended, residual, _, _ = kept[item]
        grad_residual, low, sums_two = second_back(
            *grads_in[item], residual, attended, cots[0], mods, item
        )
        return grad_residual, low, sums_two, swap(low, "grad_attended%d" % item)

    bounds = highs[0]
    for high in highs[1:]:
        bounds = jnp.maximum(bounds, high)
    for axis in ("fsdp", "ctx"):
        bounds = butterfly_max(bounds, axis, "bounds")
    bounds = jnp.maximum(bounds[:, 0, 0], 1e-15)
    tokens = items * here * size_c * size_f
    up_scale = 32768.0 / (bounds[0] * bounds[3] * tokens)
    down_scale = 32768.0 / (bounds[1] * bounds[2] * tokens)
    scales = jnp.where(jnp.arange(2 * hidden) < hidden, up_scale, down_scale)
    middles = [before_attention(item) for item in range(items)]
    parts = outer(
        in_second, grad_upward, 0, 768, 0, 2 * hidden, [None, None], [grads_in[1][1]]
    )
    parts = outer(
        grad_feed, activated, 0, 768, hidden // 768, 2 * hidden, parts, [middles[0][3]]
    )
    feed_rows = reduce_rows(*parts, "grad_feed", scales)
    grad_feed_weights, feed_hops = ring_reduce(feed_rows, "grad_feed", scales)

    peers = swap(out_peer, "feed_out")
    gate_sums = []
    for item in range(items):
        out_half, gate_sum = finish(
            out_own, peers, bias_down, kept[item][3], cots[0], mods, out_half, item
        )
        gate_sums.append(gate_sum)
    output = order([out_half], [swap(out_half, "output")], items)

    grad_blocks = []
    for item in range(items):
        _, low, _, low_peer = middles[item]
        grad_attended, grad_mixed = grad_mixed_of(
            low, low_peer, proj_full, grad_attended, item, items
        )
        grad_blocks.append(
            exchange(grad_mixed.reshape(size_c, group, here), "grad_mixed%d" % item)
        )

    def mark(x):
        return x.reshape(-1, x.shape[-1])[:8, :128].astype(F32)

    input_grads, input_peers, mod_terms = [], [], []
    for item in range(items):
        qkv_t, logs, _, _, _, _ = kept[item]
        grad_qkv, blocks = attend_back(
            qkv_t,
            grad_blocks[item],
            logs,
            grad_qkv,
            item,
            items,
            [parts[0]] if item == 0 else [],
        )
        own, peer = back_to_rows(
            exchange(blocks, "grad_qkv%d" % item),
            qkv_full,
            1,
            after=[feed_rows] if item == 0 else [],
        )
        grad_latent, sums_one = first_back(
            own,
            swap(peer, "grad_in_first%d" % item),
            *latent[item],
            middles[item][0],
            mods,
            item,
            [],
        )
        input_grads.append(grad_latent)
        input_peers.append(swap(grad_latent, "grad_latent%d" % item))
        mod_terms.append(jnp.concatenate([sums_one, middles[item][2][:3], gate_sums[item]], 0))

    proj_parts = outer(grad_attended, mixed, 1, half_width, 0, half_width, [None, None])
    grad_proj = ring_reduce(reduce_rows(*proj_parts, "grad_proj"), "grad_proj")[0].T
    grad_qkv = grad_qkv.reshape(3 * group, -1)
    qkv_rows = reduce_rows(*long_outer(in_first, grad_qkv, items), "grad_qkvw")
    grad_qkv_weight = (
        exchange(qkv_rows, "grad_qkvw_c")
        .reshape(size_c, rows, 3, group)
        .transpose(1, 2, 0, 3)
        .reshape(rows, 3, half_width)
    )

    down_sum = sum(
        jnp.sum(grad_feed[item * here : item * here + half].astype(F32), 0)
        for item in range(items)
    )
    qkv_sum = jnp.sum(grad_qkv.astype(F32), 1).reshape(3, group)
    pair_sum = jnp.stack([qkv_sum[0], qkv_sum[2]])
    up_total = lax.dynamic_update_slice_in_dim(
        jnp.zeros(up_bias.shape, F32), sum(up_sums)[0], t * hidden, 0
    )
    pair_total = lax.dynamic_update_slice_in_dim(
        jnp.zeros(qv_bias.shape, F32), pair_sum, first_column + c * group, 1
    )
    proj_sum = sum(middle[2][3] for middle in middles)
    sums = jnp.concatenate(
        [jnp.stack(mod_terms).reshape(-1), up_total, pair_total.reshape(-1), proj_sum, down_sum]
    ).reshape(-1, 128)
    sums = butterfly_sum(butterfly_sum(sums, "tp", "sums"), "ctx", "sums")
    sums = cube_gather(sums, "sums").reshape(size_f, -1)
    edge = items * 6 * model
    grad_mod_all = sums[:, :edge].astype(BF16).reshape(size_f, items, 6, model)
    ada_sum = tree_sum(jnp.sum(grad_mod_all.astype(F32), 1))
    bias_sum = tree_sum(sums[:, edge:])
    ends = [up_bias.shape[0], up_bias.shape[0] + qv_bias.size]

    mod_here = lax.dynamic_slice_in_dim(grad_mod_all, first_column, half_width, 3).reshape(
        size_f * items, -1
    )
    grad_ada = dot(silu_here, mod_here, ((0,), (0,))).reshape(rows, 6, half_width)
    cond_part = dot(mod_here, ada_weight.reshape(rows, -1), ((1,), (1,)))
    cond_part = lax.dynamic_update_slice_in_dim(
        jnp.zeros((size_f * items, model), F32), cond_part, first_row, 1
    ).reshape(size_f, items, model)
    cond_total = cube_reduce(cond_part, "grad_cond")
    for axis in ("ctx", "tp"):
        cond_total = butterfly_sum(cond_total, axis, "grad_cond")
    grad_cond = jax.vjp(jax.nn.silu, cond)[1](cond_total)[0]

    return (
        output.reshape(latents.shape),
        order(input_grads, input_peers, items).reshape(latents.shape),
        grad_cond.reshape(condition.shape),
        grad_ada,
        ada_sum,
        grad_qkv_weight,
        bias_sum[ends[0] : ends[1]].reshape(qv_bias.shape),
        grad_proj,
        bias_sum[ends[1] : ends[1] + model],
        grad_feed_weights[:, :hidden],
        bias_sum[: ends[0]],
        grad_feed_weights[:, hidden:].T,
        bias_sum[ends[1] + model :],
    )


def tree_sum(entries):
    while entries.shape[0] > 1:
        entries = entries[0::2] + entries[1::2]
    return entries[0]


def solution(mesh):
    in_specs = (
        P(None, "fsdp", "ctx", None),
        P(None, "fsdp", None),
        P(None, "fsdp", "ctx", None),
        P(("fsdp", "ctx"), None, "tp"),
        P(),
        P(("fsdp", "ctx"), None, "tp"),
        P(),
        P("tp", ("fsdp", "ctx")),
        P(),
        P(("fsdp", "ctx"), "tp"),
        P(),
        P("tp", ("fsdp", "ctx")),
        P(),
    )
    out_specs = (
        P(None, "fsdp", "ctx", None),
        P(None, "fsdp", "ctx", None),
        P(None, "fsdp", None),
        P(("fsdp", "ctx"), None, "tp"),
        P(),
        P(("fsdp", "ctx"), None, "tp"),
        P(),
        P("tp", ("fsdp", "ctx")),
        P(),
        P(("fsdp", "ctx"), "tp"),
        P(),
        P("tp", ("fsdp", "ctx")),
        P(),
    )
    return jax.shard_map(body, mesh=mesh, in_specs=in_specs, out_specs=out_specs, check_vma=False)
```

```python
from functools import partial

import jax
import jax.numpy as jnp
from jax import lax
from jax.experimental import pallas as pl
from jax.experimental.pallas import tpu as pltpu
from jax.sharding import PartitionSpec as P

HEADS = 16
HEAD_DIM = 72
LOG2E = 1.4426950408889634
F32 = jnp.float32
BF16 = jnp.bfloat16


def dot(a, b, dims):
    return lax.dot_general(a, b, (dims, ((), ())), preferred_element_type=F32)


def normalize(values):
    centre = values - jnp.mean(values, -1, keepdims=True)
    inverse = lax.rsqrt(jnp.mean(centre * centre, -1, keepdims=True) + 1e-06)
    return (centre * inverse, inverse)


def norm_back(incoming, normed, inverse):
    return inverse * (
        incoming
        - jnp.mean(incoming, -1, keepdims=True)
        - normed * jnp.mean(incoming * normed, -1, keepdims=True)
    )


def shift(x, k, name="shift"):
    size = lax.axis_size("ctx")
    with jax.named_scope(name):
        return lax.ppermute(x, "ctx", [(i, (i + k) % size) for i in range(size)])


def flip(x, axis, bit, name="flip"):
    size = lax.axis_size(axis)
    with jax.named_scope(name):
        return lax.ppermute(x, axis, [(i, i ^ (1 << bit)) for i in range(size)])


def exchange(x, name):
    with jax.named_scope(name):
        return lax.all_to_all(x, "ctx", 0, 0)


def gather_rows(x, name):
    with jax.named_scope(name):
        return lax.all_gather(x, ("fsdp", "ctx"), tiled=True)


def bits_of(axis):
    return lax.axis_size(axis).bit_length() - 1


def ring_gather(x, name, second=lambda x: x):
    size = lax.axis_size("ctx")
    blocks = [x] * size
    moving = x
    for step in range(1, size // 2 + 1):
        moving = shift(second(moving) if step == 2 else moving, 1, name + "_right")
        blocks[step] = moving
    moving = x
    for step in range(1, (size - 1) // 2 + 1):
        moving = shift(moving, -1, name + "_left")
        blocks[size - step] = moving
    return blocks


def butterfly_sum(x, axis, name):
    for bit in range(bits_of(axis)):
        x = x + flip(x, axis, bit, name)
    return x


def butterfly_max(x, axis, name):
    for bit in range(bits_of(axis)):
        x = jnp.maximum(x, flip(x, axis, bit, name))
    return x


def cube_gather(x, name):
    x = x[None]
    for bit in range(bits_of("fsdp")):
        x = jnp.concatenate([x, flip(x, "fsdp", bit, name)], 0)
    return x


def cube_reduce(x, name):
    for bit in reversed(range(bits_of("fsdp"))):
        half = x.shape[0] // 2
        x = x[:half] + flip(x[half:], "fsdp", bit, name)
    return x[0]


def spread(pieces, name):
    for bit in reversed(range(bits_of("fsdp"))):
        pieces = pieces + [
            (offset ^ (1 << bit), places, flip(block, "fsdp", bit, name + "_%d" % bit))
            for offset, places, block in pieces
        ]
    return pieces


def gather_stacked(shard, name):
    blocks = ring_gather(shard, name)
    return spread([(0, "before", jnp.stack(blocks))], name)


def place_kernel(targets, widths, *refs):
    count = len(targets)
    ins, outs = refs[:count], refs[-3 - len(widths) : -3]
    held, in_sem, out_sem = refs[-3:]
    own_f = lax.axis_index("fsdp")
    own_c = lax.axis_index("ctx")
    size_c = lax.axis_size("ctx")
    arriving, leaving = [], []
    for (offset, places), ref in zip(targets, ins):
        row = jnp.bitwise_xor(own_f, offset)
        for at in range(size_c):
            column = at if places == "own" else lax.rem(own_c + size_c - at, size_c)
            slot = len(arriving)
            arriving.append(pltpu.make_async_copy(ref.at[at], held.at[slot], in_sem.at[slot]))
            first = 0
            for width, out in zip(widths, outs):
                leaving.append(
                    pltpu.make_async_copy(
                        held.at[slot, :, pl.ds(first, width)],
                        out.at[row, column],
                        out_sem.at[len(leaving)],
                    )
                )
                first += width
    for copy in arriving:
        copy.start()
    each = len(widths)
    for slot, copy in enumerate(arriving):
        copy.wait()
        for out_copy in leaving[slot * each : (slot + 1) * each]:
            out_copy.start()
    for copy in leaving:
        copy.wait()


def place(pieces, widths, after=()):
    size_f, size_c = lax.axis_size("fsdp"), lax.axis_size("ctx")
    rows, total = pieces[0][2].shape[1:]
    count = size_f * size_c
    outs = pl.pallas_call(
        partial(place_kernel, [piece[:2] for piece in pieces], widths),
        out_shape=[jax.ShapeDtypeStruct((size_f, size_c, rows, width), BF16) for width in widths],
        in_specs=[ANYWHERE] * (len(pieces) + len(after)),
        out_specs=[ANYWHERE] * len(widths),
        scratch_shapes=[
            pltpu.VMEM((count, rows, total), BF16),
            pltpu.SemaphoreType.DMA((count,)),
            pltpu.SemaphoreType.DMA((count * len(widths),)),
        ],
        compiler_params=pltpu.CompilerParams(vmem_limit_bytes=40 << 20),
        cost_estimate=pl.CostEstimate(
            flops=0, bytes_accessed=4 * count * rows * total, transcendentals=0
        ),
    )(*[piece[2] for piece in pieces], *after)
    return [out.reshape(-1, width) for out, width in zip(outs, widths)]


def lower(x, scale):
    return x if scale is None else (x * scale).astype(jnp.float16)


def higher(x, scale):
    return x if scale is None else x.astype(F32) * (1.0 / scale)


def reduce_rows(send, keep, name, scale=None):
    size_c = lax.axis_size("ctx")
    own_f = lax.axis_index("fsdp")
    _, width, columns = keep.shape
    parts = [keep, flip(send, "fsdp", 0, name + "_0")]
    for bit in range(1, bits_of("fsdp")):
        own_bit = (own_f >> bit) % 2
        pairs = [part.reshape(-1, 2, width, columns) for part in parts]
        got = sum(lax.dynamic_index_in_dim(pair, 1 - own_bit, 1, False) for pair in pairs)
        got = flip(lower(got, scale), "fsdp", bit, name + "_%d" % bit)
        parts = [lax.dynamic_index_in_dim(pair, own_bit, 1, False) for pair in pairs]
        parts.append(higher(got, scale))
    return sum(parts).reshape(size_c, width // size_c, columns)


def ring_reduce(blocks, name, scale=None):
    size = lax.axis_size("ctx")
    own = lax.axis_index("ctx")

    def block(offset):
        return lax.dynamic_index_in_dim(blocks, (own + offset) % size, 0, False)

    total = block(0)
    hops = []
    for sign, reach in ((1, size // 2), (-1, (size - 1) // 2)):
        moving = None
        for distance in range(reach, 0, -1):
            term = block(sign * distance)
            if moving is not None:
                term = term + moving
            hops.append(shift(lower(term, scale), sign, name + "_ring"))
            moving = higher(hops[-1], scale)
        if moving is not None:
            total = total + moving
    return total, hops


def whole(shape):
    return pl.BlockSpec(tuple(shape), lambda *_: (0,) * len(shape))


def struct(shape, dtype):
    return jax.ShapeDtypeStruct(tuple(shape), dtype)


ANYWHERE = pl.BlockSpec(memory_space=pltpu.HBM)
PARAMS = pltpu.CompilerParams(vmem_limit_bytes=48 << 20)


def cost(flops, nbytes, exps=0):
    return pl.CostEstimate(flops=int(flops), bytes_accessed=int(nbytes), transcendentals=int(exps))


def mods_spec(mods, item):
    return pl.BlockSpec((None,) + mods.shape[1:], lambda *_: (item, 0, 0))


def largest(x):
    return jnp.full((8, 128), jnp.max(jnp.abs(x)), F32)


def slab_call(kernel, args, in_specs, helds, after=(), **options):
    taken = [held for held in helds if held is not None]
    count = len(args)
    more = len(taken) + len(after)

    def run(*refs):
        kernel(*refs[:count], *refs[count + more :])

    return pl.pallas_call(
        run,
        in_specs=in_specs + [ANYWHERE] * more,
        input_output_aliases={count + at: at for at in range(len(taken))},
        compiler_params=PARAMS,
        **options,
    )(*args, *taken, *after)


def halves_kernel(first, both_ref, own_ref, peer_ref):
    count, half, _ = own_ref.shape
    t = lax.axis_index("tp")
    for rank, out in ((t, own_ref), (1 - t, peer_ref)):
        rows = pl.ds(pl.multiple_of(rank * half, half), half)
        for at in range(count):
            out[at] = both_ref[first + at, rows, :]


def halves(x, first, count, after=()):
    items, here, model = x.shape
    shape = (count, here // 2, model)
    return slab_call(
        partial(halves_kernel, first),
        [x],
        [whole(x.shape)],
        [],
        after,
        grid=(1,),
        out_specs=[whole(shape)] * 2,
        out_shape=[struct(shape, x.dtype)] * 2,
        cost_estimate=cost(0, 4 * count * here * model),
    )


def wait_kernel(in_ref, out_ref):
    out_ref[...] = in_ref[...]


def once_after(x, after):
    return slab_call(
        wait_kernel,
        [x],
        [whole(x.shape)],
        [],
        after,
        grid=(1,),
        out_specs=whole(x.shape),
        out_shape=struct(x.shape, x.dtype),
        cost_estimate=cost(0, 4 * x.size),
    )


def project_kernel(count, *refs):
    pieces = refs[:count]
    mods_ref, weight_ref, bias_ref, in_ref, out_ref = refs[count:]
    for pair in range(count // 2):
        rows = jnp.concatenate([pieces[2 * pair][...], pieces[2 * pair + 1][...]], 0)
        here = rows.shape[0]
        normed, _ = normalize(rows.astype(F32))
        in_first = (normed * (1.0 + mods_ref[1:2, :]) + mods_ref[0:1, :]).astype(BF16)
        in_ref[pl.ds(pair * here, here), :] = in_first
        product = dot(weight_ref[...], in_first, ((1,), (1,))) + bias_ref[...]
        out_ref[:, pl.ds(pair * here, here)] = product.astype(BF16)


def project(pieces, place_in, mods, item, items, weight_t, bias, held, after=()):
    _, half, model = pieces[0].shape
    total = half * len(pieces)
    piece_spec = pl.BlockSpec((None, half, model), lambda i: (place_in, 0, 0))
    width = weight_t.shape[0]
    return slab_call(
        partial(project_kernel, len(pieces)),
        [*pieces, mods, weight_t, bias],
        [piece_spec] * len(pieces)
        + [mods_spec(mods, item), whole(weight_t.shape), whole(bias.shape)],
        [held],
        after,
        grid=(1,),
        out_specs=[
            pl.BlockSpec((total, model), lambda i: (item, 0)),
            whole((width, total)),
        ],
        out_shape=[struct((items * total, model), BF16), struct((width, total), BF16)],
        cost_estimate=cost(2 * total * model * width, 6 * total * model),
    )


def head_rows(values, head):
    values = values.astype(F32)
    row = lax.broadcasted_iota(jnp.int32, values.shape, 0)
    inside = (row >= head * HEAD_DIM) & (row < (head + 1) * HEAD_DIM)
    return jnp.where(inside, values, 0.0).astype(BF16), inside


def attend_kernel(heads, steps, q_ref, kt_ref, vt_ref, out_ref, log_ref, k_ref):
    step = pl.program_id(0)
    factor = HEAD_DIM ** (-0.5) * LOG2E

    @pl.when(step == 0)
    def _():
        k_ref[...] = kt_ref[...].T

    total = None
    for head in range(heads):
        q_head, inside = head_rows(q_ref[...], head)
        scores = dot(k_ref[...], q_head, ((1,), (0,)))
        highest = jnp.max(scores, 0, keepdims=True)
        exponent = jnp.exp2((scores - highest) * factor)
        summed = jnp.sum(exponent, 0, keepdims=True)
        chances = (exponent * (1.0 / summed)).astype(BF16)
        mixed = dot(vt_ref[...], chances, ((1,), (0,)))
        total = mixed if total is None else jnp.where(inside, mixed, total)
        log_ref[pl.ds(head, 1), :] = highest * factor + jnp.log2(summed)
    out_ref[lax.rem(lax.axis_index("ctx") + steps - step, steps)] = total.astype(BF16)


def attend(qkv_t, here, after=()):
    group, total = qkv_t.shape[0] // 3, qkv_t.shape[1]
    heads, steps = group // HEAD_DIM, total // here
    thirds = qkv_t.reshape(3, group, total)
    return slab_call(
        partial(attend_kernel, heads, steps),
        [thirds, thirds, thirds],
        [
            pl.BlockSpec((None, group, here), lambda i: (0, 0, i)),
            pl.BlockSpec((None, group, total), lambda i: (1, 0, 0)),
            pl.BlockSpec((None, group, total), lambda i: (2, 0, 0)),
        ],
        [],
        after,
        grid=(steps,),
        out_specs=[
            whole((steps, group, here)),
            pl.BlockSpec((heads, here), lambda i: (0, i)),
        ],
        out_shape=[struct((steps, group, here), BF16), struct((heads, total), F32)],
        scratch_shapes=[pltpu.VMEM((total, group), BF16)],
        cost_estimate=cost(heads * total * total * 1600, 8 * group * total, heads * total * total),
    )


def attend_back_kernel(
    heads,
    steps,
    q_ref,
    kt_ref,
    vt_ref,
    log_ref,
    grad_ref,
    all_ref,
    out_ref,
    k_ref,
    v_ref,
    dk_ref,
    dv_ref,
):
    step = pl.program_id(0)
    own_c = lax.axis_index("ctx")
    scaling = HEAD_DIM ** (-0.5)
    group, block = q_ref.shape

    @pl.when(step == 0)
    def _():
        dk_ref[...] = jnp.zeros_like(dk_ref)
        dv_ref[...] = jnp.zeros_like(dv_ref)
        k_ref[...] = kt_ref[...].T
        v_ref[...] = vt_ref[...].T

    grad = grad_ref[lax.rem(own_c + steps - step, steps)]
    grad_query = None
    for head in range(heads):
        q_head, inside = head_rows(q_ref[...], head)
        do_head, _ = head_rows(grad, head)
        scores = dot(k_ref[...], q_head, ((1,), (0,)))
        chances = jnp.exp2(scores * (scaling * LOG2E) - log_ref[pl.ds(head, 1), :])
        grad_chances = dot(v_ref[...], do_head, ((1,), (0,)))
        weighted = jnp.sum(chances * grad_chances, 0, keepdims=True)
        grad_scores = (chances * (grad_chances - weighted)).astype(BF16)
        term = dot(kt_ref[...], grad_scores, ((1,), (0,)))
        grad_query = term if grad_query is None else jnp.where(inside, term, grad_query)
        dk_ref[...] += dot(q_head, grad_scores, ((1,), (1,)))
        dv_ref[...] += dot(do_head, chances.astype(BF16), ((1,), (1,)))
    columns = pl.ds(pl.multiple_of(step * block, block), block)
    all_ref[0, :, columns] = (grad_query * scaling).astype(BF16)

    @pl.when(step == steps - 1)
    def _():
        all_ref[1] = (dk_ref[...] * scaling).astype(BF16)
        all_ref[2] = dv_ref[...].astype(BF16)
        for at in range(steps):
            out_ref[lax.rem(own_c + steps - at, steps)] = all_ref[
                :, :, at * block : (at + 1) * block
            ]


def attend_back(qkv_t, grads, logs, held, item, items, after=()):
    group, total = qkv_t.shape[0] // 3, qkv_t.shape[1]
    heads, steps = group // HEAD_DIM, grads.shape[0]
    here = total // steps
    thirds = qkv_t.reshape(3, group, total)
    return slab_call(
        partial(attend_back_kernel, heads, steps),
        [thirds, thirds, thirds, logs, grads],
        [
            pl.BlockSpec((None, group, here), lambda i: (0, 0, i)),
            pl.BlockSpec((None, group, total), lambda i: (1, 0, 0)),
            pl.BlockSpec((None, group, total), lambda i: (2, 0, 0)),
            pl.BlockSpec((heads, here), lambda i: (0, i)),
            whole(grads.shape),
        ],
        [held],
        after,
        grid=(steps,),
        out_specs=[
            pl.BlockSpec((3, group, total), lambda i: (0, 0, item)),
            whole((steps, 3, group, here)),
        ],
        out_shape=[
            struct((3, group, items * total), BF16),
            struct((steps, 3, group, here), BF16),
        ],
        scratch_shapes=[
            pltpu.VMEM((total, group), BF16),
            pltpu.VMEM((total, group), BF16),
            pltpu.VMEM((group, total), F32),
            pltpu.VMEM((group, total), F32),
        ],
        cost_estimate=cost(heads * total * total * 4000, 16 * group * total, heads * total * total),
    )


def back_to_rows_kernel(contract, keep, blocks_ref, weight_ref, *outs):
    own_ref, peer_ref = outs[-2:]
    rows = blocks_ref[...].reshape(-1, blocks_ref.shape[-1])
    if keep:
        outs[0][...] = rows
    total = dot(rows, weight_ref[...], ((0,), (contract,)))
    half = own_ref.shape[0]
    own_ref[...] = total[:half]
    peer_ref[...] = total[half:]


def back_to_rows(blocks, weight, contract, keep=False, held=None, item=0, items=1, after=()):
    here = blocks.shape[-1]
    features, model = weight.shape[contract], weight.shape[1 - contract]
    half = here // 2
    out_specs = [whole((half, model))] * 2
    out_shape = [struct((half, model), F32)] * 2
    if keep:
        out_specs = [pl.BlockSpec((features, here), lambda i: (0, item))] + out_specs
        out_shape = [struct((features, items * here), BF16)] + out_shape
    return slab_call(
        partial(back_to_rows_kernel, contract, keep),
        [blocks, weight],
        [whole(blocks.shape), whole(weight.shape)],
        [held],
        after,
        grid=(1,),
        out_specs=out_specs,
        out_shape=out_shape,
        cost_estimate=cost(
            2 * here * features * model, 2 * features * model + 8 * here * model
        ),
    )


def second_kernel(own_ref, peer_ref, bias_ref, latent_ref, mods_ref, att_ref, res_ref, in_ref):
    attended = own_ref[...] + peer_ref[...] + bias_ref[...]
    residual = latent_ref[...].astype(F32) + mods_ref[2:3, :] * attended
    normed, _ = normalize(residual)
    att_ref[...] = attended
    res_ref[...] = residual
    in_ref[...] = (normed * (1.0 + mods_ref[4:5, :]) + mods_ref[3:4, :]).astype(BF16)


def second(own, peer, bias, latent, place_in, mods, item, after=()):
    shape = own.shape
    return slab_call(
        second_kernel,
        [own, peer, bias, latent, mods],
        [
            whole(shape),
            whole(shape),
            whole(bias.shape),
            pl.BlockSpec((None,) + shape, lambda i: (place_in, 0, 0)),
            mods_spec(mods, item),
        ],
        [],
        after,
        grid=(1,),
        out_specs=[whole(shape)] * 3,
        out_shape=[struct(shape, F32), struct(shape, F32), struct(shape, BF16)],
        cost_estimate=cost(20 * own.size, 20 * own.size),
    )


def feed_kernel(
    steps,
    own_ref,
    peer_ref,
    cot_own,
    cot_peer,
    mods_ref,
    up_ref,
    down_ref,
    bias_ref,
    in_all,
    grad_all,
    act_ref,
    gup_ref,
    out_own,
    out_peer,
    gin_own,
    gin_peer,
    sum_ref,
    highs,
    in_ref,
    grad_ref,
    out_acc,
    gin_acc,
):
    step = pl.program_id(0)
    half = own_ref.shape[0]

    @pl.when(step == 0)
    def _():
        in_ref[:half, :] = own_ref[...]
        in_ref[half:, :] = peer_ref[...]
        in_all[...] = in_ref[...]
        gate = mods_ref[5:6, :]
        grad_ref[:half, :] = (cot_own[...].astype(F32) * gate).astype(BF16)
        grad_ref[half:, :] = (cot_peer[...].astype(F32) * gate).astype(BF16)
        grad_all[...] = grad_ref[...]
        highs[0] = largest(in_ref[...].astype(F32))
        highs[1] = largest(grad_ref[...].astype(F32))
        highs[2] = jnp.zeros((8, 128), F32)
        highs[3] = jnp.zeros((8, 128), F32)

    upward = dot(in_ref[...], up_ref[...], ((1,), (0,))) + bias_ref[...]
    grad_act = dot(grad_ref[...], down_ref[...], ((1,), (0,)))
    inner = 0.7978845608028654
    squared = upward * upward
    curve = jnp.tanh(inner * upward * (1.0 + 0.044715 * squared))
    activated = (0.5 * upward * (1.0 + curve)).astype(BF16)
    slope = 0.5 * (1.0 + curve) + (0.5 * inner) * upward * (1.0 - curve * curve) * (
        1.0 + (3.0 * 0.044715) * squared
    )
    grad_up = (slope * grad_act).astype(BF16)
    act_ref[...] = activated
    gup_ref[...] = grad_up
    wide = grad_up.astype(F32)
    sum_ref[...] = jnp.sum(wide, 0, keepdims=True)
    highs[2] = jnp.maximum(highs[2], largest(activated.astype(F32)))
    highs[3] = jnp.maximum(highs[3], largest(wide))
    out_term = dot(activated, down_ref[...], ((1,), (1,)))
    gin_term = dot(grad_up, up_ref[...], ((1,), (1,)))

    @pl.when(step == 0)
    def _():
        out_acc[...] = out_term
        gin_acc[...] = gin_term

    @pl.when(step > 0)
    def _():
        out_acc[...] += out_term
        gin_acc[...] += gin_term

    @pl.when(step == steps - 1)
    def _():
        out_own[...] = out_acc[:half, :]
        out_peer[...] = out_acc[half:, :].astype(BF16)
        gin_own[...] = gin_acc[:half, :]
        gin_peer[...] = gin_acc[half:, :]


def feed(own, peer, cots, mods, weights, bias, helds, item, items, after=()):
    half, model = own.shape
    here, hidden = 2 * half, weights.shape[1] // 2
    cot = pl.BlockSpec((None, half, model), lambda j: (item, 0, 0))
    tile = 768
    steps = hidden // tile
    rows = pl.BlockSpec((here, model), lambda j: (item, 0))
    slab = pl.BlockSpec((here, tile), lambda j: (item, j))
    return slab_call(
        partial(feed_kernel, steps),
        [own, peer, *cots, mods, weights, weights, bias],
        [whole(own.shape)] * 2
        + [cot] * 2
        + [
            mods_spec(mods, item),
            pl.BlockSpec((model, tile), lambda j: (0, j)),
            pl.BlockSpec((model, tile), lambda j: (0, j + steps)),
            pl.BlockSpec((1, tile), lambda j: (0, j)),
        ],
        helds,
        after,
        grid=(steps,),
        out_specs=[rows, rows, slab, slab]
        + [pl.BlockSpec((half, model), lambda j: (item, 0))] * 2
        + [whole(own.shape)] * 2
        + [pl.BlockSpec((1, tile), lambda j: (0, j)), whole((4, 8, 128))],
        out_shape=[
            struct((items * here, model), BF16),
            struct((items * here, model), BF16),
            struct((items * here, hidden), BF16),
            struct((items * here, hidden), BF16),
            struct((items * half, model), F32),
            struct((items * half, model), BF16),
            struct(own.shape, F32),
            struct(own.shape, F32),
            struct((1, hidden), F32),
            struct((4, 8, 128), F32),
        ],
        scratch_shapes=[
            pltpu.VMEM((here, model), BF16),
            pltpu.VMEM((here, model), BF16),
            pltpu.VMEM((here, model), F32),
            pltpu.VMEM((here, model), F32),
        ],
        cost_estimate=cost(8 * here * model * hidden, 4 * model * hidden + 4 * here * hidden),
    )


def finish_kernel(own_ref, peer_ref, bias_ref, res_ref, cot_ref, mods_ref, out_ref, sum_ref):
    feed_out = own_ref[...] + peer_ref[...].astype(F32) + bias_ref[...]
    out_ref[...] = (res_ref[...] + mods_ref[5:6, :] * feed_out).astype(BF16)
    sum_ref[...] = jnp.sum(cot_ref[...].astype(F32) * feed_out, 0, keepdims=True)


def finish(own, peer, bias, residual, cots, mods, held, item, after=()):
    items, half, model = cots.shape
    part = pl.BlockSpec((half, model), lambda i: (item, 0))
    return slab_call(
        finish_kernel,
        [own, peer, bias, residual, cots, mods],
        [
            part,
            part,
            whole(bias.shape),
            whole((half, model)),
            pl.BlockSpec((None, half, model), lambda i: (item, 0, 0)),
            mods_spec(mods, item),
        ],
        [held],
        after,
        grid=(1,),
        out_specs=[part, whole(bias.shape)],
        out_shape=[struct((items * half, model), BF16), struct(bias.shape, F32)],
        cost_estimate=cost(8 * half * model, 16 * half * model),
    )


def second_back_kernel(
    own_ref, peer_ref, res_ref, att_ref, cot_ref, mods_ref, grad_ref, low_ref, sum_ref
):
    incoming = own_ref[...] + peer_ref[...]
    normed, inverse = normalize(res_ref[...])
    grad = cot_ref[...].astype(F32) + norm_back(
        incoming * (1.0 + mods_ref[4:5, :]), normed, inverse
    )
    low = (grad * mods_ref[2:3, :]).astype(BF16)
    grad_ref[...] = grad
    low_ref[...] = low
    sum_ref[0:1, :] = jnp.sum(grad * att_ref[...], 0, keepdims=True)
    sum_ref[1:2, :] = jnp.sum(incoming, 0, keepdims=True)
    sum_ref[2:3, :] = jnp.sum(incoming * normed, 0, keepdims=True)
    sum_ref[3:4, :] = jnp.sum(low.astype(F32), 0, keepdims=True)


def second_back(own, peer, residual, attended, cots, mods, item, after=()):
    shape = own.shape
    return slab_call(
        second_back_kernel,
        [own, peer, residual, attended, cots, mods],
        [whole(shape)] * 4
        + [pl.BlockSpec((None,) + shape, lambda i: (item, 0, 0)), mods_spec(mods, item)],
        [],
        after,
        grid=(1,),
        out_specs=[whole(shape), whole(shape), whole((4, shape[1]))],
        out_shape=[struct(shape, F32), struct(shape, BF16), struct((4, shape[1]), F32)],
        cost_estimate=cost(30 * own.size, 24 * own.size),
    )


def grad_mixed_kernel(own_ref, peer_ref, weight_ref, all_ref, out_ref):
    rows = jnp.concatenate([own_ref[...], peer_ref[...]], 0)
    all_ref[...] = rows
    out_ref[...] = dot(weight_ref[...], rows, ((1,), (1,))).astype(BF16)


def grad_mixed_of(own, peer, weight, held, item, items, after=()):
    features, model = weight.shape
    here = 2 * own.shape[0]
    return slab_call(
        grad_mixed_kernel,
        [own, peer, weight],
        [whole(own.shape), whole(own.shape), whole(weight.shape)],
        [held],
        after,
        grid=(1,),
        out_specs=[
            pl.BlockSpec((here, model), lambda i: (item, 0)),
            whole((features, here)),
        ],
        out_shape=[struct((items * here, model), BF16), struct((features, here), BF16)],
        cost_estimate=cost(2 * here * features * model, 2 * features * model),
    )


def first_back_kernel(own_ref, peer_ref, latent_ref, res_ref, mods_ref, grad_ref, sum_ref):
    incoming = own_ref[...] + peer_ref[...]
    normed, inverse = normalize(latent_ref[...].astype(F32))
    grad_ref[...] = res_ref[...] + norm_back(
        incoming * (1.0 + mods_ref[1:2, :]), normed, inverse
    )
    sum_ref[0:1, :] = jnp.sum(incoming, 0, keepdims=True)
    sum_ref[1:2, :] = jnp.sum(incoming * normed, 0, keepdims=True)


def first_back(own, peer, latent, place_in, grad_residual, mods, item, after=()):
    shape = own.shape
    return slab_call(
        first_back_kernel,
        [own, peer, latent, grad_residual, mods],
        [
            whole(shape),
            whole(shape),
            pl.BlockSpec((None,) + shape, lambda i: (place_in, 0, 0)),
            whole(shape),
            mods_spec(mods, item),
        ],
        [],
        after,
        grid=(1,),
        out_specs=[whole(shape), whole((2, shape[1]))],
        out_shape=[struct(shape, F32), struct((2, shape[1]), F32)],
        cost_estimate=cost(30 * own.size, 20 * own.size),
    )


def split_rows(product_ref, send_ref, keep_ref):
    width = keep_ref.shape[1]
    core = lax.rem(lax.axis_index("fsdp"), 2)
    for high in range(keep_ref.shape[0]):
        theirs = pl.multiple_of((2 * high + 1 - core) * width, 8)
        mine = pl.multiple_of((2 * high + core) * width, 8)
        send_ref[high] = product_ref[pl.ds(theirs, width), :]
        keep_ref[high] = product_ref[pl.ds(mine, width), :]


def outer_kernel(right, left_ref, right_ref, send_ref, keep_ref, left_t, *product):
    @pl.when(pl.program_id(0) == 0)
    def _():
        left_t[...] = left_ref[...].T

    if product:
        product[0][...] = dot(left_t[...], right_ref[...], ((1,), (right,)))
        split_rows(product[0], send_ref, keep_ref)
        return
    width = keep_ref.shape[1]
    core = lax.rem(lax.axis_index("fsdp"), 2)
    for high in range(keep_ref.shape[0]):
        for out, which in ((send_ref, 1 - core), (keep_ref, core)):
            rows = pl.ds(pl.multiple_of((2 * high + which) * width, 8), width)
            out[high] = dot(left_t[rows, :], right_ref[...], ((1,), (right,)))


def outer(left, right, contract, tile, first, columns, helds, after=()):
    rows, model = left.shape
    size_f = lax.axis_size("fsdp")
    wide = right.shape[1 - contract]
    shape = (size_f // 2, model // size_f, columns)
    block = pl.BlockSpec(shape[:2] + (tile,), lambda j: (0, 0, j + first))
    right_spec = (
        pl.BlockSpec((rows, tile), lambda j: (0, j))
        if contract == 0
        else pl.BlockSpec((tile, rows), lambda j: (j, 0))
    )
    return slab_call(
        partial(outer_kernel, contract),
        [left, right],
        [whole(left.shape), right_spec],
        helds,
        after,
        grid=(wide // tile,),
        out_specs=[block] * 2,
        out_shape=[struct(shape, F32)] * 2,
        scratch_shapes=[pltpu.VMEM((model, rows), BF16)]
        + ([pltpu.VMEM((model, tile), F32)] if shape[1] % 16 else []),
        cost_estimate=cost(2 * rows * model * wide, 2 * rows * wide + 4 * model * wide),
    )


def long_outer_kernel(steps, left_ref, right_ref, send_ref, keep_ref, product):
    step = pl.program_id(0)
    term = dot(left_ref[...], right_ref[...], ((0,), (1,)))

    @pl.when(step == 0)
    def _():
        product[...] = term

    @pl.when(step > 0)
    def _():
        product[...] += term

    @pl.when(step == steps - 1)
    def _():
        split_rows(product, send_ref, keep_ref)


def long_outer(left, right, steps, after=()):
    rows, model = left.shape
    wide = right.shape[0]
    size_f = lax.axis_size("fsdp")
    shape = (size_f // 2, model // size_f, wide)
    return slab_call(
        partial(long_outer_kernel, steps),
        [left, right],
        [
            pl.BlockSpec((rows // steps, model), lambda j: (j, 0)),
            pl.BlockSpec((wide, rows // steps), lambda j: (0, j)),
        ],
        [],
        after,
        grid=(steps,),
        out_specs=[whole(shape)] * 2,
        out_shape=[struct(shape, F32)] * 2,
        scratch_shapes=[pltpu.VMEM((model, wide), F32)],
        cost_estimate=cost(2 * rows * model * wide, 2 * rows * (model + wide)),
    )


def order_kernel(count, *refs):
    out_ref = refs[-1]
    half = out_ref.shape[1] // 2
    items = out_ref.shape[0]
    t = lax.axis_index("tp")
    for rank, parts in ((t, refs[:count]), (1 - t, refs[count : 2 * count])):
        rows = pl.ds(pl.multiple_of(rank * half, half), half)
        for item in range(items):
            part = parts[0][item * half : (item + 1) * half, :] if count == 1 else parts[item][...]
            out_ref[item, rows, :] = part


def order(owns, peers, items, after=()):
    model = owns[0].shape[1]
    half = sum(own.shape[0] for own in owns) // items
    return slab_call(
        partial(order_kernel, len(owns)),
        [*owns, *peers],
        [whole(part.shape) for part in (*owns, *peers)],
        [],
        after,
        grid=(1,),
        out_specs=whole((items, 2 * half, model)),
        out_shape=struct((items, 2 * half, model), owns[0].dtype),
        cost_estimate=cost(0, 16 * items * half * model),
    )


def body(
    latents,
    condition,
    grad_out,
    ada_weight,
    ada_bias,
    qkv_weight,
    qv_bias,
    proj_weight,
    proj_bias,
    up_weight,
    up_bias,
    down_weight,
    down_bias,
):
    t = lax.axis_index("tp")
    c = lax.axis_index("ctx")
    f = lax.axis_index("fsdp")
    size_c = lax.axis_size("ctx")
    size_f = lax.axis_size("fsdp")
    micro, batch, here, model = latents.shape
    items = micro * batch
    half = here // 2
    half_width = qkv_weight.shape[2]
    group = half_width // size_c
    hidden = up_weight.shape[1]
    rows = qkv_weight.shape[0]
    first_column = t * half_width

    def swap(x, name):
        return flip(x, "tp", 0, name)

    def both(own, peer, axis):
        return jnp.where(
            t == 0,
            jnp.concatenate([own, peer], axis),
            jnp.concatenate([peer, own], axis),
        )

    qkv_groups = (
        qkv_weight.reshape(rows, 3, size_c, group)
        .transpose(2, 0, 1, 3)
        .reshape(size_c, rows, 3 * group)
    )
    qkv_came = exchange(qkv_groups, "qkv_c")

    flat_latents = latents.reshape(items, here, model)

    def swapped_ring(first, count, after=(), second=lambda x: x):
        own, peer = halves(flat_latents, first, count, after)
        pairs = [own, peer]
        for piece in ring_gather(own, "latent%d" % first, second)[1:]:
            pairs += [piece, swap(piece, "latent%d_t" % first)]
        return pairs

    rings = [swapped_ring(0, 1)]

    cond = condition.reshape(items, model).astype(F32)
    silu_all = cube_gather(jax.nn.silu(cond).astype(BF16), "cond")
    first_row = (f * size_c + c) * rows
    silu_here = lax.dynamic_slice_in_dim(silu_all, first_row, rows, 2).reshape(-1, rows)
    mod_part = dot(silu_here, ada_weight.reshape(rows, -1), ((1,), (0,)))
    mod_part = cube_reduce(mod_part.reshape(size_f, items, -1), "mod_f")
    mod_part = butterfly_sum(mod_part, "ctx", "mod_c")
    bias_mod = lax.dynamic_slice_in_dim(ada_bias.astype(F32), first_column, half_width, 1)
    mod_half = (mod_part.reshape(items, 6, half_width) + bias_mod).astype(BF16)
    mods = both(mod_half, swap(mod_half, "mod_t"), 2).astype(F32)
    mods = once_after(mods, [qkv_came, rings[0][4], rings[0][3], rings[0][-1]])

    pieces = spread([(0, "own", qkv_came)], "qkv")
    (qkv_mine,) = place(pieces, [3 * group])
    bias_pair = lax.dynamic_slice_in_dim(
        qv_bias.astype(F32), first_column + c * group, group, 1
    )
    bias_mine = jnp.concatenate([bias_pair[0], jnp.zeros((group,), F32), bias_pair[1]])
    bias_mine = bias_mine.reshape(-1, 1)
    qkv_mine = qkv_mine.T

    in_first, qkv_t = project(rings[0], 0, mods, 0, items, qkv_mine, bias_mine, None)
    qkv_ts = [qkv_t]
    outs, logs = attend(qkv_t, here)
    first_attended = exchange(outs, "mixed0"), logs
    rings.append(swapped_ring(1, items - 1, [mods], lambda x: once_after(x, [logs])))
    latent = [(pairs[0], at) for pairs in rings for at in range(pairs[0].shape[0])]

    proj_full = gather_rows(proj_weight.T, "proj_weights").T
    feed_shard = jnp.concatenate([up_weight, down_weight.T], 1)
    feed_full = gather_rows(once_after(feed_shard, [logs, rings[1][2], rings[1][-2]]), "feed_weights")
    cots = halves(grad_out.reshape(items, here, model), 0, items)

    bias_proj = proj_bias.astype(F32).reshape(1, -1)
    bias_down = down_bias.astype(F32).reshape(1, -1)
    bias_up = lax.dynamic_slice_in_dim(up_bias.astype(F32), t * hidden, hidden, 0)
    bias_up = bias_up.reshape(1, -1)
    mixed = in_second = grad_feed = activated = grad_upward = None
    grad_attended = grad_qkv = out_own = out_peer = out_half = None

    kept = []
    for item in range(items):
        if item:
            in_first, qkv_t = project(
                rings[1], item - 1, mods, item, items, qkv_mine, bias_mine, in_first
            )
            qkv_ts.append(qkv_t)
        qkv_t = qkv_ts[item]
        if item:
            outs, logs = attend(qkv_t, here)
            came = exchange(outs, "mixed%d" % item)
        else:
            came, logs = first_attended
        mixed, own, peer = back_to_rows(came, proj_full, 0, True, mixed, item, items)
        attended, residual, in_half = second(
            own, swap(peer, "attended%d" % item), bias_proj, *latent[item], mods, item
        )
        in_peer = swap(in_half, "in_second%d" % item)
        kept.append((qkv_t, logs, attended, residual, in_half, in_peer))

    qkv_rows = once_after(qkv_groups.transpose(1, 0, 2).reshape(rows, -1), [kept[0][5]])
    qkv_full = gather_rows(qkv_rows, "qkv_weights")

    up_sums, grads_in, highs = [], [], []
    for item in range(items):
        _, _, _, _, in_half, in_peer = kept[item]
        (
            in_second,
            grad_feed,
            activated,
            grad_upward,
            out_own,
            out_peer,
            gin_own,
            gin_peer,
            up_sum,
            high,
        ) = feed(
            in_half,
            in_peer,
            cots,
            mods,
            feed_full,
            bias_up,
            (in_second, grad_feed, activated, grad_upward, out_own, out_peer),
            item,
            items,
            [grads_in[0][1]] if item == items - 1 else [],
        )
        grads_in.append((gin_own, swap(gin_peer, "grad_in_second%d" % item)))
        up_sums.append(up_sum)
        highs.append(high)

    def before_attention(item):
        _, _, attended, residual, _, _ = kept[item]
        grad_residual, low, sums_two = second_back(
            *grads_in[item], residual, attended, cots[0], mods, item
        )
        return grad_residual, low, sums_two, swap(low, "grad_attended%d" % item)

    bounds = highs[0]
    for high in highs[1:]:
        bounds = jnp.maximum(bounds, high)
    for axis in ("fsdp", "ctx"):
        bounds = butterfly_max(bounds, axis, "bounds")
    bounds = jnp.maximum(bounds[:, 0, 0], 1e-15)
    tokens = items * here * size_c * size_f
    up_scale = 32768.0 / (bounds[0] * bounds[3] * tokens)
    down_scale = 32768.0 / (bounds[1] * bounds[2] * tokens)
    scales = jnp.where(jnp.arange(2 * hidden) < hidden, up_scale, down_scale)
    middles = [before_attention(item) for item in range(items)]
    parts = outer(
        in_second, grad_upward, 0, 768, 0, 2 * hidden, [None, None]
    )
    parts = outer(
        grad_feed, activated, 0, 768, hidden // 768, 2 * hidden, parts, [middles[0][3]]
    )
    feed_rows = reduce_rows(*parts, "grad_feed", scales)
    grad_feed_weights, feed_hops = ring_reduce(feed_rows, "grad_feed", scales)

    peers = swap(out_peer, "feed_out")
    gate_sums = []
    for item in range(items):
        out_half, gate_sum = finish(
            out_own, peers, bias_down, kept[item][3], cots[0], mods, out_half, item
        )
        gate_sums.append(gate_sum)
    out_swapped = swap(out_half, "output")
    output = order([out_half], [out_swapped], items)

    grad_blocks = []
    for item in range(items):
        _, low, _, low_peer = middles[item]
        grad_attended, grad_mixed = grad_mixed_of(
            low, low_peer, proj_full, grad_attended, item, items
        )
        grad_blocks.append(
            exchange(grad_mixed.reshape(size_c, group, here), "grad_mixed%d" % item)
        )

    def mark(x):
        return x.reshape(-1, x.shape[-1])[:8, :128].astype(F32)

    input_grads, input_peers, mod_terms = [], [], []
    for item in range(items):
        qkv_t, logs, _, _, _, _ = kept[item]
        grad_qkv, blocks = attend_back(
            qkv_t,
            grad_blocks[item],
            logs,
            grad_qkv,
            item,
            items,
            [parts[0]] if item == 0 else [],
        )
        own, peer = back_to_rows(
            exchange(blocks, "grad_qkv%d" % item),
            qkv_full,
            1,
            after=[feed_rows] if item == 0 else [],
        )
        grad_latent, sums_one = first_back(
            own,
            swap(peer, "grad_in_first%d" % item),
            *latent[item],
            middles[item][0],
            mods,
            item,
            [out_swapped] if item == 1 else [],
        )
        input_grads.append(grad_latent)
        input_peers.append(swap(grad_latent, "grad_latent%d" % item))
        mod_terms.append(jnp.concatenate([sums_one, middles[item][2][:3], gate_sums[item]], 0))

    proj_parts = outer(grad_attended, mixed, 1, half_width, 0, half_width, [None, None])
    grad_proj = ring_reduce(reduce_rows(*proj_parts, "grad_proj"), "grad_proj")[0].T
    grad_qkv = grad_qkv.reshape(3 * group, -1)
    qkv_rows = reduce_rows(*long_outer(in_first, grad_qkv, items), "grad_qkvw")
    grad_qkv_weight = (
        exchange(qkv_rows, "grad_qkvw_c")
        .reshape(size_c, rows, 3, group)
        .transpose(1, 2, 0, 3)
        .reshape(rows, 3, half_width)
    )

    down_sum = sum(
        jnp.sum(grad_feed[item * here : item * here + half].astype(F32), 0)
        for item in range(items)
    )
    qkv_sum = jnp.sum(grad_qkv.astype(F32), 1).reshape(3, group)
    pair_sum = jnp.stack([qkv_sum[0], qkv_sum[2]])
    up_total = lax.dynamic_update_slice_in_dim(
        jnp.zeros(up_bias.shape, F32), sum(up_sums)[0], t * hidden, 0
    )
    pair_total = lax.dynamic_update_slice_in_dim(
        jnp.zeros(qv_bias.shape, F32), pair_sum, first_column + c * group, 1
    )
    proj_sum = sum(middle[2][3] for middle in middles)
    sums = jnp.concatenate(
        [jnp.stack(mod_terms).reshape(-1), up_total, pair_total.reshape(-1), proj_sum, down_sum]
    ).reshape(-1, 128)
    sums = butterfly_sum(butterfly_sum(sums, "tp", "sums"), "ctx", "sums")
    sums = cube_gather(sums, "sums").reshape(size_f, -1)
    edge = items * 6 * model
    grad_mod_all = sums[:, :edge].astype(BF16).reshape(size_f, items, 6, model)
    ada_sum = tree_sum(jnp.sum(grad_mod_all.astype(F32), 1))
    bias_sum = tree_sum(sums[:, edge:])
    ends = [up_bias.shape[0], up_bias.shape[0] + qv_bias.size]

    mod_here = lax.dynamic_slice_in_dim(grad_mod_all, first_column, half_width, 3).reshape(
        size_f * items, -1
    )
    grad_ada = dot(silu_here, mod_here, ((0,), (0,))).reshape(rows, 6, half_width)
    cond_part = dot(mod_here, ada_weight.reshape(rows, -1), ((1,), (1,)))
    cond_part = lax.dynamic_update_slice_in_dim(
        jnp.zeros((size_f * items, model), F32), cond_part, first_row, 1
    ).reshape(size_f, items, model)
    cond_total = cube_reduce(cond_part, "grad_cond")
    for axis in ("ctx", "tp"):
        cond_total = butterfly_sum(cond_total, axis, "grad_cond")
    grad_cond = jax.vjp(jax.nn.silu, cond)[1](cond_total)[0]

    return (
        output.reshape(latents.shape),
        order(input_grads, input_peers, items).reshape(latents.shape),
        grad_cond.reshape(condition.shape),
        grad_ada,
        ada_sum,
        grad_qkv_weight,
        bias_sum[ends[0] : ends[1]].reshape(qv_bias.shape),
        grad_proj,
        bias_sum[ends[1] : ends[1] + model],
        grad_feed_weights[:, :hidden],
        bias_sum[: ends[0]],
        grad_feed_weights[:, hidden:].T,
        bias_sum[ends[1] + model :],
    )


def tree_sum(entries):
    while entries.shape[0] > 1:
        entries = entries[0::2] + entries[1::2]
    return entries[0]


def solution(mesh):
    in_specs = (
        P(None, "fsdp", "ctx", None),
        P(None, "fsdp", None),
        P(None, "fsdp", "ctx", None),
        P(("fsdp", "ctx"), None, "tp"),
        P(),
        P(("fsdp", "ctx"), None, "tp"),
        P(),
        P("tp", ("fsdp", "ctx")),
        P(),
        P(("fsdp", "ctx"), "tp"),
        P(),
        P("tp", ("fsdp", "ctx")),
        P(),
    )
    out_specs = (
        P(None, "fsdp", "ctx", None),
        P(None, "fsdp", "ctx", None),
        P(None, "fsdp", None),
        P(("fsdp", "ctx"), None, "tp"),
        P(),
        P(("fsdp", "ctx"), None, "tp"),
        P(),
        P("tp", ("fsdp", "ctx")),
        P(),
        P(("fsdp", "ctx"), "tp"),
        P(),
        P("tp", ("fsdp", "ctx")),
        P(),
    )
    return jax.shard_map(body, mesh=mesh, in_specs=in_specs, out_specs=out_specs, check_vma=False)
```

```python
from functools import partial

import jax
import jax.numpy as jnp
from jax import lax
from jax.experimental import pallas as pl
from jax.experimental.pallas import tpu as pltpu
from jax.sharding import PartitionSpec as P

HEADS = 16
HEAD_DIM = 72
LOG2E = 1.4426950408889634
F32 = jnp.float32
BF16 = jnp.bfloat16


def dot(a, b, dims):
    return lax.dot_general(a, b, (dims, ((), ())), preferred_element_type=F32)


def normalize(values):
    centre = values - jnp.mean(values, -1, keepdims=True)
    inverse = lax.rsqrt(jnp.mean(centre * centre, -1, keepdims=True) + 1e-06)
    return (centre * inverse, inverse)


def norm_back(incoming, normed, inverse):
    return inverse * (
        incoming
        - jnp.mean(incoming, -1, keepdims=True)
        - normed * jnp.mean(incoming * normed, -1, keepdims=True)
    )


def shift(x, k, name="shift"):
    size = lax.axis_size("ctx")
    with jax.named_scope(name):
        return lax.ppermute(x, "ctx", [(i, (i + k) % size) for i in range(size)])


def flip(x, axis, bit, name="flip"):
    size = lax.axis_size(axis)
    with jax.named_scope(name):
        return lax.ppermute(x, axis, [(i, i ^ (1 << bit)) for i in range(size)])


def exchange(x, name):
    with jax.named_scope(name):
        return lax.all_to_all(x, "ctx", 0, 0)


def gather_rows(x, name):
    with jax.named_scope(name):
        return lax.all_gather(x, ("fsdp", "ctx"), tiled=True)


def bits_of(axis):
    return lax.axis_size(axis).bit_length() - 1


def ring_gather(x, name, second=lambda x: x):
    size = lax.axis_size("ctx")
    blocks = [x] * size
    moving = x
    for step in range(1, size // 2 + 1):
        moving = shift(second(moving) if step == 2 else moving, 1, name + "_right")
        blocks[step] = moving
    moving = x
    for step in range(1, (size - 1) // 2 + 1):
        moving = shift(moving, -1, name + "_left")
        blocks[size - step] = moving
    return blocks


def butterfly_sum(x, axis, name):
    for bit in range(bits_of(axis)):
        x = x + flip(x, axis, bit, name)
    return x


def butterfly_max(x, axis, name):
    for bit in range(bits_of(axis)):
        x = jnp.maximum(x, flip(x, axis, bit, name))
    return x


def cube_gather(x, name):
    x = x[None]
    for bit in range(bits_of("fsdp")):
        x = jnp.concatenate([x, flip(x, "fsdp", bit, name)], 0)
    return x


def cube_reduce(x, name):
    for bit in reversed(range(bits_of("fsdp"))):
        half = x.shape[0] // 2
        x = x[:half] + flip(x[half:], "fsdp", bit, name)
    return x[0]


def spread(pieces, name):
    for bit in reversed(range(bits_of("fsdp"))):
        pieces = pieces + [
            (offset ^ (1 << bit), places, flip(block, "fsdp", bit, name + "_%d" % bit))
            for offset, places, block in pieces
        ]
    return pieces


def gather_stacked(shard, name):
    blocks = ring_gather(shard, name)
    return spread([(0, "before", jnp.stack(blocks))], name)


def place_kernel(targets, widths, *refs):
    count = len(targets)
    ins, outs = refs[:count], refs[-3 - len(widths) : -3]
    held, in_sem, out_sem = refs[-3:]
    own_f = lax.axis_index("fsdp")
    own_c = lax.axis_index("ctx")
    size_c = lax.axis_size("ctx")
    arriving, leaving = [], []
    for (offset, places), ref in zip(targets, ins):
        row = jnp.bitwise_xor(own_f, offset)
        for at in range(size_c):
            column = at if places == "own" else lax.rem(own_c + size_c - at, size_c)
            slot = len(arriving)
            arriving.append(pltpu.make_async_copy(ref.at[at], held.at[slot], in_sem.at[slot]))
            first = 0
            for width, out in zip(widths, outs):
                leaving.append(
                    pltpu.make_async_copy(
                        held.at[slot, :, pl.ds(first, width)],
                        out.at[row, column],
                        out_sem.at[len(leaving)],
                    )
                )
                first += width
    for copy in arriving:
        copy.start()
    each = len(widths)
    for slot, copy in enumerate(arriving):
        copy.wait()
        for out_copy in leaving[slot * each : (slot + 1) * each]:
            out_copy.start()
    for copy in leaving:
        copy.wait()


def place(pieces, widths, after=()):
    size_f, size_c = lax.axis_size("fsdp"), lax.axis_size("ctx")
    rows, total = pieces[0][2].shape[1:]
    count = size_f * size_c
    outs = pl.pallas_call(
        partial(place_kernel, [piece[:2] for piece in pieces], widths),
        out_shape=[jax.ShapeDtypeStruct((size_f, size_c, rows, width), BF16) for width in widths],
        in_specs=[ANYWHERE] * (len(pieces) + len(after)),
        out_specs=[ANYWHERE] * len(widths),
        scratch_shapes=[
            pltpu.VMEM((count, rows, total), BF16),
            pltpu.SemaphoreType.DMA((count,)),
            pltpu.SemaphoreType.DMA((count * len(widths),)),
        ],
        compiler_params=pltpu.CompilerParams(vmem_limit_bytes=40 << 20),
        cost_estimate=pl.CostEstimate(
            flops=0, bytes_accessed=4 * count * rows * total, transcendentals=0
        ),
    )(*[piece[2] for piece in pieces], *after)
    return [out.reshape(-1, width) for out, width in zip(outs, widths)]


def lower(x, scale):
    return x if scale is None else (x * scale).astype(jnp.float16)


def higher(x, scale):
    return x if scale is None else x.astype(F32) * (1.0 / scale)


def reduce_rows(send, keep, name, scale=None):
    size_c = lax.axis_size("ctx")
    own_f = lax.axis_index("fsdp")
    _, width, columns = keep.shape
    parts = [keep, flip(send, "fsdp", 0, name + "_0")]
    for bit in range(1, bits_of("fsdp")):
        own_bit = (own_f >> bit) % 2
        pairs = [part.reshape(-1, 2, width, columns) for part in parts]
        got = sum(lax.dynamic_index_in_dim(pair, 1 - own_bit, 1, False) for pair in pairs)
        got = flip(lower(got, scale), "fsdp", bit, name + "_%d" % bit)
        parts = [lax.dynamic_index_in_dim(pair, own_bit, 1, False) for pair in pairs]
        parts.append(higher(got, scale))
    return sum(parts).reshape(size_c, width // size_c, columns)


def ring_reduce(blocks, name, scale=None):
    size = lax.axis_size("ctx")
    own = lax.axis_index("ctx")

    def block(offset):
        return lax.dynamic_index_in_dim(blocks, (own + offset) % size, 0, False)

    total = block(0)
    hops = []
    for sign, reach in ((1, size // 2), (-1, (size - 1) // 2)):
        moving = None
        for distance in range(reach, 0, -1):
            term = block(sign * distance)
            if moving is not None:
                term = term + moving
            hops.append(shift(lower(term, scale), sign, name + "_ring"))
            moving = higher(hops[-1], scale)
        if moving is not None:
            total = total + moving
    return total, hops


def whole(shape):
    return pl.BlockSpec(tuple(shape), lambda *_: (0,) * len(shape))


def struct(shape, dtype):
    return jax.ShapeDtypeStruct(tuple(shape), dtype)


ANYWHERE = pl.BlockSpec(memory_space=pltpu.HBM)
PARAMS = pltpu.CompilerParams(vmem_limit_bytes=48 << 20)


def cost(flops, nbytes, exps=0):
    return pl.CostEstimate(flops=int(flops), bytes_accessed=int(nbytes), transcendentals=int(exps))


def mods_spec(mods, item):
    return pl.BlockSpec((None,) + mods.shape[1:], lambda *_: (item, 0, 0))


def largest(x):
    return jnp.full((8, 128), jnp.max(jnp.abs(x)), F32)


def slab_call(kernel, args, in_specs, helds, after=(), **options):
    taken = [held for held in helds if held is not None]
    count = len(args)
    more = len(taken) + len(after)

    def run(*refs):
        kernel(*refs[:count], *refs[count + more :])

    return pl.pallas_call(
        run,
        in_specs=in_specs + [ANYWHERE] * more,
        input_output_aliases={count + at: at for at in range(len(taken))},
        compiler_params=PARAMS,
        **options,
    )(*args, *taken, *after)


def halves_kernel(first, both_ref, own_ref, peer_ref):
    count, half, _ = own_ref.shape
    t = lax.axis_index("tp")
    for rank, out in ((t, own_ref), (1 - t, peer_ref)):
        rows = pl.ds(pl.multiple_of(rank * half, half), half)
        for at in range(count):
            out[at] = both_ref[first + at, rows, :]


def halves(x, first, count, after=()):
    items, here, model = x.shape
    shape = (count, here // 2, model)
    return slab_call(
        partial(halves_kernel, first),
        [x],
        [whole(x.shape)],
        [],
        after,
        grid=(1,),
        out_specs=[whole(shape)] * 2,
        out_shape=[struct(shape, x.dtype)] * 2,
        cost_estimate=cost(0, 4 * count * here * model),
    )


def wait_kernel(in_ref, out_ref):
    out_ref[...] = in_ref[...]


def once_after(x, after):
    return slab_call(
        wait_kernel,
        [x],
        [whole(x.shape)],
        [],
        after,
        grid=(1,),
        out_specs=whole(x.shape),
        out_shape=struct(x.shape, x.dtype),
        cost_estimate=cost(0, 4 * x.size),
    )


def project_kernel(count, *refs):
    pieces = refs[:count]
    mods_ref, weight_ref, bias_ref, in_ref, out_ref = refs[count:]
    for pair in range(count // 2):
        rows = jnp.concatenate([pieces[2 * pair][...], pieces[2 * pair + 1][...]], 0)
        here = rows.shape[0]
        normed, _ = normalize(rows.astype(F32))
        in_first = (normed * (1.0 + mods_ref[1:2, :]) + mods_ref[0:1, :]).astype(BF16)
        in_ref[pl.ds(pair * here, here), :] = in_first
        product = dot(weight_ref[...], in_first, ((1,), (1,))) + bias_ref[...]
        out_ref[:, pl.ds(pair * here, here)] = product.astype(BF16)


def project(pieces, place_in, mods, item, items, weight_t, bias, held, after=()):
    _, half, model = pieces[0].shape
    total = half * len(pieces)
    piece_spec = pl.BlockSpec((None, half, model), lambda i: (place_in, 0, 0))
    width = weight_t.shape[0]
    return slab_call(
        partial(project_kernel, len(pieces)),
        [*pieces, mods, weight_t, bias],
        [piece_spec] * len(pieces)
        + [mods_spec(mods, item), whole(weight_t.shape), whole(bias.shape)],
        [held],
        after,
        grid=(1,),
        out_specs=[
            pl.BlockSpec((total, model), lambda i: (item, 0)),
            whole((width, total)),
        ],
        out_shape=[struct((items * total, model), BF16), struct((width, total), BF16)],
        cost_estimate=cost(2 * total * model * width, 6 * total * model),
    )


def head_rows(values, head):
    values = values.astype(F32)
    row = lax.broadcasted_iota(jnp.int32, values.shape, 0)
    inside = (row >= head * HEAD_DIM) & (row < (head + 1) * HEAD_DIM)
    return jnp.where(inside, values, 0.0).astype(BF16), inside


def attend_kernel(heads, steps, q_ref, kt_ref, vt_ref, out_ref, log_ref, k_ref):
    step = pl.program_id(0)
    factor = HEAD_DIM ** (-0.5) * LOG2E

    @pl.when(step == 0)
    def _():
        k_ref[...] = kt_ref[...].T

    total = None
    for head in range(heads):
        q_head, inside = head_rows(q_ref[...], head)
        scores = dot(k_ref[...], q_head, ((1,), (0,)))
        highest = jnp.max(scores, 0, keepdims=True)
        exponent = jnp.exp2((scores - highest) * factor)
        summed = jnp.sum(exponent, 0, keepdims=True)
        chances = (exponent * (1.0 / summed)).astype(BF16)
        mixed = dot(vt_ref[...], chances, ((1,), (0,)))
        total = mixed if total is None else jnp.where(inside, mixed, total)
        log_ref[pl.ds(head, 1), :] = highest * factor + jnp.log2(summed)
    out_ref[lax.rem(lax.axis_index("ctx") + steps - step, steps)] = total.astype(BF16)


def attend(qkv_t, here, after=()):
    group, total = qkv_t.shape[0] // 3, qkv_t.shape[1]
    heads, steps = group // HEAD_DIM, total // here
    thirds = qkv_t.reshape(3, group, total)
    return slab_call(
        partial(attend_kernel, heads, steps),
        [thirds, thirds, thirds],
        [
            pl.BlockSpec((None, group, here), lambda i: (0, 0, i)),
            pl.BlockSpec((None, group, total), lambda i: (1, 0, 0)),
            pl.BlockSpec((None, group, total), lambda i: (2, 0, 0)),
        ],
        [],
        after,
        grid=(steps,),
        out_specs=[
            whole((steps, group, here)),
            pl.BlockSpec((heads, here), lambda i: (0, i)),
        ],
        out_shape=[struct((steps, group, here), BF16), struct((heads, total), F32)],
        scratch_shapes=[pltpu.VMEM((total, group), BF16)],
        cost_estimate=cost(heads * total * total * 1600, 8 * group * total, heads * total * total),
    )


def attend_back_kernel(
    heads,
    steps,
    q_ref,
    kt_ref,
    vt_ref,
    log_ref,
    grad_ref,
    all_ref,
    out_ref,
    k_ref,
    v_ref,
    dk_ref,
    dv_ref,
):
    step = pl.program_id(0)
    own_c = lax.axis_index("ctx")
    scaling = HEAD_DIM ** (-0.5)
    group, block = q_ref.shape

    @pl.when(step == 0)
    def _():
        dk_ref[...] = jnp.zeros_like(dk_ref)
        dv_ref[...] = jnp.zeros_like(dv_ref)
        k_ref[...] = kt_ref[...].T
        v_ref[...] = vt_ref[...].T

    grad = grad_ref[lax.rem(own_c + steps - step, steps)]
    grad_query = None
    for head in range(heads):
        q_head, inside = head_rows(q_ref[...], head)
        do_head, _ = head_rows(grad, head)
        scores = dot(k_ref[...], q_head, ((1,), (0,)))
        chances = jnp.exp2(scores * (scaling * LOG2E) - log_ref[pl.ds(head, 1), :])
        grad_chances = dot(v_ref[...], do_head, ((1,), (0,)))
        weighted = jnp.sum(chances * grad_chances, 0, keepdims=True)
        grad_scores = (chances * (grad_chances - weighted)).astype(BF16)
        term = dot(kt_ref[...], grad_scores, ((1,), (0,)))
        grad_query = term if grad_query is None else jnp.where(inside, term, grad_query)
        dk_ref[...] += dot(q_head, grad_scores, ((1,), (1,)))
        dv_ref[...] += dot(do_head, chances.astype(BF16), ((1,), (1,)))
    columns = pl.ds(pl.multiple_of(step * block, block), block)
    all_ref[0, :, columns] = (grad_query * scaling).astype(BF16)

    @pl.when(step == steps - 1)
    def _():
        all_ref[1] = (dk_ref[...] * scaling).astype(BF16)
        all_ref[2] = dv_ref[...].astype(BF16)
        for at in range(steps):
            out_ref[lax.rem(own_c + steps - at, steps)] = all_ref[
                :, :, at * block : (at + 1) * block
            ]


def attend_back(qkv_t, grads, logs, held, item, items, after=()):
    group, total = qkv_t.shape[0] // 3, qkv_t.shape[1]
    heads, steps = group // HEAD_DIM, grads.shape[0]
    here = total // steps
    thirds = qkv_t.reshape(3, group, total)
    return slab_call(
        partial(attend_back_kernel, heads, steps),
        [thirds, thirds, thirds, logs, grads],
        [
            pl.BlockSpec((None, group, here), lambda i: (0, 0, i)),
            pl.BlockSpec((None, group, total), lambda i: (1, 0, 0)),
            pl.BlockSpec((None, group, total), lambda i: (2, 0, 0)),
            pl.BlockSpec((heads, here), lambda i: (0, i)),
            whole(grads.shape),
        ],
        [held],
        after,
        grid=(steps,),
        out_specs=[
            pl.BlockSpec((3, group, total), lambda i: (0, 0, item)),
            whole((steps, 3, group, here)),
        ],
        out_shape=[
            struct((3, group, items * total), BF16),
            struct((steps, 3, group, here), BF16),
        ],
        scratch_shapes=[
            pltpu.VMEM((total, group), BF16),
            pltpu.VMEM((total, group), BF16),
            pltpu.VMEM((group, total), F32),
            pltpu.VMEM((group, total), F32),
        ],
        cost_estimate=cost(heads * total * total * 4000, 16 * group * total, heads * total * total),
    )


def back_to_rows_kernel(contract, keep, blocks_ref, weight_ref, *outs):
    own_ref, peer_ref = outs[-2:]
    rows = blocks_ref[...].reshape(-1, blocks_ref.shape[-1])
    if keep:
        outs[0][...] = rows
    total = dot(rows, weight_ref[...], ((0,), (contract,)))
    half = own_ref.shape[0]
    own_ref[...] = total[:half]
    peer_ref[...] = total[half:]


def back_to_rows(blocks, weight, contract, keep=False, held=None, item=0, items=1, after=()):
    here = blocks.shape[-1]
    features, model = weight.shape[contract], weight.shape[1 - contract]
    half = here // 2
    out_specs = [whole((half, model))] * 2
    out_shape = [struct((half, model), F32)] * 2
    if keep:
        out_specs = [pl.BlockSpec((features, here), lambda i: (0, item))] + out_specs
        out_shape = [struct((features, items * here), BF16)] + out_shape
    return slab_call(
        partial(back_to_rows_kernel, contract, keep),
        [blocks, weight],
        [whole(blocks.shape), whole(weight.shape)],
        [held],
        after,
        grid=(1,),
        out_specs=out_specs,
        out_shape=out_shape,
        cost_estimate=cost(
            2 * here * features * model, 2 * features * model + 8 * here * model
        ),
    )


def second_kernel(own_ref, peer_ref, bias_ref, latent_ref, mods_ref, att_ref, res_ref, in_ref):
    attended = own_ref[...] + peer_ref[...] + bias_ref[...]
    residual = latent_ref[...].astype(F32) + mods_ref[2:3, :] * attended
    normed, _ = normalize(residual)
    att_ref[...] = attended
    res_ref[...] = residual
    in_ref[...] = (normed * (1.0 + mods_ref[4:5, :]) + mods_ref[3:4, :]).astype(BF16)


def second(own, peer, bias, latent, place_in, mods, item, after=()):
    shape = own.shape
    return slab_call(
        second_kernel,
        [own, peer, bias, latent, mods],
        [
            whole(shape),
            whole(shape),
            whole(bias.shape),
            pl.BlockSpec((None,) + shape, lambda i: (place_in, 0, 0)),
            mods_spec(mods, item),
        ],
        [],
        after,
        grid=(1,),
        out_specs=[whole(shape)] * 3,
        out_shape=[struct(shape, F32), struct(shape, F32), struct(shape, BF16)],
        cost_estimate=cost(20 * own.size, 20 * own.size),
    )


def feed_kernel(
    steps,
    own_ref,
    peer_ref,
    cot_own,
    cot_peer,
    mods_ref,
    up_ref,
    down_ref,
    bias_ref,
    in_all,
    grad_all,
    act_ref,
    gup_ref,
    out_own,
    out_peer,
    gin_own,
    gin_peer,
    sum_ref,
    highs,
    in_ref,
    grad_ref,
    out_acc,
    gin_acc,
):
    step = pl.program_id(0)
    half = own_ref.shape[0]

    @pl.when(step == 0)
    def _():
        in_ref[:half, :] = own_ref[...]
        in_ref[half:, :] = peer_ref[...]
        in_all[...] = in_ref[...]
        gate = mods_ref[5:6, :]
        grad_ref[:half, :] = (cot_own[...].astype(F32) * gate).astype(BF16)
        grad_ref[half:, :] = (cot_peer[...].astype(F32) * gate).astype(BF16)
        grad_all[...] = grad_ref[...]
        highs[0] = largest(in_ref[...].astype(F32))
        highs[1] = largest(grad_ref[...].astype(F32))
        highs[2] = jnp.zeros((8, 128), F32)
        highs[3] = jnp.zeros((8, 128), F32)

    upward = dot(in_ref[...], up_ref[...], ((1,), (0,))) + bias_ref[...]
    grad_act = dot(grad_ref[...], down_ref[...], ((1,), (0,)))
    inner = 0.7978845608028654
    squared = upward * upward
    curve = jnp.tanh(inner * upward * (1.0 + 0.044715 * squared))
    activated = (0.5 * upward * (1.0 + curve)).astype(BF16)
    slope = 0.5 * (1.0 + curve) + (0.5 * inner) * upward * (1.0 - curve * curve) * (
        1.0 + (3.0 * 0.044715) * squared
    )
    grad_up = (slope * grad_act).astype(BF16)
    act_ref[...] = activated
    gup_ref[...] = grad_up
    wide = grad_up.astype(F32)
    sum_ref[...] = jnp.sum(wide, 0, keepdims=True)
    highs[2] = jnp.maximum(highs[2], largest(activated.astype(F32)))
    highs[3] = jnp.maximum(highs[3], largest(wide))
    out_term = dot(activated, down_ref[...], ((1,), (1,)))
    gin_term = dot(grad_up, up_ref[...], ((1,), (1,)))

    @pl.when(step == 0)
    def _():
        out_acc[...] = out_term
        gin_acc[...] = gin_term

    @pl.when(step > 0)
    def _():
        out_acc[...] += out_term
        gin_acc[...] += gin_term

    @pl.when(step == steps - 1)
    def _():
        out_own[...] = out_acc[:half, :]
        out_peer[...] = out_acc[half:, :].astype(BF16)
        gin_own[...] = gin_acc[:half, :]
        gin_peer[...] = gin_acc[half:, :]


def feed(own, peer, cots, mods, weights, bias, helds, item, items, after=()):
    half, model = own.shape
    here, hidden = 2 * half, weights.shape[1] // 2
    cot = pl.BlockSpec((None, half, model), lambda j: (item, 0, 0))
    tile = 1152
    steps = hidden // tile
    rows = pl.BlockSpec((here, model), lambda j: (item, 0))
    slab = pl.BlockSpec((here, tile), lambda j: (item, j))
    return slab_call(
        partial(feed_kernel, steps),
        [own, peer, *cots, mods, weights, weights, bias],
        [whole(own.shape)] * 2
        + [cot] * 2
        + [
            mods_spec(mods, item),
            pl.BlockSpec((model, tile), lambda j: (0, j)),
            pl.BlockSpec((model, tile), lambda j: (0, j + steps)),
            pl.BlockSpec((1, tile), lambda j: (0, j)),
        ],
        helds,
        after,
        grid=(steps,),
        out_specs=[rows, rows, slab, slab]
        + [pl.BlockSpec((half, model), lambda j: (item, 0))] * 2
        + [whole(own.shape)] * 2
        + [pl.BlockSpec((1, tile), lambda j: (0, j)), whole((4, 8, 128))],
        out_shape=[
            struct((items * here, model), BF16),
            struct((items * here, model), BF16),
            struct((items * here, hidden), BF16),
            struct((items * here, hidden), BF16),
            struct((items * half, model), F32),
            struct((items * half, model), BF16),
            struct(own.shape, F32),
            struct(own.shape, F32),
            struct((1, hidden), F32),
            struct((4, 8, 128), F32),
        ],
        scratch_shapes=[
            pltpu.VMEM((here, model), BF16),
            pltpu.VMEM((here, model), BF16),
            pltpu.VMEM((here, model), F32),
            pltpu.VMEM((here, model), F32),
        ],
        cost_estimate=cost(8 * here * model * hidden, 4 * model * hidden + 4 * here * hidden),
    )


def finish_kernel(own_ref, peer_ref, bias_ref, res_ref, cot_ref, mods_ref, out_ref, sum_ref):
    feed_out = own_ref[...] + peer_ref[...].astype(F32) + bias_ref[...]
    out_ref[...] = (res_ref[...] + mods_ref[5:6, :] * feed_out).astype(BF16)
    sum_ref[...] = jnp.sum(cot_ref[...].astype(F32) * feed_out, 0, keepdims=True)


def finish(own, peer, bias, residual, cots, mods, held, item, after=()):
    items, half, model = cots.shape
    part = pl.BlockSpec((half, model), lambda i: (item, 0))
    return slab_call(
        finish_kernel,
        [own, peer, bias, residual, cots, mods],
        [
            part,
            part,
            whole(bias.shape),
            whole((half, model)),
            pl.BlockSpec((None, half, model), lambda i: (item, 0, 0)),
            mods_spec(mods, item),
        ],
        [held],
        after,
        grid=(1,),
        out_specs=[part, whole(bias.shape)],
        out_shape=[struct((items * half, model), BF16), struct(bias.shape, F32)],
        cost_estimate=cost(8 * half * model, 16 * half * model),
    )


def second_back_kernel(
    own_ref, peer_ref, res_ref, att_ref, cot_ref, mods_ref, grad_ref, low_ref, sum_ref
):
    incoming = own_ref[...] + peer_ref[...]
    normed, inverse = normalize(res_ref[...])
    grad = cot_ref[...].astype(F32) + norm_back(
        incoming * (1.0 + mods_ref[4:5, :]), normed, inverse
    )
    low = (grad * mods_ref[2:3, :]).astype(BF16)
    grad_ref[...] = grad
    low_ref[...] = low
    sum_ref[0:1, :] = jnp.sum(grad * att_ref[...], 0, keepdims=True)
    sum_ref[1:2, :] = jnp.sum(incoming, 0, keepdims=True)
    sum_ref[2:3, :] = jnp.sum(incoming * normed, 0, keepdims=True)
    sum_ref[3:4, :] = jnp.sum(low.astype(F32), 0, keepdims=True)


def second_back(own, peer, residual, attended, cots, mods, item, after=()):
    shape = own.shape
    return slab_call(
        second_back_kernel,
        [own, peer, residual, attended, cots, mods],
        [whole(shape)] * 4
        + [pl.BlockSpec((None,) + shape, lambda i: (item, 0, 0)), mods_spec(mods, item)],
        [],
        after,
        grid=(1,),
        out_specs=[whole(shape), whole(shape), whole((4, shape[1]))],
        out_shape=[struct(shape, F32), struct(shape, BF16), struct((4, shape[1]), F32)],
        cost_estimate=cost(30 * own.size, 24 * own.size),
    )


def grad_mixed_kernel(own_ref, peer_ref, weight_ref, all_ref, out_ref):
    rows = jnp.concatenate([own_ref[...], peer_ref[...]], 0)
    all_ref[...] = rows
    out_ref[...] = dot(weight_ref[...], rows, ((1,), (1,))).astype(BF16)


def grad_mixed_of(own, peer, weight, held, item, items, after=()):
    features, model = weight.shape
    here = 2 * own.shape[0]
    return slab_call(
        grad_mixed_kernel,
        [own, peer, weight],
        [whole(own.shape), whole(own.shape), whole(weight.shape)],
        [held],
        after,
        grid=(1,),
        out_specs=[
            pl.BlockSpec((here, model), lambda i: (item, 0)),
            whole((features, here)),
        ],
        out_shape=[struct((items * here, model), BF16), struct((features, here), BF16)],
        cost_estimate=cost(2 * here * features * model, 2 * features * model),
    )


def first_back_kernel(own_ref, peer_ref, latent_ref, res_ref, mods_ref, grad_ref, sum_ref):
    incoming = own_ref[...] + peer_ref[...]
    normed, inverse = normalize(latent_ref[...].astype(F32))
    grad_ref[...] = res_ref[...] + norm_back(
        incoming * (1.0 + mods_ref[1:2, :]), normed, inverse
    )
    sum_ref[0:1, :] = jnp.sum(incoming, 0, keepdims=True)
    sum_ref[1:2, :] = jnp.sum(incoming * normed, 0, keepdims=True)


def first_back(own, peer, latent, place_in, grad_residual, mods, item, after=()):
    shape = own.shape
    return slab_call(
        first_back_kernel,
        [own, peer, latent, grad_residual, mods],
        [
            whole(shape),
            whole(shape),
            pl.BlockSpec((None,) + shape, lambda i: (place_in, 0, 0)),
            whole(shape),
            mods_spec(mods, item),
        ],
        [],
        after,
        grid=(1,),
        out_specs=[whole(shape), whole((2, shape[1]))],
        out_shape=[struct(shape, F32), struct((2, shape[1]), F32)],
        cost_estimate=cost(30 * own.size, 20 * own.size),
    )


def split_rows(product_ref, send_ref, keep_ref):
    width = keep_ref.shape[1]
    core = lax.rem(lax.axis_index("fsdp"), 2)
    for high in range(keep_ref.shape[0]):
        theirs = pl.multiple_of((2 * high + 1 - core) * width, 8)
        mine = pl.multiple_of((2 * high + core) * width, 8)
        send_ref[high] = product_ref[pl.ds(theirs, width), :]
        keep_ref[high] = product_ref[pl.ds(mine, width), :]


def outer_kernel(right, left_ref, right_ref, send_ref, keep_ref, left_t, *product):
    @pl.when(pl.program_id(0) == 0)
    def _():
        left_t[...] = left_ref[...].T

    if product:
        product[0][...] = dot(left_t[...], right_ref[...], ((1,), (right,)))
        split_rows(product[0], send_ref, keep_ref)
        return
    width = keep_ref.shape[1]
    core = lax.rem(lax.axis_index("fsdp"), 2)
    for high in range(keep_ref.shape[0]):
        for out, which in ((send_ref, 1 - core), (keep_ref, core)):
            rows = pl.ds(pl.multiple_of((2 * high + which) * width, 8), width)
            out[high] = dot(left_t[rows, :], right_ref[...], ((1,), (right,)))


def outer(left, right, contract, tile, first, columns, helds, after=()):
    rows, model = left.shape
    size_f = lax.axis_size("fsdp")
    wide = right.shape[1 - contract]
    shape = (size_f // 2, model // size_f, columns)
    block = pl.BlockSpec(shape[:2] + (tile,), lambda j: (0, 0, j + first))
    right_spec = (
        pl.BlockSpec((rows, tile), lambda j: (0, j))
        if contract == 0
        else pl.BlockSpec((tile, rows), lambda j: (j, 0))
    )
    return slab_call(
        partial(outer_kernel, contract),
        [left, right],
        [whole(left.shape), right_spec],
        helds,
        after,
        grid=(wide // tile,),
        out_specs=[block] * 2,
        out_shape=[struct(shape, F32)] * 2,
        scratch_shapes=[pltpu.VMEM((model, rows), BF16)]
        + ([pltpu.VMEM((model, tile), F32)] if shape[1] % 16 else []),
        cost_estimate=cost(2 * rows * model * wide, 2 * rows * wide + 4 * model * wide),
    )


def long_outer_kernel(steps, left_ref, right_ref, send_ref, keep_ref, product):
    step = pl.program_id(0)
    term = dot(left_ref[...], right_ref[...], ((0,), (1,)))

    @pl.when(step == 0)
    def _():
        product[...] = term

    @pl.when(step > 0)
    def _():
        product[...] += term

    @pl.when(step == steps - 1)
    def _():
        split_rows(product, send_ref, keep_ref)


def long_outer(left, right, steps, after=()):
    rows, model = left.shape
    wide = right.shape[0]
    size_f = lax.axis_size("fsdp")
    shape = (size_f // 2, model // size_f, wide)
    return slab_call(
        partial(long_outer_kernel, steps),
        [left, right],
        [
            pl.BlockSpec((rows // steps, model), lambda j: (j, 0)),
            pl.BlockSpec((wide, rows // steps), lambda j: (0, j)),
        ],
        [],
        after,
        grid=(steps,),
        out_specs=[whole(shape)] * 2,
        out_shape=[struct(shape, F32)] * 2,
        scratch_shapes=[pltpu.VMEM((model, wide), F32)],
        cost_estimate=cost(2 * rows * model * wide, 2 * rows * (model + wide)),
    )


def order_kernel(count, *refs):
    out_ref = refs[-1]
    half = out_ref.shape[1] // 2
    items = out_ref.shape[0]
    t = lax.axis_index("tp")
    for rank, parts in ((t, refs[:count]), (1 - t, refs[count : 2 * count])):
        rows = pl.ds(pl.multiple_of(rank * half, half), half)
        for item in range(items):
            part = parts[0][item * half : (item + 1) * half, :] if count == 1 else parts[item][...]
            out_ref[item, rows, :] = part


def order(owns, peers, items, after=()):
    model = owns[0].shape[1]
    half = sum(own.shape[0] for own in owns) // items
    return slab_call(
        partial(order_kernel, len(owns)),
        [*owns, *peers],
        [whole(part.shape) for part in (*owns, *peers)],
        [],
        after,
        grid=(1,),
        out_specs=whole((items, 2 * half, model)),
        out_shape=struct((items, 2 * half, model), owns[0].dtype),
        cost_estimate=cost(0, 16 * items * half * model),
    )


def body(
    latents,
    condition,
    grad_out,
    ada_weight,
    ada_bias,
    qkv_weight,
    qv_bias,
    proj_weight,
    proj_bias,
    up_weight,
    up_bias,
    down_weight,
    down_bias,
):
    t = lax.axis_index("tp")
    c = lax.axis_index("ctx")
    f = lax.axis_index("fsdp")
    size_c = lax.axis_size("ctx")
    size_f = lax.axis_size("fsdp")
    micro, batch, here, model = latents.shape
    items = micro * batch
    half = here // 2
    half_width = qkv_weight.shape[2]
    group = half_width // size_c
    hidden = up_weight.shape[1]
    rows = qkv_weight.shape[0]
    first_column = t * half_width

    def swap(x, name):
        return flip(x, "tp", 0, name)

    def both(own, peer, axis):
        return jnp.where(
            t == 0,
            jnp.concatenate([own, peer], axis),
            jnp.concatenate([peer, own], axis),
        )

    qkv_groups = (
        qkv_weight.reshape(rows, 3, size_c, group)
        .transpose(2, 0, 1, 3)
        .reshape(size_c, rows, 3 * group)
    )
    qkv_came = exchange(qkv_groups, "qkv_c")

    flat_latents = latents.reshape(items, here, model)

    def swapped_ring(first, count, after=(), second=lambda x: x):
        own, peer = halves(flat_latents, first, count, after)
        pairs = [own, peer]
        for piece in ring_gather(own, "latent%d" % first, second)[1:]:
            pairs += [piece, swap(piece, "latent%d_t" % first)]
        return pairs

    rings = [swapped_ring(0, 1)]

    cond = condition.reshape(items, model).astype(F32)
    silu_all = cube_gather(jax.nn.silu(cond).astype(BF16), "cond")
    first_row = (f * size_c + c) * rows
    silu_here = lax.dynamic_slice_in_dim(silu_all, first_row, rows, 2).reshape(-1, rows)
    mod_part = dot(silu_here, ada_weight.reshape(rows, -1), ((1,), (0,)))
    mod_part = cube_reduce(mod_part.reshape(size_f, items, -1), "mod_f")
    mod_part = butterfly_sum(mod_part, "ctx", "mod_c")
    bias_mod = lax.dynamic_slice_in_dim(ada_bias.astype(F32), first_column, half_width, 1)
    mod_half = (mod_part.reshape(items, 6, half_width) + bias_mod).astype(BF16)
    mods = both(mod_half, swap(mod_half, "mod_t"), 2).astype(F32)
    mods = once_after(mods, [qkv_came, rings[0][4], rings[0][3], rings[0][-1]])

    pieces = spread([(0, "own", qkv_came)], "qkv")
    (qkv_mine,) = place(pieces, [3 * group])
    bias_pair = lax.dynamic_slice_in_dim(
        qv_bias.astype(F32), first_column + c * group, group, 1
    )
    bias_mine = jnp.concatenate([bias_pair[0], jnp.zeros((group,), F32), bias_pair[1]])
    bias_mine = bias_mine.reshape(-1, 1)
    qkv_mine = qkv_mine.T

    in_first, qkv_t = project(rings[0], 0, mods, 0, items, qkv_mine, bias_mine, None)
    qkv_ts = [qkv_t]
    outs, logs = attend(qkv_t, here)
    first_attended = exchange(outs, "mixed0"), logs
    rings.append(swapped_ring(1, items - 1, [mods], lambda x: once_after(x, [logs])))
    latent = [(pairs[0], at) for pairs in rings for at in range(pairs[0].shape[0])]

    proj_full = gather_rows(proj_weight.T, "proj_weights").T
    feed_shard = jnp.concatenate([up_weight, down_weight.T], 1)
    feed_full = gather_rows(once_after(feed_shard, [logs, rings[1][2], rings[1][-2]]), "feed_weights")
    cots = halves(grad_out.reshape(items, here, model), 0, items)

    bias_proj = proj_bias.astype(F32).reshape(1, -1)
    bias_down = down_bias.astype(F32).reshape(1, -1)
    bias_up = lax.dynamic_slice_in_dim(up_bias.astype(F32), t * hidden, hidden, 0)
    bias_up = bias_up.reshape(1, -1)
    mixed = in_second = grad_feed = activated = grad_upward = None
    grad_attended = grad_qkv = out_own = out_peer = out_half = None

    kept = []
    for item in range(items):
        if item:
            in_first, qkv_t = project(
                rings[1], item - 1, mods, item, items, qkv_mine, bias_mine, in_first
            )
            qkv_ts.append(qkv_t)
        qkv_t = qkv_ts[item]
        if item:
            outs, logs = attend(qkv_t, here)
            came = exchange(outs, "mixed%d" % item)
        else:
            came, logs = first_attended
        mixed, own, peer = back_to_rows(came, proj_full, 0, True, mixed, item, items)
        attended, residual, in_half = second(
            own, swap(peer, "attended%d" % item), bias_proj, *latent[item], mods, item
        )
        in_peer = swap(in_half, "in_second%d" % item)
        kept.append((qkv_t, logs, attended, residual, in_half, in_peer))

    qkv_rows = once_after(qkv_groups.transpose(1, 0, 2).reshape(rows, -1), [kept[0][5]])
    qkv_full = gather_rows(qkv_rows, "qkv_weights")

    up_sums, grads_in, highs = [], [], []
    for item in range(items):
        _, _, _, _, in_half, in_peer = kept[item]
        (
            in_second,
            grad_feed,
            activated,
            grad_upward,
            out_own,
            out_peer,
            gin_own,
            gin_peer,
            up_sum,
            high,
        ) = feed(
            in_half,
            in_peer,
            cots,
            mods,
            feed_full,
            bias_up,
            (in_second, grad_feed, activated, grad_upward, out_own, out_peer),
            item,
            items,
            [grads_in[0][1]] if item == items - 1 else [],
        )
        grads_in.append((gin_own, swap(gin_peer, "grad_in_second%d" % item)))
        up_sums.append(up_sum)
        highs.append(high)

    def before_attention(item):
        _, _, attended, residual, _, _ = kept[item]
        grad_residual, low, sums_two = second_back(
            *grads_in[item], residual, attended, cots[0], mods, item
        )
        return grad_residual, low, sums_two, swap(low, "grad_attended%d" % item)

    bounds = highs[0]
    for high in highs[1:]:
        bounds = jnp.maximum(bounds, high)
    for axis in ("fsdp", "ctx"):
        bounds = butterfly_max(bounds, axis, "bounds")
    bounds = jnp.maximum(bounds[:, 0, 0], 1e-15)
    tokens = items * here * size_c * size_f
    up_scale = 32768.0 / (bounds[0] * bounds[3] * tokens)
    down_scale = 32768.0 / (bounds[1] * bounds[2] * tokens)
    scales = jnp.where(jnp.arange(2 * hidden) < hidden, up_scale, down_scale)
    middles = [before_attention(item) for item in range(items)]
    parts = outer(
        in_second, grad_upward, 0, 768, 0, 2 * hidden, [None, None]
    )
    parts = outer(
        grad_feed, activated, 0, 768, hidden // 768, 2 * hidden, parts, [middles[0][3]]
    )
    feed_rows = reduce_rows(*parts, "grad_feed", scales)
    grad_feed_weights, feed_hops = ring_reduce(feed_rows, "grad_feed", scales)

    peers = swap(out_peer, "feed_out")
    gate_sums = []
    for item in range(items):
        out_half, gate_sum = finish(
            out_own, peers, bias_down, kept[item][3], cots[0], mods, out_half, item
        )
        gate_sums.append(gate_sum)
    out_swapped = swap(out_half, "output")
    output = order([out_half], [out_swapped], items)

    grad_blocks = []
    for item in range(items):
        _, low, _, low_peer = middles[item]
        grad_attended, grad_mixed = grad_mixed_of(
            low, low_peer, proj_full, grad_attended, item, items
        )
        grad_blocks.append(
            exchange(grad_mixed.reshape(size_c, group, here), "grad_mixed%d" % item)
        )

    def mark(x):
        return x.reshape(-1, x.shape[-1])[:8, :128].astype(F32)

    input_grads, input_peers, mod_terms = [], [], []
    for item in range(items):
        qkv_t, logs, _, _, _, _ = kept[item]
        grad_qkv, blocks = attend_back(
            qkv_t,
            grad_blocks[item],
            logs,
            grad_qkv,
            item,
            items,
            [parts[0]] if item == 0 else [],
        )
        own, peer = back_to_rows(
            exchange(blocks, "grad_qkv%d" % item),
            qkv_full,
            1,
            after=[feed_rows] if item == 0 else [],
        )
        grad_latent, sums_one = first_back(
            own,
            swap(peer, "grad_in_first%d" % item),
            *latent[item],
            middles[item][0],
            mods,
            item,
            [out_swapped] if item == 1 else [],
        )
        input_grads.append(grad_latent)
        input_peers.append(swap(grad_latent, "grad_latent%d" % item))
        mod_terms.append(jnp.concatenate([sums_one, middles[item][2][:3], gate_sums[item]], 0))

    proj_parts = outer(grad_attended, mixed, 1, half_width, 0, half_width, [None, None])
    grad_proj = ring_reduce(reduce_rows(*proj_parts, "grad_proj"), "grad_proj")[0].T
    grad_qkv = grad_qkv.reshape(3 * group, -1)
    qkv_rows = reduce_rows(*long_outer(in_first, grad_qkv, items), "grad_qkvw")
    grad_qkv_weight = (
        exchange(qkv_rows, "grad_qkvw_c")
        .reshape(size_c, rows, 3, group)
        .transpose(1, 2, 0, 3)
        .reshape(rows, 3, half_width)
    )

    down_sum = sum(
        jnp.sum(grad_feed[item * here : item * here + half].astype(F32), 0)
        for item in range(items)
    )
    qkv_sum = jnp.sum(grad_qkv.astype(F32), 1).reshape(3, group)
    pair_sum = jnp.stack([qkv_sum[0], qkv_sum[2]])
    up_total = lax.dynamic_update_slice_in_dim(
        jnp.zeros(up_bias.shape, F32), sum(up_sums)[0], t * hidden, 0
    )
    pair_total = lax.dynamic_update_slice_in_dim(
        jnp.zeros(qv_bias.shape, F32), pair_sum, first_column + c * group, 1
    )
    proj_sum = sum(middle[2][3] for middle in middles)
    sums = jnp.concatenate(
        [jnp.stack(mod_terms).reshape(-1), up_total, pair_total.reshape(-1), proj_sum, down_sum]
    ).reshape(-1, 128)
    sums = butterfly_sum(butterfly_sum(sums, "tp", "sums"), "ctx", "sums")
    sums = cube_gather(sums, "sums").reshape(size_f, -1)
    edge = items * 6 * model
    grad_mod_all = sums[:, :edge].astype(BF16).reshape(size_f, items, 6, model)
    ada_sum = tree_sum(jnp.sum(grad_mod_all.astype(F32), 1))
    bias_sum = tree_sum(sums[:, edge:])
    ends = [up_bias.shape[0], up_bias.shape[0] + qv_bias.size]

    mod_here = lax.dynamic_slice_in_dim(grad_mod_all, first_column, half_width, 3).reshape(
        size_f * items, -1
    )
    grad_ada = dot(silu_here, mod_here, ((0,), (0,))).reshape(rows, 6, half_width)
    cond_part = dot(mod_here, ada_weight.reshape(rows, -1), ((1,), (1,)))
    cond_part = lax.dynamic_update_slice_in_dim(
        jnp.zeros((size_f * items, model), F32), cond_part, first_row, 1
    ).reshape(size_f, items, model)
    cond_total = cube_reduce(cond_part, "grad_cond")
    for axis in ("ctx", "tp"):
        cond_total = butterfly_sum(cond_total, axis, "grad_cond")
    grad_cond = jax.vjp(jax.nn.silu, cond)[1](cond_total)[0]

    return (
        output.reshape(latents.shape),
        order(input_grads, input_peers, items).reshape(latents.shape),
        grad_cond.reshape(condition.shape),
        grad_ada,
        ada_sum,
        grad_qkv_weight,
        bias_sum[ends[0] : ends[1]].reshape(qv_bias.shape),
        grad_proj,
        bias_sum[ends[1] : ends[1] + model],
        grad_feed_weights[:, :hidden],
        bias_sum[: ends[0]],
        grad_feed_weights[:, hidden:].T,
        bias_sum[ends[1] + model :],
    )


def tree_sum(entries):
    while entries.shape[0] > 1:
        entries = entries[0::2] + entries[1::2]
    return entries[0]


def solution(mesh):
    in_specs = (
        P(None, "fsdp", "ctx", None),
        P(None, "fsdp", None),
        P(None, "fsdp", "ctx", None),
        P(("fsdp", "ctx"), None, "tp"),
        P(),
        P(("fsdp", "ctx"), None, "tp"),
        P(),
        P("tp", ("fsdp", "ctx")),
        P(),
        P(("fsdp", "ctx"), "tp"),
        P(),
        P("tp", ("fsdp", "ctx")),
        P(),
    )
    out_specs = (
        P(None, "fsdp", "ctx", None),
        P(None, "fsdp", "ctx", None),
        P(None, "fsdp", None),
        P(("fsdp", "ctx"), None, "tp"),
        P(),
        P(("fsdp", "ctx"), None, "tp"),
        P(),
        P("tp", ("fsdp", "ctx")),
        P(),
        P(("fsdp", "ctx"), "tp"),
        P(),
        P("tp", ("fsdp", "ctx")),
        P(),
    )
    return jax.shard_map(body, mesh=mesh, in_specs=in_specs, out_specs=out_specs, check_vma=False)
```
